128 devices in a mesh: expert: 32 (over x, z, core), tensor: 4 (over y).
Axes of the slice: x: 4, y: 4, z: 4, core: 2. Of those that a mesh axis runs over, the one named last changes fastest.
Arguments:
- stream: bfloat16 [8192, 2048], P('expert'), may hold values from -6 to 6
- segment_ids: int32 [32, 256], P('expert'), may hold values from 0 to 3, never falling along the last dimension, each value on 1 to 128 neighbouring positions
- expert_ids: int32 [8192, 6], P('expert'), may hold values from 0 to 63, all different within a row; in each aligned block of 256 rows (0 to 255, 256 to 511, ...) at most 32 rows name the same one
- first_gain: bfloat16 [2048], P('expert'), may hold values from 0.5 to 1.5
- query_proj: bfloat16 [2048, 3072], P('expert', 'tensor'), may hold values from -0.125 to 0.125
- latent_down: bfloat16 [2048, 576], P('expert'), may hold values from -0.125 to 0.125
- latent_gain: bfloat16 [512], P('expert'), may hold values from 0.5 to 1.5
- latent_up: bfloat16 [512, 4096], P('expert', 'tensor'), may hold values from -0.25 to 0.25
- output_proj: bfloat16 [2048, 2048], P('tensor', 'expert'), may hold values from -1 to 1
- second_gain: bfloat16 [2048], P('expert'), may hold values from 0.5 to 1.5
- router_proj: bfloat16 [2048, 64], P('expert'), may hold values from -0.0625 to 0.0625
- shared_gate: bfloat16 [2048, 2816], P('expert', 'tensor'), may hold values from -0.125 to 0.125
- shared_up: bfloat16 [2048, 2816], P('expert', 'tensor'), may hold values from -0.125 to 0.125
- shared_down: bfloat16 [2816, 2048], P('tensor', 'expert'), may hold values from -0.109375 to 0.109375
- expert_gate: bfloat16 [64, 2048, 1408], P('expert', None, 'tensor'), may hold values from -0.125 to 0.125
- expert_up: bfloat16 [64, 2048, 1408], P('expert', None, 'tensor'), may hold values from -0.125 to 0.125
- expert_down: bfloat16 [64, 1408, 2048], P('expert', 'tensor'), may hold values from -1.75 to 1.75
- cotangent: float32 [8192, 2048], P('expert'), may hold values from -6 to 6
Outputs:
- result: float32 [8192, 2048], P('expert')
- stream_grad: float32 [8192, 2048], P('expert')
- first_gain_grad: float32 [2048], P('expert')
- query_proj_grad: float32 [2048, 3072], P('expert', 'tensor')
- latent_down_grad: float32 [2048, 576], P('expert')
- latent_gain_grad: float32 [512], P('expert')
- latent_up_grad: float32 [512, 4096], P('expert', 'tensor')
- output_proj_grad: float32 [2048, 2048], P('tensor', 'expert')
- second_gain_grad: float32 [2048], P('expert')
- router_proj_grad: float32 [2048, 64], P('expert')
- shared_gate_grad: float32 [2048, 2816], P('expert', 'tensor')
- shared_up_grad: float32 [2048, 2816], P('expert', 'tensor')
- shared_down_grad: float32 [2816, 2048], P('tensor', 'expert')
- expert_gate_grad: float32 [64, 2048, 1408], P('expert', None, 'tensor')
- expert_up_grad: float32 [64, 2048, 1408], P('expert', None, 'tensor')
- expert_down_grad: float32 [64, 1408, 2048], P('expert', 'tensor')
The draws below stay inside these ranges and needn't reach their ends.
Inputs may be any that keep to these rules, and one draw needn't show every extreme that they name: `expert_ids`: each row names 6 different experts. Among the 256 rows of one index of expert no expert is named by more than 32 rows, a bound that some block reaches. `segment_ids`: within a sequence the numbers never fall; a document holds at most 128 tokens, and one holds exactly that many.
All inputs are finite; a program needn't handle non-finite values.
Results may differ from the reference program's by a relative error of at most 0.018.
Values may be sent and summed in bfloat16 or wider, within the bound.
No kernel may reach another device: no remote copies, remote signals or barrier semaphores. Data moves between devices by JAX's collectives and lax.ppermute only.
A program may use at most 320 MiB of HBM per device.

```python
import math
import jax
import jax.numpy as jnp
import numpy as np
from jax import lax

D = 2048
HEADS = 16
NOPE = 128
ROPE = 64
VDIM = 128
LATENT = 512
FF_EXP = 1408
SHARED_FF = 2816
TOPK = 6
TOK_DEV = 256
EXPERTS = 64
SEQS = 32
TOKENS = 8192
CAP = 32


def shard_levels(stream_key, dims, cuts, least, largest):
    gain, own = 1.0, jax.random.fold_in(stream_key, 6)
    for dim, parts in cuts:
        heights = jnp.exp(jax.random.uniform(jax.random.fold_in(own, dim), (parts,), jnp.float32, least / len(cuts), largest / len(cuts)))
        gain = gain * jnp.repeat(heights, dims[dim] // parts).reshape([-1 if axis == dim else 1 for axis in range(len(dims))])
    return gain


def profile(amount, total, reach, slope):
    portions = [(1 << 20) // math.isqrt(rank ** slope) + 1 for rank in range(2, amount + 1)]
    rest, given = total - reach - (amount - 1), [1] * (amount - 1)
    while rest > 0:
        free = [i for i in range(amount - 1) if given[i] < reach]
        pool, left = sum([portions[i] for i in free]), rest
        for i in free:
            addition = min(reach - given[i], max(1, left * portions[i] // pool), rest)
            given[i] = given[i] + addition
            rest = rest - addition
    return np.array([reach] + given)


def uneven_parts(key, number_of, total, reach, skew):
    if number_of == 2:
        one = jax.random.randint(key, (), max(1, total - reach), min(reach, total - 1) + 1)
        return jnp.stack([one, total - one])
    lengths = jnp.asarray(profile(number_of, total, reach, skew), jnp.int32)
    couples = (number_of - 1) // 2
    source_of, receiver = lengths[1:1 + 2 * couples:2], lengths[2:2 + 2 * couples:2]
    room = jnp.minimum(source_of - 1, reach - receiver)
    shifted = jax.random.randint(jax.random.fold_in(key, 1), (couples,), 0, 1 << 20) % (room + 1)
    lengths = lengths.at[1:1 + 2 * couples:2].set(source_of - shifted).at[2:2 + 2 * couples:2].set(receiver + shifted)
    return lengths[jax.random.permutation(jax.random.fold_in(key, 2), number_of)]


def deal_out(own_key, own, number, rows, number_of, top, reach, skew):
    order = jax.random.permutation(own_key, number_of)
    crowded, usual = load_shares(number_of, rows * top, reach, skew, True), load_shares(number_of, rows * top, reach, skew, False)
    places = jnp.arange(number_of)

    def named(tallies, offset_by):
        used = int((tallies > 0).sum())
        fixed = max(1, used // 4)
        moved = fixed + (places - fixed + offset_by * (used - fixed)) % max(1, number_of - fixed)
        return jnp.zeros((number_of,), jnp.int32).at[order[jnp.where(places < fixed, places, moved)]].set(jnp.asarray(tallies, jnp.int32))

    tallies = jnp.where(number % 4 == 0, named(crowded, number // 4), named(usual, number - number // 4 - 1))
    mixed = jax.random.permutation(jax.random.fold_in(own, 3), number_of)
    donor, taker = mixed[0:number_of // 2 * 2:2], mixed[1:number_of // 2 * 2:2]
    room = jnp.minimum(tallies[donor] - 1, reach - tallies[taker]) // 2
    room = jnp.where((donor == order[0]) | (taker == order[0]) | (tallies[taker] == 0), 0, jnp.maximum(room, 0))
    moved = jax.random.randint(jax.random.fold_in(own, 4), (number_of // 2,), 0, 1 << 20) % (room + 1)
    tallies = tallies.at[donor].add(-moved).at[taker].add(moved)
    items = jnp.searchsorted(jnp.cumsum(tallies), jnp.arange(rows * top), side="right").astype(jnp.int32)
    listing = items.reshape(top, rows).T
    listing = listing[jax.random.permutation(jax.random.fold_in(own, 1), rows)]
    offset_by = jax.random.randint(jax.random.fold_in(own, 2), (rows, 1), 0, top)
    return jnp.take_along_axis(listing, (jnp.arange(top)[None, :] + offset_by) % top, axis=1)


def load_shares(number_of, total, most, slope, full):
    weights = [(1 << 20) // math.isqrt(rank ** slope) + 1 for rank in range(1, number_of + 1)]
    largest = most if full else min(most, max(-(-total // number_of), total * weights[0] // sum(weights)))
    least = 1 if total - largest >= number_of - 1 else 0
    holding, surplus = [largest] + [least] * (number_of - 1), total - largest - least * (number_of - 1)
    while surplus > 0:
        free = [i for i in range(1, number_of) if holding[i] < largest] or [i for i in range(1, number_of) if holding[i] < most]
        mass, budget = sum([weights[i] for i in free]), surplus
        for i in free:
            addition = min(most - holding[i], max(1, budget * weights[i] // mass), surplus)
            holding[i] = holding[i] + addition
            surplus = surplus - addition
    return np.array(holding)


def bell_draw(rng, extent, spread, most, shards=(), kind=jnp.bfloat16):
    drawn = spread * jax.random.normal(rng, extent, jnp.float32)
    if shards:
        drawn = drawn * shard_levels(rng, extent, shards, -0.22, 0.18)
    return jnp.clip(drawn, -most, most).astype(kind)


def setup_inputs(seed: int = 0) -> dict:
    splits = jax.random.split(jax.random.key(seed), 19)
    stream = bell_draw(splits[0], (TOKENS, D), 1.0, 6.0, ((0, 32),))
    segment_ids = jax.vmap(lambda own: jnp.searchsorted(jnp.cumsum(uneven_parts(own, 4, TOK_DEV, TOK_DEV // 2, 0)), jnp.arange(TOK_DEV), side="right"))(jax.random.split(splits[1], SEQS)).reshape((SEQS, TOK_DEV)).astype(jnp.int32)
    expert_ids_keys = jax.random.split(jax.random.fold_in(splits[2], 1), TOKENS // TOK_DEV)
    expert_ids_turns = jax.random.permutation(jax.random.fold_in(splits[2], 3), TOKENS // TOK_DEV)
    expert_ids = jax.vmap(lambda own, number: deal_out(jax.random.fold_in(splits[2], 2), own, number, TOK_DEV, EXPERTS, TOPK, CAP, 1))(expert_ids_keys, expert_ids_turns).reshape((TOKENS, TOPK))
    first_gain = jnp.clip(1.0 + 0.1 * jax.random.normal(splits[3], (D,), jnp.float32), 0.5, 1.5).astype(jnp.bfloat16)
    query_proj = bell_draw(splits[4], (D, HEADS * (NOPE + ROPE)), D ** -0.5, 0.125, ((0, 32), (1, 4)))
    latent_down = bell_draw(splits[5], (D, LATENT + ROPE), D ** -0.5, 0.125, ((0, 32),))
    latent_gain = jnp.clip(1.0 + 0.1 * jax.random.normal(splits[6], (LATENT,), jnp.float32), 0.5, 1.5).astype(jnp.bfloat16)
    latent_up = bell_draw(splits[7], (LATENT, HEADS * (NOPE + VDIM)), LATENT ** -0.5, 0.25, ((0, 32), (1, 4)))
    output_proj = bell_draw(splits[8], (HEADS * VDIM, D), (max(HEADS * VDIM // 64, 1)) ** -0.5, 1.0, ((0, 4), (1, 32)))
    second_gain = jnp.clip(1.0 + 0.1 * jax.random.normal(splits[9], (D,), jnp.float32), 0.5, 1.5).astype(jnp.bfloat16)
    router_proj = bell_draw(splits[10], (D, EXPERTS), (4 * D) ** -0.5, 0.0625, ((0, 32),))
    shared_gate = bell_draw(splits[11], (D, SHARED_FF), D ** -0.5, 0.125, ((0, 32), (1, 4)))
    shared_up = bell_draw(splits[12], (D, SHARED_FF), D ** -0.5, 0.125, ((0, 32), (1, 4)))
    shared_down = bell_draw(splits[13], (SHARED_FF, D), SHARED_FF ** -0.5, 0.109375, ((0, 4), (1, 32)))
    expert_gate = bell_draw(splits[14], (EXPERTS, D, FF_EXP), D ** -0.5, 0.125, ((0, 32), (2, 4)))
    expert_up = bell_draw(splits[15], (EXPERTS, D, FF_EXP), D ** -0.5, 0.125, ((0, 32), (2, 4)))
    expert_down = bell_draw(splits[16], (EXPERTS, FF_EXP, D), (max(FF_EXP // 128, 1)) ** -0.5, 1.75, ((0, 32), (1, 4)))
    cotangent = bell_draw(splits[17], (TOKENS, D), 1.0, 6.0, ((0, 32),), jnp.float32)
    return dict(stream=stream, segment_ids=segment_ids, expert_ids=expert_ids, first_gain=first_gain, query_proj=query_proj, latent_down=latent_down, latent_gain=latent_gain, latent_up=latent_up, output_proj=output_proj, second_gain=second_gain, router_proj=router_proj, shared_gate=shared_gate, shared_up=shared_up, shared_down=shared_down, expert_gate=expert_gate, expert_up=expert_up, expert_down=expert_down, cotangent=cotangent)


EPSILON = 1e-06
ROTARY_BASE = 10000.0

@jax.custom_vjp
def low(v):
    return lax.optimization_barrier(v.astype(jnp.bfloat16)).astype(jnp.float32)

@jax.custom_vjp
def low_back(v):
    return v

def low_keep(v):
    return (low(v), None)

def low_pass(kept, grad):
    return (grad,)

def back_keep(v):
    return (v, None)

def back_low(kept, grad):
    return (low(grad),)
low.defvjp(low_keep, low_pass)
low_back.defvjp(back_keep, back_low)

def product(left, right):
    return jnp.dot(left, right, precision=lax.Precision.HIGHEST, preferred_element_type=jnp.float32)

def contract(pattern, left, right):
    return jnp.einsum(pattern, left, right, precision=lax.Precision.HIGHEST, preferred_element_type=jnp.float32)

def rms_scale(values, gain_vector):
    return values * lax.rsqrt(lax.optimization_barrier(jnp.mean(values * values, axis=-1, keepdims=True)) + EPSILON) * gain_vector

def rotary_tables(length, rotary_width):
    position = jnp.arange(length).astype(jnp.float32)
    exponent = jnp.arange(rotary_width // 2).astype(jnp.float32) * (2.0 / rotary_width)
    frequency = jnp.exp(-math.log(ROTARY_BASE) * exponent)
    angles = position[:, None] * frequency[None, :]
    angles = jnp.concatenate([angles, angles], axis=-1)
    return (jnp.cos(angles), jnp.sin(angles))

def rotate(values, cosine_table, sine_table):
    halfway = values.shape[-1] // 2
    turned = jnp.concatenate([-values[..., halfway:], values[..., :halfway]], axis=-1)
    return values * cosine_table + turned * sine_table

def attend_sequence(queries, key_nope, key_rope, values, segment):
    score_scale = (NOPE + ROPE) ** (-0.5)
    raw_scores = contract('thd,uhd->htu', queries[..., :NOPE], key_nope) + contract('thr,ur->htu', queries[..., NOPE:], key_rope)
    raw_scores = low_back(raw_scores)
    positions = jnp.arange(segment.shape[0])
    allowed = (segment[:, None] == segment[None, :]) & (positions[None, :] <= positions[:, None])
    scores = jnp.where(allowed[None], raw_scores * score_scale, -1e+30)
    weights_att = low(jax.nn.softmax(scores, axis=-1))
    return contract('htu,uhv->thv', weights_att, values)

def forward_layer(stream, first_gain, query_proj, latent_down, latent_gain, latent_up, output_proj, second_gain, router_proj, shared_gate, shared_up, shared_down, expert_gate, expert_up, expert_down, segment_ids, expert_ids, slot_index, pair_slot):
    tokens_all = stream.shape[0]
    cosine_table, sine_table = rotary_tables(TOK_DEV, ROPE)
    cosine_all = jnp.tile(cosine_table, (SEQS, 1))
    sine_all = jnp.tile(sine_table, (SEQS, 1))
    normed_first = low(rms_scale(stream, first_gain))
    query_raw = low_back(product(normed_first, query_proj)).reshape(tokens_all, HEADS, NOPE + ROPE)
    queries = low(jnp.concatenate([query_raw[..., :NOPE], rotate(query_raw[..., NOPE:], cosine_all[:, None, :], sine_all[:, None, :])], axis=-1))
    compressed = low_back(product(normed_first, latent_down))
    latent = low(rms_scale(compressed[:, :LATENT], latent_gain))
    key_rope = low(rotate(compressed[:, LATENT:], cosine_all, sine_all))
    expanded = low(low_back(product(latent, latent_up))).reshape(tokens_all, HEADS, NOPE + VDIM)
    group_size = math.gcd(SEQS, max(1, 4096 // TOK_DEV))
    group_count = SEQS // group_size

    def regroup(grouped_in):
        return grouped_in.reshape((group_count, group_size, TOK_DEV) + grouped_in.shape[1:])
    attended = lax.map(jax.checkpoint(lambda pieces: jax.vmap(attend_sequence)(*pieces)), (regroup(queries), regroup(expanded[..., :NOPE]), regroup(key_rope), regroup(expanded[..., NOPE:]), segment_ids.reshape(group_count, group_size, TOK_DEV)))
    attended = low(low_back(attended.reshape(tokens_all, HEADS * VDIM)))
    middle = stream + low_back(product(attended, output_proj))
    normed_second = low(rms_scale(middle, second_gain))
    router_probs = jax.nn.softmax(low_back(product(normed_second, router_proj)), axis=-1)
    gate_values = jnp.take_along_axis(router_probs, expert_ids, axis=1)
    gate_pre = low_back(product(normed_second, shared_gate))
    up_pre = low_back(product(normed_second, shared_up))
    shared_out = low_back(product(low(jax.nn.silu(gate_pre) * up_pre), shared_down))
    padded = jnp.concatenate([normed_second, jnp.zeros((1, normed_second.shape[1]), normed_second.dtype)], axis=0)

    def expert_rows(pieces):
        row_index, gate_weight, up_weight, down_weight = pieces
        rows_in = padded[row_index]
        gate_rows = low_back(product(rows_in, gate_weight))
        up_rows = low_back(product(rows_in, up_weight))
        return low_back(product(low(jax.nn.silu(gate_rows) * up_rows), down_weight))
    expert_out = lax.map(jax.checkpoint(expert_rows), (slot_index, expert_gate, expert_up, expert_down))
    picked = expert_out.reshape(-1, expert_out.shape[-1])[pair_slot]
    routed = lax.optimization_barrier(jnp.sum(gate_values[..., None] * picked, axis=1))
    return middle + shared_out + routed

def reference(stream, segment_ids, expert_ids, first_gain, query_proj, latent_down, latent_gain, latent_up, output_proj, second_gain, router_proj, shared_gate, shared_up, shared_down, expert_gate, expert_up, expert_down, cotangent):
    flat_expert = expert_ids.reshape(SEQS, TOK_DEV * TOPK).astype(jnp.int32)
    expert_range = jnp.arange(EXPERTS).astype(jnp.int32)
    onehot = (flat_expert[..., None] == expert_range).astype(jnp.int32)
    position = lax.optimization_barrier(jnp.sum((jnp.cumsum(onehot, axis=1) - onehot) * onehot, axis=-1)).astype(jnp.int32)
    row_number = (jnp.arange(SEQS).astype(jnp.int32)[:, None] * CAP + position).reshape(-1).astype(jnp.int32)
    expert_flat = flat_expert.reshape(-1)
    token_ids = (jnp.arange(TOKENS * TOPK).astype(jnp.int32) // TOPK).astype(jnp.int32)
    slot_index = jnp.full((EXPERTS, SEQS * CAP), TOKENS, jnp.int32).at[expert_flat, row_number].set(token_ids)
    pair_slot = (expert_flat * (SEQS * CAP) + row_number).reshape(TOKENS, TOPK).astype(jnp.int32)
    primal = tuple((weight_in.astype(jnp.float32) for weight_in in (stream, first_gain, query_proj, latent_down, latent_gain, latent_up, output_proj, second_gain, router_proj, shared_gate, shared_up, shared_down, expert_gate, expert_up, expert_down)))
    result, pullback = jax.vjp(lambda *params: forward_layer(*params, segment_ids, expert_ids.astype(jnp.int32), slot_index, pair_slot), *primal)
    gradients = pullback(cotangent.astype(jnp.float32))
    return (result, gradients[0], gradients[1], gradients[2], gradients[3], gradients[4], gradients[5], gradients[6], gradients[7], gradients[8], gradients[9], gradients[10], gradients[11], gradients[12], gradients[13], gradients[14])
```

```python
import functools
import math

import jax
import jax.numpy as jnp
from jax import lax
from jax.experimental import pallas as pl
from jax.experimental.pallas import tpu as pltpu
from jax.sharding import PartitionSpec as P

NOPE = 128
ROPE = 64
VDIM = 128
LATENT = 512
TOPK = 6
EPSILON = 1e-06
ROTARY_BASE = 10000.0

BF16 = jnp.bfloat16
F32 = jnp.float32
VMEM_BYTES = 60 * 1024 * 1024
LANES = 128
COST_SCALE = 10


def dot_nn(left, right):
    return lax.dot_general(left, right, (((1,), (0,)), ((), ())), preferred_element_type=F32)


def dot_nt(left, right):
    return lax.dot_general(left, right, (((1,), (1,)), ((), ())), preferred_element_type=F32)


def dot_tn(left, right):
    return lax.dot_general(left, right, (((0,), (0,)), ((), ())), preferred_element_type=F32)


def silu_parts(pre_values):
    sigmoid_value = 1.0 / (1.0 + jnp.exp(-pre_values))
    return (pre_values * sigmoid_value, sigmoid_value * (1.0 + pre_values * (1.0 - sigmoid_value)))


def inverse_rms(values):
    return lax.rsqrt(jnp.mean(values * values, axis=-1, keepdims=True) + EPSILON)


def rms_back(values, scale, gain, grad):
    normed = values * scale
    weighted = grad * gain
    return (
        scale * (weighted - normed * jnp.mean(weighted * normed, axis=-1, keepdims=True)),
        grad * normed,
    )


def turned(values):
    width = values.shape[1]
    lane = lax.broadcasted_iota(jnp.int32, values.shape, 1) % ROPE
    half = ROPE // 2
    return jnp.where(
        lane < half, pltpu.roll(values, width - half, 1), pltpu.roll(values, half, 1)
    )


def rotated(values, cosine, sine):
    return values * cosine + turned(values) * sine


def block_at(me, step, count, width):
    return pl.ds(pl.multiple_of(lax.rem(me + step, count) * width, width), width)


def run(kernel, outs, args, flops, scratch=(), name=None, places=None, aliases=None, out_places=None):
    places = places or {}
    out_places = out_places or {}
    in_specs = [pl.BlockSpec(memory_space=places.get(i, pltpu.VMEM)) for i in range(len(args))]
    out_specs = [pl.BlockSpec(memory_space=out_places.get(i, pltpu.VMEM)) for i in range(len(outs))]
    moved = sum(a.size * a.dtype.itemsize for a in args) + sum(
        math.prod(shape) * jnp.dtype(dtype).itemsize for shape, dtype in outs
    )
    return pl.pallas_call(
        kernel,
        in_specs=in_specs,
        out_specs=out_specs,
        out_shape=[jax.ShapeDtypeStruct(shape, dtype) for shape, dtype in outs],
        scratch_shapes=list(scratch),
        input_output_aliases=aliases or {},
        compiler_params=pltpu.CompilerParams(vmem_limit_bytes=VMEM_BYTES),
        cost_estimate=pl.CostEstimate(
            flops=flops // COST_SCALE, bytes_accessed=moved // COST_SCALE, transcendentals=0
        ),
        name=name,
    )(*args)


def routing_kernel(me_ref, ids_ref, cot_ref, t0_ref, t1_ref, low_ref, out_ref):
    choices, tokens = ids_ref.shape
    owners, local, capacity, piece = out_ref.shape
    experts = owners * local
    rows = owners * capacity
    expert = lax.broadcasted_iota(jnp.int32, (experts, tokens), 0)
    chosen = jnp.zeros((experts, tokens), F32)
    for choice in range(choices):
        chosen += jnp.where(ids_ref[choice : choice + 1, :] == expert, 1.0, 0.0)
    before = jnp.where(
        lax.broadcasted_iota(jnp.int32, (tokens, tokens), 0)
        < lax.broadcasted_iota(jnp.int32, (tokens, tokens), 1),
        1.0,
        0.0,
    ).astype(BF16)
    place = dot_nn(chosen.astype(BF16), before)
    place = jnp.where(chosen > 0.5, place, -1.0).astype(BF16)
    low = cot_ref[...].astype(BF16)
    low_ref[...] = low
    mine = cot_ref[:, block_at(me_ref[0], 0, cot_ref.shape[1] // piece, piece)].astype(BF16)
    slot = (lax.broadcasted_iota(jnp.int32, (tokens, rows), 1) % capacity).astype(F32)
    for index, t_ref in ((0, t0_ref), (1, t1_ref)):
        spread = jnp.where(
            lax.broadcasted_iota(jnp.int32, (experts, rows), 0)
            == lax.broadcasted_iota(jnp.int32, (experts, rows), 1) // capacity * local + index,
            1.0,
            0.0,
        ).astype(BF16)
        wanted = dot_tn(place, spread)
        matrix = jnp.where(wanted == slot, 1.0, 0.0).astype(BF16)
        t_ref[...] = matrix
        out_ref[:, index] = dot_tn(matrix, mine).astype(BF16).reshape(owners, capacity, piece)


def attend_kernel(
    me_ref,
    stream_ref,
    w_ref,
    seg_row_ref,
    seg_col_ref,
    cos_ref,
    sin_ref,
    own_ref,
    send1_ref,
    send2_ref,
    send3_ref,
    normed_ref,
    query_ref,
    expanded_ref,
    key_ref,
    latent_ref,
    compressed_ref,
    probs_ref,
    attended_ref,
    gains_ref,
    latent_gain_ref,
):
    heads, tokens, _ = probs_ref.shape
    width = stream_ref.shape[1]
    piece = own_ref.shape[1]
    nope = heads * NOPE
    queries = nope + heads * ROPE
    edge = queries + LATENT + LANES
    outer = edge + heads * VDIM
    owners = 32
    columns = jnp.concatenate(
        [w_ref[:, outer + 2 * NOPE :].astype(F32), jnp.zeros((width, ROPE), F32)], axis=1
    )
    gains = columns.T[:8, :]
    gains_ref[...] = gains
    shard = width // owners
    short = LATENT // owners
    latent_gain = (
        columns.reshape(owners, shard, LANES)[:, :short, :].reshape(LATENT, LANES).T[:8, :]
    )
    latent_gain_ref[...] = latent_gain
    stream = stream_ref[...].astype(F32)
    normed = (stream * inverse_rms(stream) * gains[0:1, :]).astype(BF16)
    normed_ref[...] = normed
    projected = dot_nn(normed, w_ref[:, :edge])
    query_ref[:, :nope] = projected[:, :nope].astype(BF16)
    query_ref[:, nope:] = rotated(projected[:, nope:queries], cos_ref[...], sin_ref[...]).astype(BF16)
    compressed = projected[:, queries : queries + LATENT]
    compressed_ref[...] = compressed
    latent = (compressed * inverse_rms(compressed) * latent_gain[2:3, :]).astype(BF16)
    latent_ref[...] = latent
    raw_key = projected[:, queries + LATENT : edge]
    key = rotated(raw_key, cos_ref[:, :LANES], sin_ref[:, :LANES])
    lane = lax.broadcasted_iota(jnp.int32, key.shape, 1)
    key = jnp.where(lane < ROPE, key, 0.0)
    key_low = key.astype(BF16)
    key_odd = pltpu.roll(key, ROPE, 1).astype(BF16)
    key_ref[...] = key_low
    row = lax.broadcasted_iota(jnp.int32, (tokens, tokens), 0)
    column = lax.broadcasted_iota(jnp.int32, (tokens, tokens), 1)
    allowed = (seg_col_ref[...] == seg_row_ref[...]) & (column <= row)
    scale = (NOPE + ROPE) ** (-0.5)
    for head in range(heads):
        block = slice(head * 2 * NOPE, (head + 1) * 2 * NOPE)
        up = w_ref[:, outer : outer + 2 * NOPE].reshape(owners, heads, short, 2 * NOPE)[:, head]
        up = up.reshape(LATENT, 2 * NOPE)
        expanded = dot_nn(latent, up).astype(BF16)
        expanded_ref[:, block] = expanded
        pair = nope + head // 2 * LANES
        raw = dot_nt(query_ref[:, head * NOPE : (head + 1) * NOPE], expanded[:, :NOPE]) + dot_nt(
            query_ref[:, pair : pair + LANES], key_odd if head % 2 else key_low
        )
        scores = jnp.where(allowed, raw * scale, -1e30)
        weight = jnp.exp(scores - jnp.max(scores, axis=-1, keepdims=True))
        probs = weight / jnp.sum(weight, axis=-1, keepdims=True)
        probs_ref[head] = probs
        attended_ref[:, head * VDIM : (head + 1) * VDIM] = dot_nn(
            probs.astype(BF16), expanded[:, NOPE:]
        ).astype(BF16)
    attended = attended_ref[...]
    for step, out_ref in enumerate((own_ref, send1_ref, send2_ref, send3_ref)):
        part = dot_nt(attended, w_ref[block_at(me_ref[0], step, width // piece, piece), edge:outer])
        out_ref[...] = part.astype(out_ref.dtype)


def dispatch_kernel(
    me_ref, stream_ref, a0_ref, a1_ref, a2_ref, a3_ref, gains_ref, t0_ref, t1_ref, middle_ref, mixed_ref, out_ref
):
    piece = a0_ref.shape[1]
    width = stream_ref.shape[1]
    count = width // piece
    owners, capacity, _ = out_ref.shape
    for step, a_ref in enumerate((a0_ref, a1_ref, a2_ref, a3_ref)):
        place = block_at(me_ref[0], step, count, piece)
        middle_ref[:, place] = stream_ref[:, place].astype(F32) + a_ref[...].astype(F32)
    middle = middle_ref[...]
    mixed = (middle * inverse_rms(middle) * gains_ref[1:2, :]).astype(BF16)
    mixed_ref[...] = mixed
    mine = mixed_ref[:, block_at(me_ref[0], 0, count, piece)]
    out_ref[:, :, width:] = dot_tn(t1_ref[...], mine).astype(BF16).reshape(owners, capacity, piece)
    out_ref[:, :, :width] = dot_tn(t0_ref[...], mixed).astype(BF16).reshape(owners, capacity, width)


def shared_kernel(
    me_ref,
    mixed_ref,
    cot_ref,
    w_ref,
    router_ref,
    own_ref,
    send1_ref,
    send2_ref,
    send3_ref,
    back_ref,
    probs_ref,
    grads_ref,
):
    width = mixed_ref.shape[1]
    piece = own_ref.shape[1]
    hidden_columns = w_ref.shape[1] // 3
    mixed = mixed_ref[...]
    cot = cot_ref[...]
    pre = dot_nn(mixed, w_ref[:, : 2 * hidden_columns])
    gate_pre, up_pre = pre[:, :hidden_columns], pre[:, hidden_columns:]
    act, slope = silu_parts(gate_pre)
    hidden = (act * up_pre).astype(BF16)
    hidden_grad = dot_nn(cot, w_ref[:, 2 * hidden_columns :])
    pair = jnp.concatenate([hidden_grad * up_pre * slope, hidden_grad * act], axis=1).astype(BF16)
    grads_ref[:, : 2 * hidden_columns] = dot_tn(mixed, pair).astype(BF16)
    grads_ref[:, 2 * hidden_columns :] = dot_tn(cot, hidden).astype(BF16)
    back_ref[...] = dot_nt(pair, w_ref[:, : 2 * hidden_columns])
    logits = dot_nn(mixed, router_ref[...])
    lane = lax.broadcasted_iota(jnp.int32, logits.shape, 1)
    logits = jnp.where(lane >= ROPE, logits, -1e30)
    weight = jnp.exp(logits - jnp.max(logits, axis=-1, keepdims=True))
    probs_ref[...] = weight / jnp.sum(weight, axis=-1, keepdims=True)
    for step, out_ref in enumerate((own_ref, send1_ref, send2_ref, send3_ref)):
        place = block_at(me_ref[0], step, width // piece, piece)
        part = dot_nt(hidden, w_ref[place, 2 * hidden_columns :])
        out_ref[...] = part.astype(out_ref.dtype)


def expert_back_kernel(split, *refs):
    if split:
        me_ref, base_ref, x0_ref, x1_ref, x2_ref, x3_ref = refs[:6]
        refs = refs[6:]
    else:
        me_ref, base_ref, x_ref = refs[:3]
        refs = refs[3:]
    c0_ref, c1_ref, c2_ref, c3_ref, wg_ref, wu_ref, wd_ref, router_ref = refs[:8]
    refs = refs[8:]
    if split:
        back_ref, c_ref, hg_ref, gr_ref, ur_ref, x_ref, wide_ref, down_ref, tall_ref = refs
    else:
        back_ref, c_ref, hg_ref, gr_ref, ur_ref, wide_ref, down_ref, tall_ref = refs
    sources, capacity, width = c_ref.shape
    rows = sources * capacity
    piece = c0_ref.shape[-1]
    count = width // piece
    hidden_columns = wd_ref.shape[1]
    padded = down_ref.shape[1]
    me = me_ref[0]

    @pl.when(pl.program_id(0) == 0)
    def _():
        rest = jnp.zeros((padded - hidden_columns, width), BF16)
        gate_up = jnp.concatenate([wg_ref[0], rest, wu_ref[0], rest], axis=0)
        tall_ref[...] = gate_up
        wide_ref[...] = gate_up.T
        down_ref[...] = jnp.concatenate([wd_ref[0], rest], axis=0).T

    for step, p_ref in enumerate((c0_ref, c1_ref, c2_ref, c3_ref)):
        c_ref[:, :, block_at(me, step, count, piece)] = p_ref[:, 0]
    if split:
        for step, p_ref in enumerate((x0_ref, x1_ref, x2_ref, x3_ref)):
            x_ref[:, :, block_at(me, step, count, piece)] = p_ref[...]
    x = x_ref[...].reshape(rows, width)
    expert = base_ref[0] + (1 if split else 0) + ROPE
    logits = dot_nn(x, router_ref[...])
    lane = lax.broadcasted_iota(jnp.int32, logits.shape, 1)
    logits = jnp.where(lane >= ROPE, logits, -1e30)
    weight = jnp.exp(logits - jnp.max(logits, axis=-1, keepdims=True))
    gate = jnp.sum(jnp.where(lane == expert, weight, 0.0), axis=-1, keepdims=True) / jnp.sum(
        weight, axis=-1, keepdims=True
    )
    pre = dot_nn(x, wide_ref[...])
    gate_pre, up_pre = pre[:, :padded], pre[:, padded:]
    hidden_cot = dot_nn(c_ref[...].reshape(rows, width), down_ref[...])
    act, slope = silu_parts(gate_pre)
    hidden = (act * up_pre).astype(BF16).astype(F32)
    gate_grad = jnp.sum(hidden * hidden_cot, axis=-1, keepdims=True)
    hidden_grad = gate * hidden_cot
    gate_rows = (hidden_grad * up_pre * slope).astype(BF16)
    up_rows = (hidden_grad * act).astype(BF16)
    hg_ref[...] = (gate * hidden).astype(BF16)[:, :hidden_columns]
    gr_ref[...] = gate_rows[:, :hidden_columns]
    ur_ref[...] = up_rows[:, :hidden_columns]
    high = gate_grad.astype(BF16).astype(F32)
    low = gate_grad - high
    beside = jnp.where(lane == 0, high, 0.0) + jnp.where(lane == 1, low, 0.0)
    back = dot_nn(jnp.concatenate([gate_rows, up_rows], axis=1), tall_ref[...])
    back_ref[:, :, :width] = back.astype(BF16).reshape(sources, capacity, width)
    back_ref[:, :, width:] = beside.astype(BF16).reshape(sources, capacity, LANES)


def expert_back(split, me, base, xs, cs, wg, wu, wd, router, router_at, chunk):
    owners, local, capacity, piece = cs[0].shape
    hidden, width = wg.shape[1:]
    local_index = 1 if split else 0
    rows = owners * capacity
    padded = -(-hidden // LANES) * LANES
    scalar = pl.BlockSpec(memory_space=pltpu.SMEM)
    row_spec = pl.BlockSpec((chunk * capacity, hidden), lambda c: (c, 0))
    row_shape = jax.ShapeDtypeStruct((rows, hidden), BF16)
    wide_spec = pl.BlockSpec((chunk, capacity, width), lambda c: (c, 0, 0))
    wide_shape = jax.ShapeDtypeStruct((owners, capacity, width), BF16)
    narrow_spec = pl.BlockSpec((chunk, capacity, piece), lambda c: (c, 0, 0))
    own_spec = pl.BlockSpec((chunk, capacity, piece), lambda c: (c, 0, width // piece))
    cot_spec = pl.BlockSpec((chunk, 1, capacity, piece), lambda c: (c, local_index, 0, 0))
    weight_spec = pl.BlockSpec((1, hidden, width), lambda c: (local_index, 0, 0))
    in_specs = [scalar, scalar]
    in_specs += [own_spec] + [narrow_spec] * 3 if split else [wide_spec]
    in_specs += [cot_spec] * 4 + [weight_spec] * 3 + [pl.BlockSpec((width, LANES), lambda c: (0, router_at))]
    out_specs = [pl.BlockSpec((chunk, capacity, width + LANES), lambda c: (c, 0, 0)), wide_spec]
    out_shape = [jax.ShapeDtypeStruct((owners, capacity, width + LANES), BF16), wide_shape]
    last_spec, last_shape = ([wide_spec], [wide_shape]) if split else ([], [])
    return pl.pallas_call(
        functools.partial(expert_back_kernel, split),
        grid=(owners // chunk,),
        in_specs=in_specs,
        out_specs=out_specs + [row_spec] * 3 + last_spec,
        out_shape=out_shape + [row_shape] * 3 + last_shape,
        scratch_shapes=[
            pltpu.VMEM((width, 2 * padded), BF16),
            pltpu.VMEM((width, padded), BF16),
            pltpu.VMEM((2 * padded, width), BF16),
        ],
        compiler_params=pltpu.CompilerParams(vmem_limit_bytes=VMEM_BYTES),
        cost_estimate=pl.CostEstimate(
            flops=100 * rows * hidden * width, bytes_accessed=24 * 1024 * 1024, transcendentals=0
        ),
        name="expert_back",
    )(me, base, *xs, *cs, wg, wu, wd, router)


def expert_out_kernel(hg_ref, wd_ref, out_ref):
    pieces, sources, capacity, piece = out_ref.shape
    out = dot_nn(hg_ref[...], wd_ref[0]).astype(BF16)
    for index in range(pieces):
        out_ref[index] = out[:, index * piece : (index + 1) * piece].reshape(sources, capacity, piece)


def expert_out(expert, hg, wd, owners, pieces, chunk):
    rows, hidden = hg.shape
    width = wd.shape[2]
    capacity = rows // owners
    piece = width // pieces
    return pl.pallas_call(
        expert_out_kernel,
        grid=(owners // chunk,),
        in_specs=[
            pl.BlockSpec((chunk * capacity, hidden), lambda c: (c, 0)),
            pl.BlockSpec((1, hidden, width), lambda c: (expert, 0, 0)),
        ],
        out_specs=pl.BlockSpec((pieces, chunk, capacity, piece), lambda c: (0, c, 0, 0)),
        out_shape=jax.ShapeDtypeStruct((pieces, owners, capacity, piece), BF16),
        compiler_params=pltpu.CompilerParams(vmem_limit_bytes=VMEM_BYTES),
        cost_estimate=pl.CostEstimate(
            flops=rows * hidden * width // 5, bytes_accessed=6 * 1024 * 102, transcendentals=0
        ),
        name="expert_out",
    )(hg, wd)


def expert_grads_kernel(
    x0_ref, c0_ref, hg0_ref, gr0_ref, ur0_ref, x1_ref, c1_ref, hg1_ref, gr1_ref, ur1_ref, dg_ref, du_ref, dd_ref
):
    owners, capacity, piece = x0_ref.shape
    rows = owners * capacity

    def step(x_ref, c_ref, hg_ref, gr_ref, ur_ref):
        x = x_ref[...].reshape(rows, piece)
        dg_ref[0] = dot_tn(gr_ref[...], x)
        du_ref[0] = dot_tn(ur_ref[...], x)
        dd_ref[0] = dot_tn(hg_ref[...], c_ref[...].reshape(rows, piece))

    pl.when(pl.program_id(0) == 0)(lambda: step(x0_ref, c0_ref, hg0_ref, gr0_ref, ur0_ref))
    pl.when(pl.program_id(0) == 1)(lambda: step(x1_ref, c1_ref, hg1_ref, gr1_ref, ur1_ref))


def expert_grads(first, second, pieces):
    owners, capacity, width = first[1].shape
    rows, hidden = first[2].shape
    piece = width // pieces
    row_spec = pl.BlockSpec((rows, hidden), lambda e, j: (0, 0))

    def specs(expert):
        stay = 0 if expert else pieces - 1
        wide = pl.BlockSpec(
            (owners, capacity, piece), lambda e, j: (0, 0, jnp.where(e == expert, j, stay))
        )
        return [wide, wide, row_spec, row_spec, row_spec]

    out_spec = pl.BlockSpec((1, hidden, piece), lambda e, j: (e, 0, j))
    out_shape = jax.ShapeDtypeStruct((2, hidden, width), F32)
    return pl.pallas_call(
        expert_grads_kernel,
        grid=(2, pieces),
        in_specs=specs(0) + specs(1),
        out_specs=[out_spec] * 3,
        out_shape=[out_shape] * 3,
        compiler_params=pltpu.CompilerParams(vmem_limit_bytes=VMEM_BYTES),
        cost_estimate=pl.CostEstimate(
            flops=rows * hidden * width, bytes_accessed=40 * 1024 * 102, transcendentals=0
        ),
        name="expert_grads",
    )(*first, *second)


def combine_kernel(
    me_ref, t0_ref, t1_ref, b0_ref, b1_ref, shared_ref, own_ref, probs_ref, send1_ref, send2_ref, send3_ref
):
    owners, capacity, _ = b0_ref.shape
    rows = owners * capacity
    width = shared_ref.shape[1]
    piece = own_ref.shape[1]
    me = me_ref[0]
    t0, t1 = t0_ref[...], t1_ref[...]
    lane = lax.broadcasted_iota(jnp.int32, (rows, LANES), 1)
    owner = lax.broadcasted_iota(jnp.int32, (rows, LANES), 0) // capacity
    spreads = []
    for index, b_ref in ((0, b0_ref), (1, b1_ref)):
        beside = b_ref[:, :, width:].reshape(rows, LANES).astype(F32)
        expert = 2 * owner + index
        spreads.append(
            (
                jnp.where(lane == expert + ROPE, beside[:, 0:1], 0.0)
                + jnp.where(lane == expert, beside[:, 1:2], 0.0)
            ).astype(BF16)
        )
    probs = dot_nn(t0, spreads[0]) + dot_nn(t1, spreads[1])
    probs = probs + pltpu.roll(probs, ROPE, 1)
    probs_ref[...] = probs
    high = probs.astype(BF16)
    low = (probs - high.astype(F32)).astype(BF16)
    short = lax.broadcasted_iota(jnp.int32, probs.shape, 1)
    message = jnp.where(short >= ROPE, high.astype(F32), low.astype(F32)).astype(BF16)
    for step, out_ref in enumerate((own_ref, send1_ref, send2_ref, send3_ref)):
        place = block_at(me, step, width // piece, piece)
        part = (
            dot_nn(t0, b0_ref[:, :, place].reshape(rows, piece))
            + dot_nn(t1, b1_ref[:, :, place].reshape(rows, piece))
            + shared_ref[:, place]
        )
        if step == 0:
            own_ref[...] = part
        else:
            out_ref[:, :piece] = part.astype(BF16)
            out_ref[:, piece:] = message


def attend_back_kernel(
    me_ref,
    core_ref,
    stream_ref,
    cot_ref,
    middle_ref,
    a0_ref,
    a1_ref,
    a2_ref,
    a3_ref,
    r1_ref,
    r2_ref,
    r3_ref,
    probs_own_ref,
    router_probs_ref,
    w_ref,
    router_ref,
    mixed_ref,
    normed_ref,
    query_ref,
    expanded_ref,
    key_ref,
    latent_ref,
    compressed_ref,
    probs_ref,
    attended_ref,
    gains_ref,
    latent_gain_ref,
    cos_ref,
    sin_ref,
    keep_ref,
    pass_ref,
    middle_grad_ref,
    own_ref,
    send1_ref,
    send2_ref,
    send3_ref,
    scr_ref,
    low_ref,
    wide_ref,
    sems,
):
    heads, tokens, _ = probs_ref.shape
    width = stream_ref.shape[1]
    piece = own_ref.shape[1]
    nope = heads * NOPE
    queries = nope + heads * ROPE
    edge = queries + LATENT + LANES
    outer = edge + heads * VDIM
    owners = 32
    shard = width // owners
    short = LATENT // owners
    count = width // piece
    me = me_ref[0]
    probs_grad = probs_own_ref[...]
    for r_ref in (r1_ref, r2_ref, r3_ref):
        other = r_ref[:, piece:].astype(F32)
        probs_grad = probs_grad + other + pltpu.roll(other, ROPE, 1)
    router_probs = router_probs_ref[...]
    logits_low = (
        router_probs * (probs_grad - jnp.sum(router_probs * probs_grad, axis=-1, keepdims=True))
    ).astype(BF16)
    router_back = dot_nt(logits_low, router_ref[...])
    for step, a_ref in enumerate((a0_ref, a1_ref, a2_ref, a3_ref)):
        wide_ref[:, block_at(me, step, count, piece)] = a_ref[...].astype(F32)
    mixed_grad = wide_ref[...] + router_back
    middle = middle_ref[...]
    norm_grad, second_gain_rows = rms_back(middle, inverse_rms(middle), gains_ref[1:2, :], mixed_grad)
    second_gain_grad = jnp.sum(second_gain_rows, axis=0, keepdims=True)
    middle_grad = cot_ref[...] + norm_grad
    middle_grad_ref[...] = middle_grad
    middle_low = middle_grad.astype(BF16)
    attended_grad = dot_nn(middle_low, w_ref[:, edge:outer]).astype(BF16)
    scale = (NOPE + ROPE) ** (-0.5)
    key_low = key_ref[...]
    key_odd = pltpu.roll(key_low.astype(F32), ROPE, 1).astype(BF16)
    latent = latent_ref[...]
    latent_part = jnp.zeros((tokens, LATENT), F32)
    key_even_grad = jnp.zeros((tokens, LANES), F32)
    key_odd_grad = jnp.zeros((tokens, LANES), F32)
    rope_grads = []
    grads4 = scr_ref.reshape(owners, shard, scr_ref.shape[1])
    for head in range(heads):
        pair = nope + head // 2 * LANES
        expanded = expanded_ref[:, head * 2 * NOPE : (head + 1) * 2 * NOPE]
        probs = probs_ref[head]
        head_grad = attended_grad[:, head * VDIM : (head + 1) * VDIM]
        value_grad = dot_tn(probs.astype(BF16), head_grad)
        probs_att = dot_nt(head_grad, expanded[:, NOPE:])
        scores = probs * (probs_att - jnp.sum(probs * probs_att, axis=-1, keepdims=True))
        raw_low = (scores * scale).astype(BF16)
        low_ref[:, head * NOPE : (head + 1) * NOPE] = dot_nn(raw_low, expanded[:, :NOPE]).astype(BF16)
        turn_grad = dot_nn(raw_low, key_odd if head % 2 else key_low)
        if head % 2:
            rope_grads[-1] = rope_grads[-1] + turn_grad
            key_odd_grad += dot_tn(raw_low, query_ref[:, pair : pair + LANES])
        else:
            rope_grads.append(turn_grad)
            key_even_grad += dot_tn(raw_low, query_ref[:, pair : pair + LANES])
        key_grad = dot_tn(raw_low, query_ref[:, head * NOPE : (head + 1) * NOPE])
        expanded_low = jnp.concatenate([key_grad, value_grad], axis=1).astype(BF16)
        up = w_ref[:, outer : outer + 2 * NOPE].reshape(owners, heads, short, 2 * NOPE)[:, head]
        up = up.reshape(LATENT, 2 * NOPE)
        latent_part += dot_nt(expanded_low, up)
        grads4[:, head * short : (head + 1) * short, outer : outer + 2 * NOPE] = (
            dot_tn(latent, expanded_low).astype(BF16).reshape(owners, short, 2 * NOPE)
        )
    rope_grad = jnp.concatenate(rope_grads, axis=1)
    low_ref[:, nope:queries] = rotated(rope_grad, cos_ref[...], -sin_ref[...]).astype(BF16)
    compressed = compressed_ref[...]
    latent_grad, latent_gain_rows = rms_back(
        compressed, inverse_rms(compressed), latent_gain_ref[2:3, :], latent_part
    )
    latent_gain_grad = jnp.sum(latent_gain_rows, axis=0, keepdims=True)
    low_ref[:, queries : queries + LATENT] = latent_grad.astype(BF16)
    lane = lax.broadcasted_iota(jnp.int32, (tokens, LANES), 1)
    key_grad = jnp.where(lane < ROPE, key_even_grad + pltpu.roll(key_odd_grad, ROPE, 1), 0.0)
    key_grad = rotated(key_grad, cos_ref[:, :LANES], -sin_ref[:, :LANES])
    low_ref[:, queries + LATENT : edge] = jnp.where(lane < ROPE, key_grad, 0.0).astype(BF16)
    low = low_ref[...]
    for step, out_ref in enumerate((own_ref, send1_ref, send2_ref, send3_ref)):
        place = block_at(me, step, count, piece)
        part = dot_nt(low, w_ref[place, :edge])
        wide_ref[:, place] = part
        out_ref[...] = part.astype(out_ref.dtype)
    stream = stream_ref[...].astype(F32)
    first_gain_grad = jnp.sum(wide_ref[...] * (stream * inverse_rms(stream)), axis=0, keepdims=True)
    late = dot_tn(normed_ref[...], low[:, queries:])
    sub = lax.broadcasted_iota(jnp.int32, (LANES, width), 0)
    gain_columns = (
        jnp.where(sub == ROPE, first_gain_grad, 0.0)
        + jnp.where(sub == ROPE + 1, second_gain_grad * (1.0 / count), 0.0)
    ).T
    key_columns = (late[:, LATENT:] + gain_columns).reshape(owners, shard, LANES)
    sub = lax.broadcasted_iota(jnp.int32, (LANES, LATENT), 0)
    latent_columns = jnp.where(sub == ROPE + 2, latent_gain_grad, 0.0).T.reshape(owners, short, LANES)
    grads4[:, :, queries : queries + LATENT] = (
        late[:, :LATENT].astype(BF16).reshape(owners, shard, LATENT)
    )
    grads4[:, :, queries + LATENT : edge] = key_columns.astype(BF16)
    grads4[:, :short, queries + LATENT : edge] = (key_columns[:, :short] + latent_columns).astype(BF16)
    scr_ref[:, edge:outer] = dot_tn(middle_low, attended_ref[...]).astype(BF16)
    scr_ref[:, :queries] = dot_tn(normed_ref[...], low[:, :queries]).astype(BF16)
    router_grad = dot_tn(mixed_ref[...], logits_low)
    scr_ref[:, outer + 2 * NOPE :] = router_grad[:, ROPE:].astype(BF16)
    halves = scr_ref.reshape(owners // 2, 2, shard, scr_ref.shape[1])
    core = core_ref[0]
    first = pltpu.make_async_copy(halves.at[:, 1 - core], pass_ref, sems.at[0])
    second = pltpu.make_async_copy(halves.at[:, core], keep_ref, sems.at[1])
    first.start()
    second.start()
    first.wait()
    second.wait()


def unpack_kernel(parts_ref, query_ref, late_ref, output_ref, up_ref, router_ref):
    heads = up_ref.shape[1] // (2 * NOPE)
    short = up_ref.shape[0]
    nope = heads * NOPE
    queries = nope + heads * ROPE
    edge = queries + LATENT + LANES
    outer = edge + heads * VDIM
    total = jnp.sum(parts_ref[...].astype(F32), axis=0)
    for head in range(heads):
        start = head * (NOPE + ROPE)
        query_ref[:, start : start + NOPE] = total[:, head * NOPE : (head + 1) * NOPE]
        query_ref[:, start + NOPE : start + NOPE + ROPE] = total[
            :, nope + head * ROPE : nope + (head + 1) * ROPE
        ]
        up_ref[:, head * 2 * NOPE : (head + 1) * 2 * NOPE] = total[
            head * short : (head + 1) * short, outer : outer + 2 * NOPE
        ]
    late_ref[...] = total[:, queries:edge]
    output_ref[...] = total[:, edge:outer]
    router_ref[...] = total[:, outer + 2 * NOPE :]


def late_kernel(own_ref, r1_ref, r2_ref, r3_ref, down_ref, gains_ref):
    total = own_ref[...] + r1_ref[...] + r2_ref[...] + r3_ref[...]
    down_ref[...] = total[:, : down_ref.shape[1]]
    columns = total[:, LATENT:]
    columns = jnp.concatenate([columns, jnp.zeros(columns.shape, F32)], axis=0)
    gains_ref[...] = columns.T[ROPE : ROPE + 8, :]


def stream_kernel(me_ref, middle_grad_ref, stream_ref, gains_ref, a0_ref, a1_ref, a2_ref, a3_ref, out_ref, wide_ref):
    piece = a0_ref.shape[1]
    count = stream_ref.shape[1] // piece
    for step, a_ref in enumerate((a0_ref, a1_ref, a2_ref, a3_ref)):
        wide_ref[:, block_at(me_ref[0], step, count, piece)] = a_ref[...].astype(F32)
    stream = stream_ref[...].astype(F32)
    norm_grad, _ = rms_back(stream, inverse_rms(stream), gains_ref[0:1, :], wide_ref[...])
    out_ref[...] = middle_grad_ref[...] + norm_grad


def routed_kernel(t0_ref, t1_ref, o_ref, own_ref, r1_ref, r2_ref, r3_ref, out_ref):
    owners, _, capacity, piece = o_ref.shape
    rows = owners * capacity
    total = own_ref[...]
    for r_ref in (r1_ref, r2_ref, r3_ref):
        total = total + r_ref[...].astype(F32)
    for index, t_ref in ((0, t0_ref), (1, t1_ref)):
        total = total + dot_nn(t_ref[...], o_ref[:, index].reshape(rows, piece))
    out_ref[...] = total.astype(BF16)


def result_kernel(me_ref, middle_ref, a0_ref, a1_ref, a2_ref, a3_ref, out_ref):
    piece = a0_ref.shape[1]
    count = middle_ref.shape[1] // piece
    for step, a_ref in enumerate((a0_ref, a1_ref, a2_ref, a3_ref)):
        place = block_at(me_ref[0], step, count, piece)
        out_ref[:, place] = middle_ref[:, place] + a_ref[...].astype(F32)


def shift(array, step):
    size = lax.axis_size("tensor")
    return lax.ppermute(array, "tensor", [(i, (i + step) % size) for i in range(size)])


def send_blocks(sends):
    return [shift(array, step + 1) for step, array in enumerate(sends)]


def share_small(low):
    size = lax.axis_size("tensor")
    return [low] + [shift(low, size - step) for step in range(1, size)]


def ring_first(rows):
    return shift(rows, 1), shift(rows, lax.axis_size("tensor") - 1)


def ring_second(rows, before, after):
    half = rows.shape[0] // 2
    across = [shift(before[:half], 1), shift(after[half:], lax.axis_size("tensor") - 1)]
    return [rows, after, jnp.concatenate(across, axis=0), before]


def after(array, *others):
    return lax.optimization_barrier((array, *others))[0]


def exchange(rows):
    shape = rows.shape
    return lax.all_to_all(
        rows.reshape(shape[0], -1, shape[-1]), "expert", split_axis=0, concat_axis=0, tiled=True
    ).reshape(shape)


def per_device(
    stream,
    segment_ids,
    expert_ids,
    first_gain,
    query_proj,
    latent_down,
    latent_gain,
    latent_up,
    output_proj,
    second_gain,
    router_proj,
    shared_gate,
    shared_up,
    shared_down,
    expert_gate,
    expert_up,
    expert_down,
    cotangent,
):
    tokens, width = stream.shape
    owners = lax.axis_size("expert")
    tensors = lax.axis_size("tensor")
    shard = query_proj.shape[0]
    heads = query_proj.shape[1] // (NOPE + ROPE)
    short = latent_up.shape[0]
    experts = router_proj.shape[1]
    hidden_columns = shared_gate.shape[1]
    local, _, expert_hidden = expert_gate.shape
    capacity = tokens * TOPK * 4 // (3 * experts)
    rows = owners * capacity
    piece = width // tensors
    nope = heads * NOPE
    queries = nope + heads * ROPE
    edge = queries + LATENT + LANES
    outer = edge + heads * VDIM
    me = lax.axis_index("tensor").astype(jnp.int32).reshape(1)
    base = (lax.axis_index("expert") * local).astype(jnp.int32).reshape(1)
    core = lax.rem(lax.axis_index("expert"), 2).astype(jnp.int32).reshape(1)
    smem = {0: pltpu.SMEM}

    gains = jnp.concatenate(
        [
            first_gain[:, None],
            second_gain[:, None],
            jnp.pad(latent_gain, (0, shard - short))[:, None],
            jnp.zeros((shard, ROPE - 3), BF16),
        ],
        axis=1,
    )
    by_head = query_proj.reshape(shard, heads, NOPE + ROPE)
    pack_one = jnp.concatenate(
        [
            by_head[:, :, :NOPE].reshape(shard, nope),
            by_head[:, :, NOPE:].reshape(shard, heads * ROPE),
            latent_down,
            router_proj,
            output_proj.T,
            latent_up.reshape(short, heads, 2 * NOPE).transpose(1, 0, 2).reshape(shard, 2 * NOPE),
            gains,
        ],
        axis=1,
    )
    pack_two = jnp.concatenate([shared_gate, shared_up, shared_down.T], axis=1)
    one = lax.all_gather(pack_one, "expert", axis=0, tiled=True)
    two = lax.all_gather(pack_two, "expert", axis=0, tiled=True)

    position = jnp.arange(tokens).astype(F32)
    exponent = jnp.arange(ROPE // 2).astype(F32) * (2.0 / ROPE)
    angles = position[:, None] * jnp.exp(-math.log(ROTARY_BASE) * exponent)[None, :]
    cosine = jnp.tile(jnp.cos(angles), (1, 2 * heads))
    sine = jnp.sin(angles)
    sine = jnp.tile(jnp.concatenate([-sine, sine], axis=1), (1, heads))

    t0, t1, cot_low, cot_out = run(
        routing_kernel,
        [
            ((tokens, rows), BF16),
            ((tokens, rows), BF16),
            ((tokens, width), BF16),
            ((owners, local, capacity, piece), BF16),
        ],
        [me, expert_ids.T, cotangent],
        2 * local * tokens * rows * (piece + experts),
        places=smem,
        name="routing",
    )

    cot_own = exchange(cot_out)
    cot_before, cot_after = ring_first(cot_own)
    (
        own,
        send1,
        send2,
        send3,
        normed,
        query,
        expanded,
        key,
        latent,
        compressed,
        probs,
        attended,
        gain_rows,
        latent_gain_rows,
    ) = run(
        attend_kernel,
        [
            ((tokens, piece), F32),
            ((tokens, piece), BF16),
            ((tokens, piece), BF16),
            ((tokens, piece), BF16),
            ((tokens, width), BF16),
            ((tokens, queries), BF16),
            ((tokens, heads * 2 * NOPE), BF16),
            ((tokens, LANES), BF16),
            ((tokens, LATENT), BF16),
            ((tokens, LATENT), F32),
            ((heads, tokens, tokens), F32),
            ((tokens, heads * VDIM), BF16),
            ((8, width), F32),
            ((8, LATENT), F32),
        ],
        [after(me, cot_own), stream, one, segment_ids, segment_ids.T, cosine, sine],
        2 * tokens * width * outer,
        places=smem,
        name="attend",
    )
    got = send_blocks([send1, send2, send3])
    attention = (own + got[0].astype(F32) + got[1].astype(F32) + got[2].astype(F32)).astype(BF16)
    attention = after(attention, cot_before, cot_after)
    middle, mixed, x_out = run(
        dispatch_kernel,
        [
            ((tokens, width), F32),
            ((tokens, width), BF16),
            ((owners, capacity, width + piece), BF16),
        ],
        [me, stream, *share_small(attention), gain_rows, t0, t1],
        2 * tokens * rows * (width + piece),
        places=smem,
        name="dispatch",
    )
    x_in = exchange(x_out)
    cots = ring_second(cot_own, cot_before, cot_after)
    x1s = x_in[:, :, width:]
    x1_before, x1_after = ring_first(x1s)
    x1s = [x_in] + ring_second(x1s, x1_before, x1_after)[1:]
    router_block = one[:, queries + LATENT : edge]
    (
        shared_own,
        shared1,
        shared2,
        shared3,
        shared_back,
        router_probs,
        shared_grads,
    ) = run(
        shared_kernel,
        [
            ((tokens, piece), F32),
            ((tokens, piece), BF16),
            ((tokens, piece), BF16),
            ((tokens, piece), BF16),
            ((tokens, width), F32),
            ((tokens, LANES), F32),
            ((width, 3 * hidden_columns), BF16),
        ],
        [me, mixed, cot_low, two, router_block],
        18 * tokens * width * hidden_columns,
        places=smem,
        name="shared",
    )
    base = after(base, shared_back)

    gate_t = expert_gate.transpose(0, 2, 1)
    up_t = expert_up.transpose(0, 2, 1)
    chunk = owners // 2
    back0, c0, hg0, gr0, ur0 = expert_back(
        False, me, base, [x_in], cots, gate_t, up_t, expert_down, one, edge // LANES - 1, chunk // 2
    )
    back0 = exchange(back0)
    back1, c1, hg1, gr1, ur1, x1 = expert_back(
        True, me, after(base, hg0), x1s, cots, gate_t, up_t, expert_down, one, edge // LANES - 1, chunk // 2
    )
    back1 = exchange(after(back1, back0))
    gr0 = after(gr0, back0)
    gate_grad, up_grad, down_grad = expert_grads(
        (x_in, c0, hg0, gr0, ur0), (x1, c1, hg1, gr1, ur1), tensors
    )
    out0 = expert_out(0, hg0, expert_down, owners, tensors, chunk)
    out1 = expert_out(1, after(hg1, out0), expert_down, owners, tensors, chunk)
    out_rows = [
        lax.psum_scatter(out, "tensor", scatter_dimension=0, tiled=True).reshape(owners, 1, capacity, piece)
        for out in (out0, out1)
    ]

    out_rows = exchange(after(jnp.concatenate(out_rows, axis=1), back1, gate_grad))
    own, probs_own, send1, send2, send3 = run(
        combine_kernel,
        [
            ((tokens, piece), F32),
            ((tokens, LANES), F32),
            ((tokens, piece + LANES), BF16),
            ((tokens, piece + LANES), BF16),
            ((tokens, piece + LANES), BF16),
        ],
        [after(me, out1, gate_grad), t0, t1, back0, back1, shared_back],
        2 * tokens * rows * (width + piece),
        places=smem,
        name="combine",
    )
    got = send_blocks([send1, send2, send3])
    shared_sum = lax.psum_scatter(
        after(shared_grads, own), "expert", scatter_dimension=0, tiled=True
    )
    mixed_sum = (
        own
        + got[0][:, :piece].astype(F32)
        + got[1][:, :piece].astype(F32)
        + got[2][:, :piece].astype(F32)
    ).astype(BF16)
    keep, passed, middle_grad, own, send1, send2, send3 = run(
        attend_back_kernel,
        [
            ((owners // 2, shard, outer + 2 * NOPE + experts), BF16),
            ((owners // 2, shard, outer + 2 * NOPE + experts), BF16),
            ((tokens, width), F32),
            ((tokens, piece), F32),
            ((tokens, piece), BF16),
            ((tokens, piece), BF16),
            ((tokens, piece), BF16),
        ],
        [
            after(me, out_rows),
            core,
            stream,
            cotangent,
            middle,
            *share_small(mixed_sum),
            *got,
            probs_own,
            router_probs,
            one,
            router_block,
            mixed,
            normed,
            query,
            expanded,
            key,
            latent,
            compressed,
            probs,
            attended,
            gain_rows,
            latent_gain_rows,
            cosine,
            sine,
        ],
        2 * tokens * width * (3 * edge + 2 * outer),
        scratch=[
            pltpu.VMEM((width, outer + 2 * NOPE + experts), BF16),
            pltpu.VMEM((tokens, edge), BF16),
            pltpu.VMEM((tokens, width), F32),
            pltpu.SemaphoreType.DMA((2,)),
        ],
        places={0: pltpu.SMEM, 1: pltpu.SMEM},
        out_places={0: pl.ANY, 1: pl.ANY},
        name="attend_back",
    )
    paired = lax.ppermute(passed, "expert", [(i, i ^ 1) for i in range(owners)])
    paired = (keep.astype(F32) + paired.astype(F32)).astype(BF16)
    parts = lax.all_to_all(
        paired,
        "expert",
        split_axis=0,
        concat_axis=0,
        tiled=True,
        axis_index_groups=[[2 * i + c for i in range(owners // 2)] for c in range(2)],
    )
    query_grad, late, output_grad, latent_up_grad, router_grad = run(
        unpack_kernel,
        [
            (query_proj.shape, F32),
            ((shard, edge - queries), F32),
            ((shard, heads * VDIM), F32),
            (latent_up.shape, F32),
            (router_proj.shape, F32),
        ],
        [parts],
        0,
        name="unpack",
    )
    latent_down_grad, gain_grads = run(
        late_kernel,
        [(latent_down.shape, F32), ((8, LANES), F32)],
        [late, *(shift(late, step) for step in range(1, tensors))],
        0,
        name="late",
    )
    got = send_blocks([send1, send2, send3])
    first_sum = (own + got[0].astype(F32) + got[1].astype(F32) + got[2].astype(F32)).astype(BF16)
    (stream_grad,) = run(
        stream_kernel,
        [((tokens, width), F32)],
        [me, middle_grad, stream, gain_rows, *share_small(first_sum)],
        0,
        scratch=[pltpu.VMEM((tokens, width), F32)],
        places=smem,
        name="stream",
    )

    got = send_blocks([shared1, shared2, shared3])
    (branch,) = run(
        routed_kernel,
        [((tokens, piece), BF16)],
        [t0, t1, out_rows, shared_own, *got],
        4 * tokens * rows * piece,
        name="routed",
    )
    (result,) = run(
        result_kernel,
        [((tokens, width), F32)],
        [me, middle, *share_small(branch)],
        0,
        places=smem,
        name="result",
    )

    shared_sum = shared_sum.astype(F32)
    return (
        result,
        stream_grad,
        gain_grads[0, :shard],
        query_grad,
        latent_down_grad,
        gain_grads[2, :short],
        latent_up_grad,
        output_grad.T,
        gain_grads[1, :shard],
        router_grad,
        shared_sum[:, :hidden_columns],
        shared_sum[:, hidden_columns : 2 * hidden_columns],
        shared_sum[:, 2 * hidden_columns :].T,
        gate_grad.transpose(0, 2, 1),
        up_grad.transpose(0, 2, 1),
        down_grad,
    )


def solution(mesh):
    placed = (
        P("expert", None),
        P("expert", None),
        P("expert", None),
        P("expert"),
        P("expert", "tensor"),
        P("expert", None),
        P("expert"),
        P("expert", "tensor"),
        P("tensor", "expert"),
        P("expert"),
        P("expert", None),
        P("expert", "tensor"),
        P("expert", "tensor"),
        P("tensor", "expert"),
        P("expert", None, "tensor"),
        P("expert", None, "tensor"),
        P("expert", "tensor", None),
        P("expert", None),
    )
    return jax.shard_map(
        per_device,
        mesh=mesh,
        in_specs=placed,
        out_specs=(
            P("expert", None),
            P("expert", None),
            P("expert"),
            P("expert", "tensor"),
            P("expert", None),
            P("expert"),
            P("expert", "tensor"),
            P("tensor", "expert"),
            P("expert"),
            P("expert", None),
            P("expert", "tensor"),
            P("expert", "tensor"),
            P("tensor", "expert"),
            P("expert", None, "tensor"),
            P("expert", None, "tensor"),
            P("expert", "tensor", None),
        ),
        check_vma=False,
    )
```

```python
import functools
import math

import jax
import jax.numpy as jnp
from jax import lax
from jax.experimental import pallas as pl
from jax.experimental.pallas import tpu as pltpu
from jax.sharding import PartitionSpec as P

NOPE = 128
ROPE = 64
VDIM = 128
LATENT = 512
TOPK = 6
EPSILON = 1e-06
ROTARY_BASE = 10000.0

BF16 = jnp.bfloat16
F32 = jnp.float32
VMEM_BYTES = 60 * 1024 * 1024
LANES = 128
COST_SCALE = 10


def dot_nn(left, right):
    return lax.dot_general(left, right, (((1,), (0,)), ((), ())), preferred_element_type=F32)


def dot_nt(left, right):
    return lax.dot_general(left, right, (((1,), (1,)), ((), ())), preferred_element_type=F32)


def dot_tn(left, right):
    return lax.dot_general(left, right, (((0,), (0,)), ((), ())), preferred_element_type=F32)


def silu_parts(pre_values):
    sigmoid_value = 1.0 / (1.0 + jnp.exp(-pre_values))
    return (pre_values * sigmoid_value, sigmoid_value * (1.0 + pre_values * (1.0 - sigmoid_value)))


def inverse_rms(values):
    return lax.rsqrt(jnp.mean(values * values, axis=-1, keepdims=True) + EPSILON)


def rms_back(values, scale, gain, grad):
    normed = values * scale
    weighted = grad * gain
    return (
        scale * (weighted - normed * jnp.mean(weighted * normed, axis=-1, keepdims=True)),
        grad * normed,
    )


def turned(values):
    width = values.shape[1]
    lane = lax.broadcasted_iota(jnp.int32, values.shape, 1) % ROPE
    half = ROPE // 2
    return jnp.where(
        lane < half, pltpu.roll(values, width - half, 1), pltpu.roll(values, half, 1)
    )


def rotated(values, cosine, sine):
    return values * cosine + turned(values) * sine


def block_at(me, step, count, width):
    return pl.ds(pl.multiple_of(lax.rem(me + step, count) * width, width), width)


def run(kernel, outs, args, flops, scratch=(), name=None, places=None, aliases=None, out_places=None):
    places = places or {}
    out_places = out_places or {}
    in_specs = [pl.BlockSpec(memory_space=places.get(i, pltpu.VMEM)) for i in range(len(args))]
    out_specs = [pl.BlockSpec(memory_space=out_places.get(i, pltpu.VMEM)) for i in range(len(outs))]
    moved = sum(a.size * a.dtype.itemsize for a in args) + sum(
        math.prod(shape) * jnp.dtype(dtype).itemsize for shape, dtype in outs
    )
    return pl.pallas_call(
        kernel,
        in_specs=in_specs,
        out_specs=out_specs,
        out_shape=[jax.ShapeDtypeStruct(shape, dtype) for shape, dtype in outs],
        scratch_shapes=list(scratch),
        input_output_aliases=aliases or {},
        compiler_params=pltpu.CompilerParams(vmem_limit_bytes=VMEM_BYTES),
        cost_estimate=pl.CostEstimate(
            flops=flops // COST_SCALE, bytes_accessed=moved // COST_SCALE, transcendentals=0
        ),
        name=name,
    )(*args)


def routing_kernel(me_ref, ids_ref, cot_ref, t0_ref, t1_ref, low_ref, out_ref):
    choices, tokens = ids_ref.shape
    owners, local, capacity, piece = out_ref.shape
    experts = owners * local
    rows = owners * capacity
    expert = lax.broadcasted_iota(jnp.int32, (experts, tokens), 0)
    chosen = jnp.zeros((experts, tokens), F32)
    for choice in range(choices):
        chosen += jnp.where(ids_ref[choice : choice + 1, :] == expert, 1.0, 0.0)
    before = jnp.where(
        lax.broadcasted_iota(jnp.int32, (tokens, tokens), 0)
        < lax.broadcasted_iota(jnp.int32, (tokens, tokens), 1),
        1.0,
        0.0,
    ).astype(BF16)
    place = dot_nn(chosen.astype(BF16), before)
    place = jnp.where(chosen > 0.5, place, -1.0).astype(BF16)
    low = cot_ref[...].astype(BF16)
    low_ref[...] = low
    mine = cot_ref[:, block_at(me_ref[0], 0, cot_ref.shape[1] // piece, piece)].astype(BF16)
    slot = (lax.broadcasted_iota(jnp.int32, (tokens, rows), 1) % capacity).astype(F32)
    for index, t_ref in ((0, t0_ref), (1, t1_ref)):
        spread = jnp.where(
            lax.broadcasted_iota(jnp.int32, (experts, rows), 0)
            == lax.broadcasted_iota(jnp.int32, (experts, rows), 1) // capacity * local + index,
            1.0,
            0.0,
        ).astype(BF16)
        wanted = dot_tn(place, spread)
        matrix = jnp.where(wanted == slot, 1.0, 0.0).astype(BF16)
        t_ref[...] = matrix
        out_ref[:, index] = dot_tn(matrix, mine).astype(BF16).reshape(owners, capacity, piece)


def attend_kernel(
    me_ref,
    stream_ref,
    w_ref,
    seg_row_ref,
    seg_col_ref,
    cos_ref,
    sin_ref,
    own_ref,
    send1_ref,
    send2_ref,
    send3_ref,
    normed_ref,
    query_ref,
    expanded_ref,
    key_ref,
    latent_ref,
    compressed_ref,
    probs_ref,
    attended_ref,
    gains_ref,
    latent_gain_ref,
):
    heads, tokens, _ = probs_ref.shape
    width = stream_ref.shape[1]
    piece = own_ref.shape[1]
    nope = heads * NOPE
    queries = nope + heads * ROPE
    edge = queries + LATENT + LANES
    outer = edge + heads * VDIM
    owners = 32
    columns = jnp.concatenate(
        [w_ref[:, outer + 2 * NOPE :].astype(F32), jnp.zeros((width, ROPE), F32)], axis=1
    )
    gains = columns.T[:8, :]
    gains_ref[...] = gains
    shard = width // owners
    short = LATENT // owners
    latent_gain = (
        columns.reshape(owners, shard, LANES)[:, :short, :].reshape(LATENT, LANES).T[:8, :]
    )
    latent_gain_ref[...] = latent_gain
    stream = stream_ref[...].astype(F32)
    normed = (stream * inverse_rms(stream) * gains[0:1, :]).astype(BF16)
    normed_ref[...] = normed
    projected = dot_nn(normed, w_ref[:, :edge])
    query_ref[:, :nope] = projected[:, :nope].astype(BF16)
    query_ref[:, nope:] = rotated(projected[:, nope:queries], cos_ref[...], sin_ref[...]).astype(BF16)
    compressed = projected[:, queries : queries + LATENT]
    compressed_ref[...] = compressed
    latent = (compressed * inverse_rms(compressed) * latent_gain[2:3, :]).astype(BF16)
    latent_ref[...] = latent
    raw_key = projected[:, queries + LATENT : edge]
    key = rotated(raw_key, cos_ref[:, :LANES], sin_ref[:, :LANES])
    lane = lax.broadcasted_iota(jnp.int32, key.shape, 1)
    key = jnp.where(lane < ROPE, key, 0.0)
    key_low = key.astype(BF16)
    key_odd = pltpu.roll(key, ROPE, 1).astype(BF16)
    key_ref[...] = key_low
    row = lax.broadcasted_iota(jnp.int32, (tokens, tokens), 0)
    column = lax.broadcasted_iota(jnp.int32, (tokens, tokens), 1)
    allowed = (seg_col_ref[...] == seg_row_ref[...]) & (column <= row)
    scale = (NOPE + ROPE) ** (-0.5)
    for head in range(heads):
        block = slice(head * 2 * NOPE, (head + 1) * 2 * NOPE)
        up = w_ref[:, outer : outer + 2 * NOPE].reshape(owners, heads, short, 2 * NOPE)[:, head]
        up = up.reshape(LATENT, 2 * NOPE)
        expanded = dot_nn(latent, up).astype(BF16)
        expanded_ref[:, block] = expanded
        pair = nope + head // 2 * LANES
        raw = dot_nt(query_ref[:, head * NOPE : (head + 1) * NOPE], expanded[:, :NOPE]) + dot_nt(
            query_ref[:, pair : pair + LANES], key_odd if head % 2 else key_low
        )
        scores = jnp.where(allowed, raw * scale, -1e30)
        weight = jnp.exp(scores - jnp.max(scores, axis=-1, keepdims=True))
        probs = weight / jnp.sum(weight, axis=-1, keepdims=True)
        probs_ref[head] = probs
        attended_ref[:, head * VDIM : (head + 1) * VDIM] = dot_nn(
            probs.astype(BF16), expanded[:, NOPE:]
        ).astype(BF16)
    attended = attended_ref[...]
    for step, out_ref in enumerate((own_ref, send1_ref, send2_ref, send3_ref)):
        part = dot_nt(attended, w_ref[block_at(me_ref[0], step, width // piece, piece), edge:outer])
        out_ref[...] = part.astype(out_ref.dtype)


def dispatch_kernel(
    me_ref, stream_ref, a0_ref, a1_ref, a2_ref, a3_ref, gains_ref, t0_ref, t1_ref, middle_ref, mixed_ref, out_ref
):
    piece = a0_ref.shape[1]
    width = stream_ref.shape[1]
    count = width // piece
    owners, capacity, _ = out_ref.shape
    for step, a_ref in enumerate((a0_ref, a1_ref, a2_ref, a3_ref)):
        place = block_at(me_ref[0], step, count, piece)
        middle_ref[:, place] = stream_ref[:, place].astype(F32) + a_ref[...].astype(F32)
    middle = middle_ref[...]
    mixed = (middle * inverse_rms(middle) * gains_ref[1:2, :]).astype(BF16)
    mixed_ref[...] = mixed
    mine = mixed_ref[:, block_at(me_ref[0], 0, count, piece)]
    out_ref[:, :, width:] = dot_tn(t1_ref[...], mine).astype(BF16).reshape(owners, capacity, piece)
    out_ref[:, :, :width] = dot_tn(t0_ref[...], mixed).astype(BF16).reshape(owners, capacity, width)


def shared_kernel(
    me_ref,
    mixed_ref,
    cot_ref,
    w_ref,
    router_ref,
    own_ref,
    send1_ref,
    send2_ref,
    send3_ref,
    back_ref,
    probs_ref,
    grads_ref,
):
    width = mixed_ref.shape[1]
    piece = own_ref.shape[1]
    hidden_columns = w_ref.shape[1] // 3
    mixed = mixed_ref[...]
    cot = cot_ref[...]
    pre = dot_nn(mixed, w_ref[:, : 2 * hidden_columns])
    gate_pre, up_pre = pre[:, :hidden_columns], pre[:, hidden_columns:]
    act, slope = silu_parts(gate_pre)
    hidden = (act * up_pre).astype(BF16)
    hidden_grad = dot_nn(cot, w_ref[:, 2 * hidden_columns :])
    pair = jnp.concatenate([hidden_grad * up_pre * slope, hidden_grad * act], axis=1).astype(BF16)
    grads_ref[:, : 2 * hidden_columns] = dot_tn(mixed, pair).astype(BF16)
    grads_ref[:, 2 * hidden_columns :] = dot_tn(cot, hidden).astype(BF16)
    back_ref[...] = dot_nt(pair, w_ref[:, : 2 * hidden_columns])
    logits = dot_nn(mixed, router_ref[...])
    lane = lax.broadcasted_iota(jnp.int32, logits.shape, 1)
    logits = jnp.where(lane >= ROPE, logits, -1e30)
    weight = jnp.exp(logits - jnp.max(logits, axis=-1, keepdims=True))
    probs_ref[...] = weight / jnp.sum(weight, axis=-1, keepdims=True)
    for step, out_ref in enumerate((own_ref, send1_ref, send2_ref, send3_ref)):
        place = block_at(me_ref[0], step, width // piece, piece)
        part = dot_nt(hidden, w_ref[place, 2 * hidden_columns :])
        out_ref[...] = part.astype(out_ref.dtype)


def expert_back_kernel(split, *refs):
    if split:
        me_ref, base_ref, x0_ref, x1_ref, x2_ref, x3_ref = refs[:6]
        refs = refs[6:]
    else:
        me_ref, base_ref, x_ref = refs[:3]
        refs = refs[3:]
    c0_ref, c1_ref, c2_ref, c3_ref, wg_ref, wu_ref, wd_ref, router_ref = refs[:8]
    refs = refs[8:]
    if split:
        back_ref, c_ref, hg_ref, gr_ref, ur_ref, x_ref, wide_ref, down_ref, tall_ref = refs
    else:
        back_ref, c_ref, hg_ref, gr_ref, ur_ref, wide_ref, down_ref, tall_ref = refs
    sources, capacity, width = c_ref.shape
    rows = sources * capacity
    piece = c0_ref.shape[-1]
    count = width // piece
    hidden_columns = wd_ref.shape[1]
    padded = down_ref.shape[1]
    me = me_ref[0]

    @pl.when(pl.program_id(0) == 0)
    def _():
        rest = jnp.zeros((padded - hidden_columns, width), BF16)
        gate_up = jnp.concatenate([wg_ref[0], rest, wu_ref[0], rest], axis=0)
        tall_ref[...] = gate_up
        wide_ref[...] = gate_up.T
        down_ref[...] = jnp.concatenate([wd_ref[0], rest], axis=0).T

    for step, p_ref in enumerate((c0_ref, c1_ref, c2_ref, c3_ref)):
        c_ref[:, :, block_at(me, step, count, piece)] = p_ref[:, 0]
    if split:
        for step, p_ref in enumerate((x0_ref, x1_ref, x2_ref, x3_ref)):
            x_ref[:, :, block_at(me, step, count, piece)] = p_ref[...]
    x = x_ref[...].reshape(rows, width)
    expert = base_ref[0] + (1 if split else 0) + ROPE
    logits = dot_nn(x, router_ref[...])
    lane = lax.broadcasted_iota(jnp.int32, logits.shape, 1)
    logits = jnp.where(lane >= ROPE, logits, -1e30)
    weight = jnp.exp(logits - jnp.max(logits, axis=-1, keepdims=True))
    gate = jnp.sum(jnp.where(lane == expert, weight, 0.0), axis=-1, keepdims=True) / jnp.sum(
        weight, axis=-1, keepdims=True
    )
    pre = dot_nn(x, wide_ref[...])
    gate_pre, up_pre = pre[:, :padded], pre[:, padded:]
    hidden_cot = dot_nn(c_ref[...].reshape(rows, width), down_ref[...])
    act, slope = silu_parts(gate_pre)
    hidden = (act * up_pre).astype(BF16).astype(F32)
    gate_grad = jnp.sum(hidden * hidden_cot, axis=-1, keepdims=True)
    hidden_grad = gate * hidden_cot
    gate_rows = (hidden_grad * up_pre * slope).astype(BF16)
    up_rows = (hidden_grad * act).astype(BF16)
    hg_ref[...] = (gate * hidden).astype(BF16)[:, :hidden_columns]
    gr_ref[...] = gate_rows[:, :hidden_columns]
    ur_ref[...] = up_rows[:, :hidden_columns]
    high = gate_grad.astype(BF16).astype(F32)
    low = gate_grad - high
    beside = jnp.where(lane == 0, high, 0.0) + jnp.where(lane == 1, low, 0.0)
    back = dot_nn(jnp.concatenate([gate_rows, up_rows], axis=1), tall_ref[...])
    back_ref[:, :, :width] = back.astype(BF16).reshape(sources, capacity, width)
    back_ref[:, :, width:] = beside.astype(BF16).reshape(sources, capacity, LANES)


def expert_back(split, me, base, xs, cs, wg, wu, wd, router, router_at, chunk):
    owners, local, capacity, piece = cs[0].shape
    hidden, width = wg.shape[1:]
    local_index = 1 if split else 0
    rows = owners * capacity
    padded = -(-hidden // LANES) * LANES
    scalar = pl.BlockSpec(memory_space=pltpu.SMEM)
    row_spec = pl.BlockSpec((chunk * capacity, hidden), lambda c: (c, 0))
    row_shape = jax.ShapeDtypeStruct((rows, hidden), BF16)
    wide_spec = pl.BlockSpec((chunk, capacity, width), lambda c: (c, 0, 0))
    wide_shape = jax.ShapeDtypeStruct((owners, capacity, width), BF16)
    narrow_spec = pl.BlockSpec((chunk, capacity, piece), lambda c: (c, 0, 0))
    own_spec = pl.BlockSpec((chunk, capacity, piece), lambda c: (c, 0, width // piece))
    cot_spec = pl.BlockSpec((chunk, 1, capacity, piece), lambda c: (c, local_index, 0, 0))
    weight_spec = pl.BlockSpec((1, hidden, width), lambda c: (local_index, 0, 0))
    in_specs = [scalar, scalar]
    in_specs += [own_spec] + [narrow_spec] * 3 if split else [wide_spec]
    in_specs += [cot_spec] * 4 + [weight_spec] * 3 + [pl.BlockSpec((width, LANES), lambda c: (0, router_at))]
    out_specs = [pl.BlockSpec((chunk, capacity, width + LANES), lambda c: (c, 0, 0)), wide_spec]
    out_shape = [jax.ShapeDtypeStruct((owners, capacity, width + LANES), BF16), wide_shape]
    last_spec, last_shape = ([wide_spec], [wide_shape]) if split else ([], [])
    return pl.pallas_call(
        functools.partial(expert_back_kernel, split),
        grid=(owners // chunk,),
        in_specs=in_specs,
        out_specs=out_specs + [row_spec] * 3 + last_spec,
        out_shape=out_shape + [row_shape] * 3 + last_shape,
        scratch_shapes=[
            pltpu.VMEM((width, 2 * padded), BF16),
            pltpu.VMEM((width, padded), BF16),
            pltpu.VMEM((2 * padded, width), BF16),
        ],
        compiler_params=pltpu.CompilerParams(vmem_limit_bytes=VMEM_BYTES),
        cost_estimate=pl.CostEstimate(
            flops=100 * rows * hidden * width, bytes_accessed=24 * 1024 * 1024, transcendentals=0
        ),
        name="expert_back",
    )(me, base, *xs, *cs, wg, wu, wd, router)


def expert_out_kernel(hg_ref, wd_ref, out_ref):
    pieces, sources, capacity, piece = out_ref.shape
    out = dot_nn(hg_ref[...], wd_ref[0]).astype(BF16)
    for index in range(pieces):
        out_ref[index] = out[:, index * piece : (index + 1) * piece].reshape(sources, capacity, piece)


def expert_out(expert, hg, wd, owners, pieces, chunk):
    rows, hidden = hg.shape
    width = wd.shape[2]
    capacity = rows // owners
    piece = width // pieces
    return pl.pallas_call(
        expert_out_kernel,
        grid=(owners // chunk,),
        in_specs=[
            pl.BlockSpec((chunk * capacity, hidden), lambda c: (c, 0)),
            pl.BlockSpec((1, hidden, width), lambda c: (expert, 0, 0)),
        ],
        out_specs=pl.BlockSpec((pieces, chunk, capacity, piece), lambda c: (0, c, 0, 0)),
        out_shape=jax.ShapeDtypeStruct((pieces, owners, capacity, piece), BF16),
        compiler_params=pltpu.CompilerParams(vmem_limit_bytes=VMEM_BYTES),
        cost_estimate=pl.CostEstimate(
            flops=rows * hidden * width // 5, bytes_accessed=6 * 1024 * 102, transcendentals=0
        ),
        name="expert_out",
    )(hg, wd)


def expert_grads_kernel(
    x0_ref, c0_ref, hg0_ref, gr0_ref, ur0_ref, x1_ref, c1_ref, hg1_ref, gr1_ref, ur1_ref, dg_ref, du_ref, dd_ref
):
    owners, capacity, piece = x0_ref.shape
    rows = owners * capacity

    def step(x_ref, c_ref, hg_ref, gr_ref, ur_ref):
        x = x_ref[...].reshape(rows, piece)
        dg_ref[0] = dot_tn(gr_ref[...], x)
        du_ref[0] = dot_tn(ur_ref[...], x)
        dd_ref[0] = dot_tn(hg_ref[...], c_ref[...].reshape(rows, piece))

    pl.when(pl.program_id(0) == 0)(lambda: step(x0_ref, c0_ref, hg0_ref, gr0_ref, ur0_ref))
    pl.when(pl.program_id(0) == 1)(lambda: step(x1_ref, c1_ref, hg1_ref, gr1_ref, ur1_ref))


def expert_grads(first, second, pieces):
    owners, capacity, width = first[1].shape
    rows, hidden = first[2].shape
    piece = width // pieces
    row_spec = pl.BlockSpec((rows, hidden), lambda e, j: (0, 0))

    def specs(expert):
        stay = 0 if expert else pieces - 1
        wide = pl.BlockSpec(
            (owners, capacity, piece), lambda e, j: (0, 0, jnp.where(e == expert, j, stay))
        )
        return [wide, wide, row_spec, row_spec, row_spec]

    out_spec = pl.BlockSpec((1, hidden, piece), lambda e, j: (e, 0, j))
    out_shape = jax.ShapeDtypeStruct((2, hidden, width), F32)
    return pl.pallas_call(
        expert_grads_kernel,
        grid=(2, pieces),
        in_specs=specs(0) + specs(1),
        out_specs=[out_spec] * 3,
        out_shape=[out_shape] * 3,
        compiler_params=pltpu.CompilerParams(vmem_limit_bytes=VMEM_BYTES),
        cost_estimate=pl.CostEstimate(
            flops=rows * hidden * width, bytes_accessed=40 * 1024 * 102, transcendentals=0
        ),
        name="expert_grads",
    )(*first, *second)


def slot_probs(t_ref, b_ref, index, width):
    owners, capacity, _ = b_ref.shape
    rows = owners * capacity
    beside = b_ref[:, :, width:].reshape(rows, LANES).astype(F32)
    lane = lax.broadcasted_iota(jnp.int32, (rows, LANES), 1)
    expert = 2 * (lax.broadcasted_iota(jnp.int32, (rows, LANES), 0) // capacity) + index
    spread = jnp.where(lane == expert + ROPE, beside[:, 0:1], 0.0) + jnp.where(
        lane == expert, beside[:, 1:2], 0.0
    )
    return dot_nn(t_ref[...], spread.astype(BF16))


def combine_first_kernel(t_ref, b_ref, shared_ref, sum_ref, probs_ref):
    owners, capacity, _ = b_ref.shape
    width = shared_ref.shape[1]
    probs_ref[...] = slot_probs(t_ref, b_ref, 0, width)
    sum_ref[...] = shared_ref[...] + dot_nn(t_ref[...], b_ref[:, :, :width].reshape(owners * capacity, width))


def combine_kernel(
    me_ref, t_ref, b_ref, sum_ref, first_probs_ref, own_ref, probs_ref, send1_ref, send2_ref, send3_ref
):
    owners, capacity, _ = b_ref.shape
    rows = owners * capacity
    width = sum_ref.shape[1]
    piece = own_ref.shape[1]
    probs = first_probs_ref[...] + slot_probs(t_ref, b_ref, 1, width)
    probs = probs + pltpu.roll(probs, ROPE, 1)
    probs_ref[...] = probs
    high = probs.astype(BF16)
    low = (probs - high.astype(F32)).astype(BF16)
    short = lax.broadcasted_iota(jnp.int32, probs.shape, 1)
    message = jnp.where(short >= ROPE, high.astype(F32), low.astype(F32)).astype(BF16)
    for step, out_ref in enumerate((own_ref, send1_ref, send2_ref, send3_ref)):
        place = block_at(me_ref[0], step, width // piece, piece)
        part = sum_ref[:, place] + dot_nn(t_ref[...], b_ref[:, :, place].reshape(rows, piece))
        if step == 0:
            own_ref[...] = part
        else:
            out_ref[:, :piece] = part.astype(BF16)
            out_ref[:, piece:] = message


def attend_back_kernel(
    me_ref,
    core_ref,
    stream_ref,
    cot_ref,
    middle_ref,
    a0_ref,
    a1_ref,
    a2_ref,
    a3_ref,
    r1_ref,
    r2_ref,
    r3_ref,
    probs_own_ref,
    router_probs_ref,
    w_ref,
    router_ref,
    mixed_ref,
    normed_ref,
    query_ref,
    expanded_ref,
    key_ref,
    latent_ref,
    compressed_ref,
    probs_ref,
    attended_ref,
    gains_ref,
    latent_gain_ref,
    cos_ref,
    sin_ref,
    keep_ref,
    pass_ref,
    middle_grad_ref,
    own_ref,
    send1_ref,
    send2_ref,
    send3_ref,
    scr_ref,
    low_ref,
    wide_ref,
    sems,
):
    heads, tokens, _ = probs_ref.shape
    width = stream_ref.shape[1]
    piece = own_ref.shape[1]
    nope = heads * NOPE
    queries = nope + heads * ROPE
    edge = queries + LATENT + LANES
    outer = edge + heads * VDIM
    owners = 32
    shard = width // owners
    short = LATENT // owners
    count = width // piece
    me = me_ref[0]
    probs_grad = probs_own_ref[...]
    for r_ref in (r1_ref, r2_ref, r3_ref):
        other = r_ref[:, piece:].astype(F32)
        probs_grad = probs_grad + other + pltpu.roll(other, ROPE, 1)
    router_probs = router_probs_ref[...]
    logits_low = (
        router_probs * (probs_grad - jnp.sum(router_probs * probs_grad, axis=-1, keepdims=True))
    ).astype(BF16)
    router_back = dot_nt(logits_low, router_ref[...])
    for step, a_ref in enumerate((a0_ref, a1_ref, a2_ref, a3_ref)):
        wide_ref[:, block_at(me, step, count, piece)] = a_ref[...].astype(F32)
    mixed_grad = wide_ref[...] + router_back
    middle = middle_ref[...]
    norm_grad, second_gain_rows = rms_back(middle, inverse_rms(middle), gains_ref[1:2, :], mixed_grad)
    second_gain_grad = jnp.sum(second_gain_rows, axis=0, keepdims=True)
    middle_grad = cot_ref[...] + norm_grad
    middle_grad_ref[...] = middle_grad
    middle_low = middle_grad.astype(BF16)
    attended_grad = dot_nn(middle_low, w_ref[:, edge:outer]).astype(BF16)
    scale = (NOPE + ROPE) ** (-0.5)
    key_low = key_ref[...]
    key_odd = pltpu.roll(key_low.astype(F32), ROPE, 1).astype(BF16)
    latent = latent_ref[...]
    latent_part = jnp.zeros((tokens, LATENT), F32)
    key_even_grad = jnp.zeros((tokens, LANES), F32)
    key_odd_grad = jnp.zeros((tokens, LANES), F32)
    rope_grads = []
    grads4 = scr_ref.reshape(owners, shard, scr_ref.shape[1])
    for head in range(heads):
        pair = nope + head // 2 * LANES
        expanded = expanded_ref[:, head * 2 * NOPE : (head + 1) * 2 * NOPE]
        probs = probs_ref[head]
        head_grad = attended_grad[:, head * VDIM : (head + 1) * VDIM]
        value_grad = dot_tn(probs.astype(BF16), head_grad)
        probs_att = dot_nt(head_grad, expanded[:, NOPE:])
        scores = probs * (probs_att - jnp.sum(probs * probs_att, axis=-1, keepdims=True))
        raw_low = (scores * scale).astype(BF16)
        low_ref[:, head * NOPE : (head + 1) * NOPE] = dot_nn(raw_low, expanded[:, :NOPE]).astype(BF16)
        turn_grad = dot_nn(raw_low, key_odd if head % 2 else key_low)
        if head % 2:
            rope_grads[-1] = rope_grads[-1] + turn_grad
            key_odd_grad += dot_tn(raw_low, query_ref[:, pair : pair + LANES])
        else:
            rope_grads.append(turn_grad)
            key_even_grad += dot_tn(raw_low, query_ref[:, pair : pair + LANES])
        key_grad = dot_tn(raw_low, query_ref[:, head * NOPE : (head + 1) * NOPE])
        expanded_low = jnp.concatenate([key_grad, value_grad], axis=1).astype(BF16)
        up = w_ref[:, outer : outer + 2 * NOPE].reshape(owners, heads, short, 2 * NOPE)[:, head]
        up = up.reshape(LATENT, 2 * NOPE)
        latent_part += dot_nt(expanded_low, up)
        grads4[:, head * short : (head + 1) * short, outer : outer + 2 * NOPE] = (
            dot_tn(latent, expanded_low).astype(BF16).reshape(owners, short, 2 * NOPE)
        )
    rope_grad = jnp.concatenate(rope_grads, axis=1)
    low_ref[:, nope:queries] = rotated(rope_grad, cos_ref[...], -sin_ref[...]).astype(BF16)
    compressed = compressed_ref[...]
    latent_grad, latent_gain_rows = rms_back(
        compressed, inverse_rms(compressed), latent_gain_ref[2:3, :], latent_part
    )
    latent_gain_grad = jnp.sum(latent_gain_rows, axis=0, keepdims=True)
    low_ref[:, queries : queries + LATENT] = latent_grad.astype(BF16)
    lane = lax.broadcasted_iota(jnp.int32, (tokens, LANES), 1)
    key_grad = jnp.where(lane < ROPE, key_even_grad + pltpu.roll(key_odd_grad, ROPE, 1), 0.0)
    key_grad = rotated(key_grad, cos_ref[:, :LANES], -sin_ref[:, :LANES])
    low_ref[:, queries + LATENT : edge] = jnp.where(lane < ROPE, key_grad, 0.0).astype(BF16)
    low = low_ref[...]
    for step, out_ref in enumerate((own_ref, send1_ref, send2_ref, send3_ref)):
        place = block_at(me, step, count, piece)
        part = dot_nt(low, w_ref[place, :edge])
        wide_ref[:, place] = part
        out_ref[...] = part.astype(out_ref.dtype)
    stream = stream_ref[...].astype(F32)
    first_gain_grad = jnp.sum(wide_ref[...] * (stream * inverse_rms(stream)), axis=0, keepdims=True)
    late = dot_tn(normed_ref[...], low[:, queries:])
    sub = lax.broadcasted_iota(jnp.int32, (LANES, width), 0)
    gain_columns = (
        jnp.where(sub == ROPE, first_gain_grad, 0.0)
        + jnp.where(sub == ROPE + 1, second_gain_grad * (1.0 / count), 0.0)
    ).T
    key_columns = (late[:, LATENT:] + gain_columns).reshape(owners, shard, LANES)
    sub = lax.broadcasted_iota(jnp.int32, (LANES, LATENT), 0)
    latent_columns = jnp.where(sub == ROPE + 2, latent_gain_grad, 0.0).T.reshape(owners, short, LANES)
    grads4[:, :, queries : queries + LATENT] = (
        late[:, :LATENT].astype(BF16).reshape(owners, shard, LATENT)
    )
    grads4[:, :, queries + LATENT : edge] = key_columns.astype(BF16)
    grads4[:, :short, queries + LATENT : edge] = (key_columns[:, :short] + latent_columns).astype(BF16)
    scr_ref[:, edge:outer] = dot_tn(middle_low, attended_ref[...]).astype(BF16)
    scr_ref[:, :queries] = dot_tn(normed_ref[...], low[:, :queries]).astype(BF16)
    router_grad = dot_tn(mixed_ref[...], logits_low)
    scr_ref[:, outer + 2 * NOPE :] = router_grad[:, ROPE:].astype(BF16)
    halves = scr_ref.reshape(owners // 2, 2, shard, scr_ref.shape[1])
    core = core_ref[0]
    first = pltpu.make_async_copy(halves.at[:, 1 - core], pass_ref, sems.at[0])
    second = pltpu.make_async_copy(halves.at[:, core], keep_ref, sems.at[1])
    first.start()
    second.start()
    first.wait()
    second.wait()


def unpack_kernel(parts_ref, query_ref, late_ref, output_ref, up_ref, router_ref):
    heads = up_ref.shape[1] // (2 * NOPE)
    short = up_ref.shape[0]
    nope = heads * NOPE
    queries = nope + heads * ROPE
    edge = queries + LATENT + LANES
    outer = edge + heads * VDIM
    total = jnp.sum(parts_ref[...].astype(F32), axis=0)
    for head in range(heads):
        start = head * (NOPE + ROPE)
        query_ref[:, start : start + NOPE] = total[:, head * NOPE : (head + 1) * NOPE]
        query_ref[:, start + NOPE : start + NOPE + ROPE] = total[
            :, nope + head * ROPE : nope + (head + 1) * ROPE
        ]
        up_ref[:, head * 2 * NOPE : (head + 1) * 2 * NOPE] = total[
            head * short : (head + 1) * short, outer : outer + 2 * NOPE
        ]
    late_ref[...] = total[:, queries:edge]
    output_ref[...] = total[:, edge:outer]
    router_ref[...] = total[:, outer + 2 * NOPE :]


def late_kernel(own_ref, r1_ref, r2_ref, r3_ref, down_ref, gains_ref):
    total = own_ref[...] + r1_ref[...] + r2_ref[...] + r3_ref[...]
    down_ref[...] = total[:, : down_ref.shape[1]]
    columns = total[:, LATENT:]
    columns = jnp.concatenate([columns, jnp.zeros(columns.shape, F32)], axis=0)
    gains_ref[...] = columns.T[ROPE : ROPE + 8, :]


def stream_kernel(me_ref, middle_grad_ref, stream_ref, gains_ref, a0_ref, a1_ref, a2_ref, a3_ref, out_ref, wide_ref):
    piece = a0_ref.shape[1]
    count = stream_ref.shape[1] // piece
    for step, a_ref in enumerate((a0_ref, a1_ref, a2_ref, a3_ref)):
        wide_ref[:, block_at(me_ref[0], step, count, piece)] = a_ref[...].astype(F32)
    stream = stream_ref[...].astype(F32)
    norm_grad, _ = rms_back(stream, inverse_rms(stream), gains_ref[0:1, :], wide_ref[...])
    out_ref[...] = middle_grad_ref[...] + norm_grad


def routed_kernel(t0_ref, t1_ref, o_ref, own_ref, r1_ref, r2_ref, r3_ref, out_ref):
    owners, _, capacity, piece = o_ref.shape
    rows = owners * capacity
    total = own_ref[...]
    for r_ref in (r1_ref, r2_ref, r3_ref):
        total = total + r_ref[...].astype(F32)
    for index, t_ref in ((0, t0_ref), (1, t1_ref)):
        total = total + dot_nn(t_ref[...], o_ref[:, index].reshape(rows, piece))
    out_ref[...] = total.astype(BF16)


def result_kernel(me_ref, middle_ref, a0_ref, a1_ref, a2_ref, a3_ref, out_ref):
    piece = a0_ref.shape[1]
    count = middle_ref.shape[1] // piece
    for step, a_ref in enumerate((a0_ref, a1_ref, a2_ref, a3_ref)):
        place = block_at(me_ref[0], step, count, piece)
        out_ref[:, place] = middle_ref[:, place] + a_ref[...].astype(F32)


def shift(array, step):
    size = lax.axis_size("tensor")
    return lax.ppermute(array, "tensor", [(i, (i + step) % size) for i in range(size)])


def send_blocks(sends):
    return [shift(array, step + 1) for step, array in enumerate(sends)]


def share_small(low):
    size = lax.axis_size("tensor")
    return [low] + [shift(low, size - step) for step in range(1, size)]


def ring_first(rows):
    return shift(rows, 1), shift(rows, lax.axis_size("tensor") - 1)


def ring_second(rows, before, after):
    half = rows.shape[0] // 2
    across = [shift(before[:half], 1), shift(after[half:], lax.axis_size("tensor") - 1)]
    return [rows, after, jnp.concatenate(across, axis=0), before]


def after(array, *others):
    return lax.optimization_barrier((array, *others))[0]


def exchange(rows):
    shape = rows.shape
    return lax.all_to_all(
        rows.reshape(shape[0], -1, shape[-1]), "expert", split_axis=0, concat_axis=0, tiled=True
    ).reshape(shape)


def per_device(
    stream,
    segment_ids,
    expert_ids,
    first_gain,
    query_proj,
    latent_down,
    latent_gain,
    latent_up,
    output_proj,
    second_gain,
    router_proj,
    shared_gate,
    shared_up,
    shared_down,
    expert_gate,
    expert_up,
    expert_down,
    cotangent,
):
    tokens, width = stream.shape
    owners = lax.axis_size("expert")
    tensors = lax.axis_size("tensor")
    shard = query_proj.shape[0]
    heads = query_proj.shape[1] // (NOPE + ROPE)
    short = latent_up.shape[0]
    experts = router_proj.shape[1]
    hidden_columns = shared_gate.shape[1]
    local, _, expert_hidden = expert_gate.shape
    capacity = tokens * TOPK * 4 // (3 * experts)
    rows = owners * capacity
    piece = width // tensors
    nope = heads * NOPE
    queries = nope + heads * ROPE
    edge = queries + LATENT + LANES
    outer = edge + heads * VDIM
    me = lax.axis_index("tensor").astype(jnp.int32).reshape(1)
    base = (lax.axis_index("expert") * local).astype(jnp.int32).reshape(1)
    core = lax.rem(lax.axis_index("expert"), 2).astype(jnp.int32).reshape(1)
    smem = {0: pltpu.SMEM}

    gains = jnp.concatenate(
        [
            first_gain[:, None],
            second_gain[:, None],
            jnp.pad(latent_gain, (0, shard - short))[:, None],
            jnp.zeros((shard, ROPE - 3), BF16),
        ],
        axis=1,
    )
    by_head = query_proj.reshape(shard, heads, NOPE + ROPE)
    pack_one = jnp.concatenate(
        [
            by_head[:, :, :NOPE].reshape(shard, nope),
            by_head[:, :, NOPE:].reshape(shard, heads * ROPE),
            latent_down,
            router_proj,
            output_proj.T,
            latent_up.reshape(short, heads, 2 * NOPE).transpose(1, 0, 2).reshape(shard, 2 * NOPE),
            gains,
        ],
        axis=1,
    )
    pack_two = jnp.concatenate([shared_gate, shared_up, shared_down.T], axis=1)
    one = lax.all_gather(pack_one, "expert", axis=0, tiled=True)

    position = jnp.arange(tokens).astype(F32)
    exponent = jnp.arange(ROPE // 2).astype(F32) * (2.0 / ROPE)
    angles = position[:, None] * jnp.exp(-math.log(ROTARY_BASE) * exponent)[None, :]
    cosine = jnp.tile(jnp.cos(angles), (1, 2 * heads))
    sine = jnp.sin(angles)
    sine = jnp.tile(jnp.concatenate([-sine, sine], axis=1), (1, heads))

    t0, t1, cot_low, cot_out = run(
        routing_kernel,
        [
            ((tokens, rows), BF16),
            ((tokens, rows), BF16),
            ((tokens, width), BF16),
            ((owners, local, capacity, piece), BF16),
        ],
        [me, expert_ids.T, cotangent],
        2 * local * tokens * rows * (piece + experts),
        places=smem,
        name="routing",
    )

    (
        own,
        send1,
        send2,
        send3,
        normed,
        query,
        expanded,
        key,
        latent,
        compressed,
        probs,
        attended,
        gain_rows,
        latent_gain_rows,
    ) = run(
        attend_kernel,
        [
            ((tokens, piece), F32),
            ((tokens, piece), BF16),
            ((tokens, piece), BF16),
            ((tokens, piece), BF16),
            ((tokens, width), BF16),
            ((tokens, queries), BF16),
            ((tokens, heads * 2 * NOPE), BF16),
            ((tokens, LANES), BF16),
            ((tokens, LATENT), BF16),
            ((tokens, LATENT), F32),
            ((heads, tokens, tokens), F32),
            ((tokens, heads * VDIM), BF16),
            ((8, width), F32),
            ((8, LATENT), F32),
        ],
        [me, stream, one, segment_ids, segment_ids.T, cosine, sine],
        2 * tokens * width * outer,
        places=smem,
        name="attend",
    )
    cot_own = exchange(after(cot_out, own))
    got = send_blocks([send1, send2, send3])
    attention = (own + got[0].astype(F32) + got[1].astype(F32) + got[2].astype(F32)).astype(BF16)
    middle, mixed, x_out = run(
        dispatch_kernel,
        [
            ((tokens, width), F32),
            ((tokens, width), BF16),
            ((owners, capacity, width + piece), BF16),
        ],
        [me, stream, *share_small(attention), gain_rows, t0, t1],
        2 * tokens * rows * (width + piece),
        places=smem,
        name="dispatch",
    )
    cot_before, cot_after = ring_first(after(cot_own, mixed))
    x_in = exchange(after(x_out, cot_own))
    cots = ring_second(cot_own, cot_before, cot_after)
    x1s = x_in[:, :, width:]
    x1_before, x1_after = ring_first(x1s)
    x1s = [x_in] + ring_second(x1s, x1_before, x1_after)[1:]
    gate_t = expert_gate.transpose(0, 2, 1)
    up_t = expert_up.transpose(0, 2, 1)
    chunk = owners // 2
    back0, c0, hg0, gr0, ur0 = expert_back(
        False, me, base, [x_in], cots, gate_t, up_t, expert_down, one, edge // LANES - 1, chunk // 2
    )
    out0 = expert_out(0, hg0, expert_down, owners, tensors, chunk)
    two = lax.all_gather(after(pack_two, out0, x1_before, x1_after), "expert", axis=0, tiled=True)
    back0 = exchange(back0)
    back1, c1, hg1, gr1, ur1, x1 = expert_back(
        True, me, after(base, hg0), x1s, cots, gate_t, up_t, expert_down, one, edge // LANES - 1, chunk // 2
    )
    back1 = exchange(after(back1, back0))
    router_block = one[:, queries + LATENT : edge]
    (
        shared_own,
        shared1,
        shared2,
        shared3,
        shared_back,
        router_probs,
        shared_grads,
    ) = run(
        shared_kernel,
        [
            ((tokens, piece), F32),
            ((tokens, piece), BF16),
            ((tokens, piece), BF16),
            ((tokens, piece), BF16),
            ((tokens, width), F32),
            ((tokens, LANES), F32),
            ((width, 3 * hidden_columns), BF16),
        ],
        [after(me, hg1), mixed, cot_low, two, router_block],
        18 * tokens * width * hidden_columns,
        places=smem,
        name="shared",
    )

    gr0 = after(gr0, back0)
    gate_grad, up_grad, down_grad = expert_grads(
        (x_in, c0, hg0, gr0, ur0), (x1, c1, hg1, gr1, ur1), tensors
    )
    out1 = expert_out(1, after(hg1, out0), expert_down, owners, tensors, chunk)
    out_rows = [
        lax.psum_scatter(out, "tensor", scatter_dimension=0, tiled=True).reshape(owners, 1, capacity, piece)
        for out in (out0, out1)
    ]

    first_sum, first_probs = run(
        combine_first_kernel,
        [((tokens, width), F32), ((tokens, LANES), F32)],
        [t0, back0, shared_back],
        2 * tokens * rows * width,
        name="combine_first",
    )
    own, probs_own, send1, send2, send3 = run(
        combine_kernel,
        [
            ((tokens, piece), F32),
            ((tokens, LANES), F32),
            ((tokens, piece + LANES), BF16),
            ((tokens, piece + LANES), BF16),
            ((tokens, piece + LANES), BF16),
        ],
        [after(me, out1, gate_grad), t1, back1, first_sum, first_probs],
        2 * tokens * rows * width,
        places=smem,
        name="combine",
    )
    got = send_blocks([send1, send2, send3])
    shared_sum = lax.psum_scatter(
        after(shared_grads, own), "expert", scatter_dimension=0, tiled=True
    )
    mixed_sum = (
        own
        + got[0][:, :piece].astype(F32)
        + got[1][:, :piece].astype(F32)
        + got[2][:, :piece].astype(F32)
    ).astype(BF16)
    mixed_sums = share_small(mixed_sum)
    out_rows = exchange(after(jnp.concatenate(out_rows, axis=1), *mixed_sums[1:]))
    keep, passed, middle_grad, own, send1, send2, send3 = run(
        attend_back_kernel,
        [
            ((owners // 2, shard, outer + 2 * NOPE + experts), BF16),
            ((owners // 2, shard, outer + 2 * NOPE + experts), BF16),
            ((tokens, width), F32),
            ((tokens, piece), F32),
            ((tokens, piece), BF16),
            ((tokens, piece), BF16),
            ((tokens, piece), BF16),
        ],
        [
            me,
            core,
            stream,
            cotangent,
            middle,
            *mixed_sums,
            *got,
            probs_own,
            router_probs,
            one,
            router_block,
            mixed,
            normed,
            query,
            expanded,
            key,
            latent,
            compressed,
            probs,
            attended,
            gain_rows,
            latent_gain_rows,
            cosine,
            sine,
        ],
        2 * tokens * width * (3 * edge + 2 * outer),
        scratch=[
            pltpu.VMEM((width, outer + 2 * NOPE + experts), BF16),
            pltpu.VMEM((tokens, edge), BF16),
            pltpu.VMEM((tokens, width), F32),
            pltpu.SemaphoreType.DMA((2,)),
        ],
        places={0: pltpu.SMEM, 1: pltpu.SMEM},
        out_places={0: pl.ANY, 1: pl.ANY},
        name="attend_back",
    )
    paired = lax.ppermute(after(passed, out_rows), "expert", [(i, i ^ 1) for i in range(owners)])
    paired = (keep.astype(F32) + paired.astype(F32)).astype(BF16)
    parts = lax.all_to_all(
        paired,
        "expert",
        split_axis=0,
        concat_axis=0,
        tiled=True,
        axis_index_groups=[[2 * i + c for i in range(owners // 2)] for c in range(2)],
    )
    got = send_blocks([send1, send2, send3])
    first_sum = (own + got[0].astype(F32) + got[1].astype(F32) + got[2].astype(F32)).astype(BF16)
    (stream_grad,) = run(
        stream_kernel,
        [((tokens, width), F32)],
        [me, middle_grad, stream, gain_rows, *share_small(first_sum)],
        0,
        scratch=[pltpu.VMEM((tokens, width), F32)],
        places=smem,
        name="stream",
    )

    got = send_blocks([shared1, shared2, shared3])
    (branch,) = run(
        routed_kernel,
        [((tokens, piece), BF16)],
        [t0, t1, out_rows, shared_own, *got],
        4 * tokens * rows * piece,
        name="routed",
    )
    (result,) = run(
        result_kernel,
        [((tokens, width), F32)],
        [me, middle, *share_small(branch)],
        0,
        places=smem,
        name="result",
    )

    shared_sum = shared_sum.astype(F32)
    gate_sum = shared_sum[:, :hidden_columns]
    up_sum = shared_sum[:, hidden_columns : 2 * hidden_columns]
    down_sum = shared_sum[:, 2 * hidden_columns :]
    parts = after(parts, stream_grad, result, gate_sum, up_sum, down_sum)
    query_grad, late, output_grad, latent_up_grad, router_grad = run(
        unpack_kernel,
        [
            (query_proj.shape, F32),
            ((shard, edge - queries), F32),
            ((shard, heads * VDIM), F32),
            (latent_up.shape, F32),
            (router_proj.shape, F32),
        ],
        [parts],
        0,
        name="unpack",
    )
    latent_down_grad, gain_grads = run(
        late_kernel,
        [(latent_down.shape, F32), ((8, LANES), F32)],
        [late, *(shift(late, step) for step in range(1, tensors))],
        0,
        name="late",
    )
    return (
        result,
        stream_grad,
        gain_grads[0, :shard],
        query_grad,
        latent_down_grad,
        gain_grads[2, :short],
        latent_up_grad,
        output_grad.T,
        gain_grads[1, :shard],
        router_grad,
        gate_sum,
        up_sum,
        down_sum.T,
        gate_grad.transpose(0, 2, 1),
        up_grad.transpose(0, 2, 1),
        down_grad,
    )


def solution(mesh):
    placed = (
        P("expert", None),
        P("expert", None),
        P("expert", None),
        P("expert"),
        P("expert", "tensor"),
        P("expert", None),
        P("expert"),
        P("expert", "tensor"),
        P("tensor", "expert"),
        P("expert"),
        P("expert", None),
        P("expert", "tensor"),
        P("expert", "tensor"),
        P("tensor", "expert"),
        P("expert", None, "tensor"),
        P("expert", None, "tensor"),
        P("expert", "tensor", None),
        P("expert", None),
    )
    return jax.shard_map(
        per_device,
        mesh=mesh,
        in_specs=placed,
        out_specs=(
            P("expert", None),
            P("expert", None),
            P("expert"),
            P("expert", "tensor"),
            P("expert", None),
            P("expert"),
            P("expert", "tensor"),
            P("tensor", "expert"),
            P("expert"),
            P("expert", None),
            P("expert", "tensor"),
            P("expert", "tensor"),
            P("tensor", "expert"),
            P("expert", None, "tensor"),
            P("expert", None, "tensor"),
            P("expert", "tensor", None),
        ),
        check_vma=False,
    )
```

```python
import functools
import math

import jax
import jax.numpy as jnp
from jax import lax
from jax.experimental import pallas as pl
from jax.experimental.pallas import tpu as pltpu
from jax.sharding import PartitionSpec as P

NOPE = 128
ROPE = 64
VDIM = 128
LATENT = 512
TOPK = 6
EPSILON = 1e-06
ROTARY_BASE = 10000.0

BF16 = jnp.bfloat16
F32 = jnp.float32
VMEM_BYTES = 60 * 1024 * 1024
LANES = 128
COST_SCALE = 10


def dot_nn(left, right):
    return lax.dot_general(left, right, (((1,), (0,)), ((), ())), preferred_element_type=F32)


def dot_nt(left, right):
    return lax.dot_general(left, right, (((1,), (1,)), ((), ())), preferred_element_type=F32)


def dot_tn(left, right):
    return lax.dot_general(left, right, (((0,), (0,)), ((), ())), preferred_element_type=F32)


def silu_parts(pre_values):
    sigmoid_value = 1.0 / (1.0 + jnp.exp(-pre_values))
    return (pre_values * sigmoid_value, sigmoid_value * (1.0 + pre_values * (1.0 - sigmoid_value)))


def inverse_rms(values):
    return lax.rsqrt(jnp.mean(values * values, axis=-1, keepdims=True) + EPSILON)


def rms_back(values, scale, gain, grad):
    normed = values * scale
    weighted = grad * gain
    return (
        scale * (weighted - normed * jnp.mean(weighted * normed, axis=-1, keepdims=True)),
        grad * normed,
    )


def turned(values):
    width = values.shape[1]
    lane = lax.broadcasted_iota(jnp.int32, values.shape, 1) % ROPE
    half = ROPE // 2
    return jnp.where(
        lane < half, pltpu.roll(values, width - half, 1), pltpu.roll(values, half, 1)
    )


def rotated(values, cosine, sine):
    return values * cosine + turned(values) * sine


def block_at(me, step, count, width):
    return pl.ds(pl.multiple_of(lax.rem(me + step, count) * width, width), width)


def run(kernel, outs, args, flops, scratch=(), name=None, places=None, aliases=None, out_places=None):
    places = places or {}
    out_places = out_places or {}
    in_specs = [pl.BlockSpec(memory_space=places.get(i, pltpu.VMEM)) for i in range(len(args))]
    out_specs = [pl.BlockSpec(memory_space=out_places.get(i, pltpu.VMEM)) for i in range(len(outs))]
    moved = sum(a.size * a.dtype.itemsize for a in args) + sum(
        math.prod(shape) * jnp.dtype(dtype).itemsize for shape, dtype in outs
    )
    return pl.pallas_call(
        kernel,
        in_specs=in_specs,
        out_specs=out_specs,
        out_shape=[jax.ShapeDtypeStruct(shape, dtype) for shape, dtype in outs],
        scratch_shapes=list(scratch),
        input_output_aliases=aliases or {},
        compiler_params=pltpu.CompilerParams(vmem_limit_bytes=VMEM_BYTES),
        cost_estimate=pl.CostEstimate(
            flops=flops // COST_SCALE, bytes_accessed=moved // COST_SCALE, transcendentals=0
        ),
        name=name,
    )(*args)


def routing_kernel(me_ref, ids_ref, cot_ref, t0_ref, t1_ref, low_ref, out_ref):
    choices, tokens = ids_ref.shape
    owners, local, capacity, piece = out_ref.shape
    experts = owners * local
    rows = owners * capacity
    expert = lax.broadcasted_iota(jnp.int32, (experts, tokens), 0)
    chosen = jnp.zeros((experts, tokens), F32)
    for choice in range(choices):
        chosen += jnp.where(ids_ref[choice : choice + 1, :] == expert, 1.0, 0.0)
    before = jnp.where(
        lax.broadcasted_iota(jnp.int32, (tokens, tokens), 0)
        < lax.broadcasted_iota(jnp.int32, (tokens, tokens), 1),
        1.0,
        0.0,
    ).astype(BF16)
    place = dot_nn(chosen.astype(BF16), before)
    place = jnp.where(chosen > 0.5, place, -1.0).astype(BF16)
    low = cot_ref[...].astype(BF16)
    low_ref[...] = low
    mine = cot_ref[:, block_at(me_ref[0], 0, cot_ref.shape[1] // piece, piece)].astype(BF16)
    slot = (lax.broadcasted_iota(jnp.int32, (tokens, rows), 1) % capacity).astype(F32)
    for index, t_ref in ((0, t0_ref), (1, t1_ref)):
        spread = jnp.where(
            lax.broadcasted_iota(jnp.int32, (experts, rows), 0)
            == lax.broadcasted_iota(jnp.int32, (experts, rows), 1) // capacity * local + index,
            1.0,
            0.0,
        ).astype(BF16)
        wanted = dot_tn(place, spread)
        matrix = jnp.where(wanted == slot, 1.0, 0.0).astype(BF16)
        t_ref[...] = matrix
        out_ref[:, index] = dot_tn(matrix, mine).astype(BF16).reshape(owners, capacity, piece)


def attend_kernel(
    me_ref,
    stream_ref,
    w_ref,
    seg_row_ref,
    seg_col_ref,
    cos_ref,
    sin_ref,
    own_ref,
    send1_ref,
    send2_ref,
    send3_ref,
    normed_ref,
    query_ref,
    expanded_ref,
    key_ref,
    latent_ref,
    compressed_ref,
    probs_ref,
    attended_ref,
    gains_ref,
    latent_gain_ref,
):
    heads, tokens, _ = probs_ref.shape
    width = stream_ref.shape[1]
    piece = own_ref.shape[1]
    nope = heads * NOPE
    queries = nope + heads * ROPE
    edge = queries + LATENT + LANES
    outer = edge + heads * VDIM
    owners = 32
    columns = jnp.concatenate(
        [w_ref[:, outer + 2 * NOPE :].astype(F32), jnp.zeros((width, ROPE), F32)], axis=1
    )
    gains = columns.T[:8, :]
    gains_ref[...] = gains
    shard = width // owners
    short = LATENT // owners
    latent_gain = (
        columns.reshape(owners, shard, LANES)[:, :short, :].reshape(LATENT, LANES).T[:8, :]
    )
    latent_gain_ref[...] = latent_gain
    stream = stream_ref[...].astype(F32)
    normed = (stream * inverse_rms(stream) * gains[0:1, :]).astype(BF16)
    normed_ref[...] = normed
    projected = dot_nn(normed, w_ref[:, :edge])
    query_ref[:, :nope] = projected[:, :nope].astype(BF16)
    query_ref[:, nope:] = rotated(projected[:, nope:queries], cos_ref[...], sin_ref[...]).astype(BF16)
    compressed = projected[:, queries : queries + LATENT]
    compressed_ref[...] = compressed
    latent = (compressed * inverse_rms(compressed) * latent_gain[2:3, :]).astype(BF16)
    latent_ref[...] = latent
    raw_key = projected[:, queries + LATENT : edge]
    key = rotated(raw_key, cos_ref[:, :LANES], sin_ref[:, :LANES])
    lane = lax.broadcasted_iota(jnp.int32, key.shape, 1)
    key = jnp.where(lane < ROPE, key, 0.0)
    key_low = key.astype(BF16)
    key_odd = pltpu.roll(key, ROPE, 1).astype(BF16)
    key_ref[...] = key_low
    row = lax.broadcasted_iota(jnp.int32, (tokens, tokens), 0)
    column = lax.broadcasted_iota(jnp.int32, (tokens, tokens), 1)
    allowed = (seg_col_ref[...] == seg_row_ref[...]) & (column <= row)
    scale = (NOPE + ROPE) ** (-0.5)
    for head in range(heads):
        block = slice(head * 2 * NOPE, (head + 1) * 2 * NOPE)
        up = w_ref[:, outer : outer + 2 * NOPE].reshape(owners, heads, short, 2 * NOPE)[:, head]
        up = up.reshape(LATENT, 2 * NOPE)
        expanded = dot_nn(latent, up).astype(BF16)
        expanded_ref[:, block] = expanded
        pair = nope + head // 2 * LANES
        raw = dot_nt(query_ref[:, head * NOPE : (head + 1) * NOPE], expanded[:, :NOPE]) + dot_nt(
            query_ref[:, pair : pair + LANES], key_odd if head % 2 else key_low
        )
        scores = jnp.where(allowed, raw * scale, -1e30)
        weight = jnp.exp(scores - jnp.max(scores, axis=-1, keepdims=True))
        probs = weight / jnp.sum(weight, axis=-1, keepdims=True)
        probs_ref[head] = probs
        attended_ref[:, head * VDIM : (head + 1) * VDIM] = dot_nn(
            probs.astype(BF16), expanded[:, NOPE:]
        ).astype(BF16)
    attended = attended_ref[...]
    for step, out_ref in enumerate((own_ref, send1_ref, send2_ref, send3_ref)):
        part = dot_nt(attended, w_ref[block_at(me_ref[0], step, width // piece, piece), edge:outer])
        out_ref[...] = part.astype(out_ref.dtype)


def dispatch_kernel(
    me_ref, stream_ref, a0_ref, a1_ref, a2_ref, a3_ref, gains_ref, t0_ref, t1_ref, middle_ref, mixed_ref, out_ref
):
    piece = a0_ref.shape[1]
    width = stream_ref.shape[1]
    count = width // piece
    owners, capacity, _ = out_ref.shape
    for step, a_ref in enumerate((a0_ref, a1_ref, a2_ref, a3_ref)):
        place = block_at(me_ref[0], step, count, piece)
        middle_ref[:, place] = stream_ref[:, place].astype(F32) + a_ref[...].astype(F32)
    middle = middle_ref[...]
    mixed = (middle * inverse_rms(middle) * gains_ref[1:2, :]).astype(BF16)
    mixed_ref[...] = mixed
    mine = mixed_ref[:, block_at(me_ref[0], 0, count, piece)]
    out_ref[:, :, width:] = dot_tn(t1_ref[...], mine).astype(BF16).reshape(owners, capacity, piece)
    out_ref[:, :, :width] = dot_tn(t0_ref[...], mixed).astype(BF16).reshape(owners, capacity, width)


def shared_kernel(
    me_ref,
    mixed_ref,
    cot_ref,
    w_ref,
    router_ref,
    own_ref,
    send1_ref,
    send2_ref,
    send3_ref,
    back_ref,
    probs_ref,
    grads_ref,
):
    width = mixed_ref.shape[1]
    piece = own_ref.shape[1]
    hidden_columns = w_ref.shape[1] // 3
    mixed = mixed_ref[...]
    cot = cot_ref[...]
    pre = dot_nn(mixed, w_ref[:, : 2 * hidden_columns])
    gate_pre, up_pre = pre[:, :hidden_columns], pre[:, hidden_columns:]
    act, slope = silu_parts(gate_pre)
    hidden = (act * up_pre).astype(BF16)
    hidden_grad = dot_nn(cot, w_ref[:, 2 * hidden_columns :])
    pair = jnp.concatenate([hidden_grad * up_pre * slope, hidden_grad * act], axis=1).astype(BF16)
    grads_ref[:, : 2 * hidden_columns] = dot_tn(mixed, pair).astype(BF16)
    grads_ref[:, 2 * hidden_columns :] = dot_tn(cot, hidden).astype(BF16)
    back_ref[...] = dot_nt(pair, w_ref[:, : 2 * hidden_columns])
    logits = dot_nn(mixed, router_ref[...])
    lane = lax.broadcasted_iota(jnp.int32, logits.shape, 1)
    logits = jnp.where(lane >= ROPE, logits, -1e30)
    weight = jnp.exp(logits - jnp.max(logits, axis=-1, keepdims=True))
    probs_ref[...] = weight / jnp.sum(weight, axis=-1, keepdims=True)
    for step, out_ref in enumerate((own_ref, send1_ref, send2_ref, send3_ref)):
        place = block_at(me_ref[0], step, width // piece, piece)
        part = dot_nt(hidden, w_ref[place, 2 * hidden_columns :])
        out_ref[...] = part.astype(out_ref.dtype)


def expert_back_kernel(split, *refs):
    if split:
        me_ref, base_ref, x0_ref, x1_ref, x2_ref, x3_ref = refs[:6]
        refs = refs[6:]
    else:
        me_ref, base_ref, x_ref = refs[:3]
        refs = refs[3:]
    c0_ref, c1_ref, c2_ref, c3_ref, wg_ref, wu_ref, wd_ref, router_ref = refs[:8]
    refs = refs[8:]
    if split:
        back_ref, c_ref, hg_ref, gr_ref, ur_ref, x_ref, wide_ref, down_ref, tall_ref = refs
    else:
        back_ref, c_ref, hg_ref, gr_ref, ur_ref, wide_ref, down_ref, tall_ref = refs
    sources, capacity, width = c_ref.shape
    rows = sources * capacity
    piece = c0_ref.shape[-1]
    count = width // piece
    hidden_columns = wd_ref.shape[1]
    padded = down_ref.shape[1]
    me = me_ref[0]

    @pl.when(pl.program_id(0) == 0)
    def _():
        rest = jnp.zeros((padded - hidden_columns, width), BF16)
        gate_up = jnp.concatenate([wg_ref[0], rest, wu_ref[0], rest], axis=0)
        tall_ref[...] = gate_up
        wide_ref[...] = gate_up.T
        down_ref[...] = jnp.concatenate([wd_ref[0], rest], axis=0).T

    for step, p_ref in enumerate((c0_ref, c1_ref, c2_ref, c3_ref)):
        c_ref[:, :, block_at(me, step, count, piece)] = p_ref[:, 0]
    if split:
        for step, p_ref in enumerate((x0_ref, x1_ref, x2_ref, x3_ref)):
            x_ref[:, :, block_at(me, step, count, piece)] = p_ref[...]
    x = x_ref[...].reshape(rows, width)
    expert = base_ref[0] + (1 if split else 0) + ROPE
    logits = dot_nn(x, router_ref[...])
    lane = lax.broadcasted_iota(jnp.int32, logits.shape, 1)
    logits = jnp.where(lane >= ROPE, logits, -1e30)
    weight = jnp.exp(logits - jnp.max(logits, axis=-1, keepdims=True))
    gate = jnp.sum(jnp.where(lane == expert, weight, 0.0), axis=-1, keepdims=True) / jnp.sum(
        weight, axis=-1, keepdims=True
    )
    pre = dot_nn(x, wide_ref[...])
    gate_pre, up_pre = pre[:, :padded], pre[:, padded:]
    hidden_cot = dot_nn(c_ref[...].reshape(rows, width), down_ref[...])
    act, slope = silu_parts(gate_pre)
    hidden = (act * up_pre).astype(BF16).astype(F32)
    gate_grad = jnp.sum(hidden * hidden_cot, axis=-1, keepdims=True)
    hidden_grad = gate * hidden_cot
    gate_rows = (hidden_grad * up_pre * slope).astype(BF16)
    up_rows = (hidden_grad * act).astype(BF16)
    hg_ref[...] = (gate * hidden).astype(BF16)[:, :hidden_columns]
    gr_ref[...] = gate_rows[:, :hidden_columns]
    ur_ref[...] = up_rows[:, :hidden_columns]
    high = gate_grad.astype(BF16).astype(F32)
    low = gate_grad - high
    beside = jnp.where(lane == 0, high, 0.0) + jnp.where(lane == 1, low, 0.0)
    back = dot_nn(jnp.concatenate([gate_rows, up_rows], axis=1), tall_ref[...])
    back_ref[:, :, :width] = back.astype(BF16).reshape(sources, capacity, width)
    back_ref[:, :, width:] = beside.astype(BF16).reshape(sources, capacity, LANES)


def expert_back(split, me, base, xs, cs, wg, wu, wd, router, router_at, chunk):
    owners, local, capacity, piece = cs[0].shape
    hidden, width = wg.shape[1:]
    local_index = 1 if split else 0
    rows = owners * capacity
    padded = -(-hidden // LANES) * LANES
    scalar = pl.BlockSpec(memory_space=pltpu.SMEM)
    row_spec = pl.BlockSpec((chunk * capacity, hidden), lambda c: (c, 0))
    row_shape = jax.ShapeDtypeStruct((rows, hidden), BF16)
    wide_spec = pl.BlockSpec((chunk, capacity, width), lambda c: (c, 0, 0))
    wide_shape = jax.ShapeDtypeStruct((owners, capacity, width), BF16)
    narrow_spec = pl.BlockSpec((chunk, capacity, piece), lambda c: (c, 0, 0))
    own_spec = pl.BlockSpec((chunk, capacity, piece), lambda c: (c, 0, width // piece))
    cot_spec = pl.BlockSpec((chunk, 1, capacity, piece), lambda c: (c, local_index, 0, 0))
    weight_spec = pl.BlockSpec((1, hidden, width), lambda c: (local_index, 0, 0))
    in_specs = [scalar, scalar]
    in_specs += [own_spec] + [narrow_spec] * 3 if split else [wide_spec]
    in_specs += [cot_spec] * 4 + [weight_spec] * 3 + [pl.BlockSpec((width, LANES), lambda c: (0, router_at))]
    out_specs = [pl.BlockSpec((chunk, capacity, width + LANES), lambda c: (c, 0, 0)), wide_spec]
    out_shape = [jax.ShapeDtypeStruct((owners, capacity, width + LANES), BF16), wide_shape]
    last_spec, last_shape = ([wide_spec], [wide_shape]) if split else ([], [])
    return pl.pallas_call(
        functools.partial(expert_back_kernel, split),
        grid=(owners // chunk,),
        in_specs=in_specs,
        out_specs=out_specs + [row_spec] * 3 + last_spec,
        out_shape=out_shape + [row_shape] * 3 + last_shape,
        scratch_shapes=[
            pltpu.VMEM((width, 2 * padded), BF16),
            pltpu.VMEM((width, padded), BF16),
            pltpu.VMEM((2 * padded, width), BF16),
        ],
        compiler_params=pltpu.CompilerParams(vmem_limit_bytes=VMEM_BYTES),
        cost_estimate=pl.CostEstimate(
            flops=100 * rows * hidden * width, bytes_accessed=24 * 1024 * 1024, transcendentals=0
        ),
        name="expert_back",
    )(me, base, *xs, *cs, wg, wu, wd, router)


def expert_out_kernel(hg_ref, wd_ref, out_ref):
    pieces, sources, capacity, piece = out_ref.shape
    out = dot_nn(hg_ref[...], wd_ref[0]).astype(BF16)
    for index in range(pieces):
        out_ref[index] = out[:, index * piece : (index + 1) * piece].reshape(sources, capacity, piece)


def expert_out(expert, hg, wd, owners, pieces, chunk):
    rows, hidden = hg.shape
    width = wd.shape[2]
    capacity = rows // owners
    piece = width // pieces
    return pl.pallas_call(
        expert_out_kernel,
        grid=(owners // chunk,),
        in_specs=[
            pl.BlockSpec((chunk * capacity, hidden), lambda c: (c, 0)),
            pl.BlockSpec((1, hidden, width), lambda c: (expert, 0, 0)),
        ],
        out_specs=pl.BlockSpec((pieces, chunk, capacity, piece), lambda c: (0, c, 0, 0)),
        out_shape=jax.ShapeDtypeStruct((pieces, owners, capacity, piece), BF16),
        compiler_params=pltpu.CompilerParams(vmem_limit_bytes=VMEM_BYTES),
        cost_estimate=pl.CostEstimate(
            flops=rows * hidden * width // 5, bytes_accessed=6 * 1024 * 102, transcendentals=0
        ),
        name="expert_out",
    )(hg, wd)


def expert_grads_kernel(
    x0_ref, c0_ref, hg0_ref, gr0_ref, ur0_ref, x1_ref, c1_ref, hg1_ref, gr1_ref, ur1_ref, dg_ref, du_ref, dd_ref
):
    owners, capacity, piece = x0_ref.shape
    rows = owners * capacity

    def step(x_ref, c_ref, hg_ref, gr_ref, ur_ref):
        x = x_ref[...].reshape(rows, piece)
        dg_ref[0] = dot_tn(gr_ref[...], x)
        du_ref[0] = dot_tn(ur_ref[...], x)
        dd_ref[0] = dot_tn(hg_ref[...], c_ref[...].reshape(rows, piece))

    pl.when(pl.program_id(0) == 0)(lambda: step(x0_ref, c0_ref, hg0_ref, gr0_ref, ur0_ref))
    pl.when(pl.program_id(0) == 1)(lambda: step(x1_ref, c1_ref, hg1_ref, gr1_ref, ur1_ref))


def expert_grads(first, second, pieces):
    owners, capacity, width = first[1].shape
    rows, hidden = first[2].shape
    piece = width // pieces
    row_spec = pl.BlockSpec((rows, hidden), lambda e, j: (0, 0))

    def specs(expert):
        stay = 0 if expert else pieces - 1
        wide = pl.BlockSpec(
            (owners, capacity, piece), lambda e, j: (0, 0, jnp.where(e == expert, j, stay))
        )
        return [wide, wide, row_spec, row_spec, row_spec]

    out_spec = pl.BlockSpec((1, hidden, piece), lambda e, j: (e, 0, j))
    out_shape = jax.ShapeDtypeStruct((2, hidden, width), F32)
    return pl.pallas_call(
        expert_grads_kernel,
        grid=(2, pieces),
        in_specs=specs(0) + specs(1),
        out_specs=[out_spec] * 3,
        out_shape=[out_shape] * 3,
        compiler_params=pltpu.CompilerParams(vmem_limit_bytes=VMEM_BYTES),
        cost_estimate=pl.CostEstimate(
            flops=rows * hidden * width, bytes_accessed=40 * 1024 * 102, transcendentals=0
        ),
        name="expert_grads",
    )(*first, *second)


def slot_probs(t_ref, b_ref, index, width):
    owners, capacity, _ = b_ref.shape
    rows = owners * capacity
    beside = b_ref[:, :, width:].reshape(rows, LANES).astype(F32)
    lane = lax.broadcasted_iota(jnp.int32, (rows, LANES), 1)
    expert = 2 * (lax.broadcasted_iota(jnp.int32, (rows, LANES), 0) // capacity) + index
    spread = jnp.where(lane == expert + ROPE, beside[:, 0:1], 0.0) + jnp.where(
        lane == expert, beside[:, 1:2], 0.0
    )
    return dot_nn(t_ref[...], spread.astype(BF16))


def combine_first_kernel(t_ref, b_ref, shared_ref, sum_ref, probs_ref):
    owners, capacity, _ = b_ref.shape
    width = shared_ref.shape[1]
    probs_ref[...] = slot_probs(t_ref, b_ref, 0, width)
    sum_ref[...] = shared_ref[...] + dot_nn(t_ref[...], b_ref[:, :, :width].reshape(owners * capacity, width))


def combine_kernel(
    me_ref, t_ref, b_ref, sum_ref, first_probs_ref, own_ref, probs_ref, send1_ref, send2_ref, send3_ref
):
    owners, capacity, _ = b_ref.shape
    rows = owners * capacity
    width = sum_ref.shape[1]
    piece = own_ref.shape[1]
    probs = first_probs_ref[...] + slot_probs(t_ref, b_ref, 1, width)
    probs = probs + pltpu.roll(probs, ROPE, 1)
    probs_ref[...] = probs
    high = probs.astype(BF16)
    low = (probs - high.astype(F32)).astype(BF16)
    short = lax.broadcasted_iota(jnp.int32, probs.shape, 1)
    message = jnp.where(short >= ROPE, high.astype(F32), low.astype(F32)).astype(BF16)
    for step, out_ref in enumerate((own_ref, send1_ref, send2_ref, send3_ref)):
        place = block_at(me_ref[0], step, width // piece, piece)
        part = sum_ref[:, place] + dot_nn(t_ref[...], b_ref[:, :, place].reshape(rows, piece))
        if step == 0:
            own_ref[...] = part
        else:
            out_ref[:, :piece] = part.astype(BF16)
            out_ref[:, piece:] = message


def attend_back_kernel(
    me_ref,
    core_ref,
    stream_ref,
    cot_ref,
    middle_ref,
    a0_ref,
    a1_ref,
    a2_ref,
    a3_ref,
    r1_ref,
    r2_ref,
    r3_ref,
    probs_own_ref,
    router_probs_ref,
    w_ref,
    router_ref,
    mixed_ref,
    normed_ref,
    query_ref,
    expanded_ref,
    key_ref,
    latent_ref,
    compressed_ref,
    probs_ref,
    attended_ref,
    gains_ref,
    latent_gain_ref,
    cos_ref,
    sin_ref,
    keep_ref,
    pass_ref,
    middle_grad_ref,
    own_ref,
    send1_ref,
    send2_ref,
    send3_ref,
    scr_ref,
    low_ref,
    wide_ref,
    sems,
):
    heads, tokens, _ = probs_ref.shape
    width = stream_ref.shape[1]
    piece = own_ref.shape[1]
    nope = heads * NOPE
    queries = nope + heads * ROPE
    edge = queries + LATENT + LANES
    outer = edge + heads * VDIM
    owners = 32
    shard = width // owners
    short = LATENT // owners
    count = width // piece
    me = me_ref[0]
    probs_grad = probs_own_ref[...]
    for r_ref in (r1_ref, r2_ref, r3_ref):
        other = r_ref[:, piece:].astype(F32)
        probs_grad = probs_grad + other + pltpu.roll(other, ROPE, 1)
    router_probs = router_probs_ref[...]
    logits_low = (
        router_probs * (probs_grad - jnp.sum(router_probs * probs_grad, axis=-1, keepdims=True))
    ).astype(BF16)
    router_back = dot_nt(logits_low, router_ref[...])
    for step, a_ref in enumerate((a0_ref, a1_ref, a2_ref, a3_ref)):
        wide_ref[:, block_at(me, step, count, piece)] = a_ref[...].astype(F32)
    mixed_grad = wide_ref[...] + router_back
    middle = middle_ref[...]
    norm_grad, second_gain_rows = rms_back(middle, inverse_rms(middle), gains_ref[1:2, :], mixed_grad)
    second_gain_grad = jnp.sum(second_gain_rows, axis=0, keepdims=True)
    middle_grad = cot_ref[...] + norm_grad
    middle_grad_ref[...] = middle_grad
    middle_low = middle_grad.astype(BF16)
    attended_grad = dot_nn(middle_low, w_ref[:, edge:outer]).astype(BF16)
    scale = (NOPE + ROPE) ** (-0.5)
    key_low = key_ref[...]
    key_odd = pltpu.roll(key_low.astype(F32), ROPE, 1).astype(BF16)
    latent = latent_ref[...]
    latent_part = jnp.zeros((tokens, LATENT), F32)
    key_even_grad = jnp.zeros((tokens, LANES), F32)
    key_odd_grad = jnp.zeros((tokens, LANES), F32)
    rope_grads = []
    grads4 = scr_ref.reshape(owners, shard, scr_ref.shape[1])
    for head in range(heads):
        pair = nope + head // 2 * LANES
        expanded = expanded_ref[:, head * 2 * NOPE : (head + 1) * 2 * NOPE]
        probs = probs_ref[head]
        head_grad = attended_grad[:, head * VDIM : (head + 1) * VDIM]
        value_grad = dot_tn(probs.astype(BF16), head_grad)
        probs_att = dot_nt(head_grad, expanded[:, NOPE:])
        scores = probs * (probs_att - jnp.sum(probs * probs_att, axis=-1, keepdims=True))
        raw_low = (scores * scale).astype(BF16)
        low_ref[:, head * NOPE : (head + 1) * NOPE] = dot_nn(raw_low, expanded[:, :NOPE]).astype(BF16)
        turn_grad = dot_nn(raw_low, key_odd if head % 2 else key_low)
        if head % 2:
            rope_grads[-1] = rope_grads[-1] + turn_grad
            key_odd_grad += dot_tn(raw_low, query_ref[:, pair : pair + LANES])
        else:
            rope_grads.append(turn_grad)
            key_even_grad += dot_tn(raw_low, query_ref[:, pair : pair + LANES])
        key_grad = dot_tn(raw_low, query_ref[:, head * NOPE : (head + 1) * NOPE])
        expanded_low = jnp.concatenate([key_grad, value_grad], axis=1).astype(BF16)
        up = w_ref[:, outer : outer + 2 * NOPE].reshape(owners, heads, short, 2 * NOPE)[:, head]
        up = up.reshape(LATENT, 2 * NOPE)
        latent_part += dot_nt(expanded_low, up)
        grads4[:, head * short : (head + 1) * short, outer : outer + 2 * NOPE] = (
            dot_tn(latent, expanded_low).astype(BF16).reshape(owners, short, 2 * NOPE)
        )
    rope_grad = jnp.concatenate(rope_grads, axis=1)
    low_ref[:, nope:queries] = rotated(rope_grad, cos_ref[...], -sin_ref[...]).astype(BF16)
    compressed = compressed_ref[...]
    latent_grad, latent_gain_rows = rms_back(
        compressed, inverse_rms(compressed), latent_gain_ref[2:3, :], latent_part
    )
    latent_gain_grad = jnp.sum(latent_gain_rows, axis=0, keepdims=True)
    low_ref[:, queries : queries + LATENT] = latent_grad.astype(BF16)
    lane = lax.broadcasted_iota(jnp.int32, (tokens, LANES), 1)
    key_grad = jnp.where(lane < ROPE, key_even_grad + pltpu.roll(key_odd_grad, ROPE, 1), 0.0)
    key_grad = rotated(key_grad, cos_ref[:, :LANES], -sin_ref[:, :LANES])
    low_ref[:, queries + LATENT : edge] = jnp.where(lane < ROPE, key_grad, 0.0).astype(BF16)
    low = low_ref[...]
    for step, out_ref in enumerate((own_ref, send1_ref, send2_ref, send3_ref)):
        place = block_at(me, step, count, piece)
        part = dot_nt(low, w_ref[place, :edge])
        wide_ref[:, place] = part
        out_ref[...] = part.astype(out_ref.dtype)
    stream = stream_ref[...].astype(F32)
    first_gain_grad = jnp.sum(wide_ref[...] * (stream * inverse_rms(stream)), axis=0, keepdims=True)
    late = dot_tn(normed_ref[...], low[:, queries:])
    sub = lax.broadcasted_iota(jnp.int32, (LANES, width), 0)
    gain_columns = (
        jnp.where(sub == ROPE, first_gain_grad, 0.0)
        + jnp.where(sub == ROPE + 1, second_gain_grad * (1.0 / count), 0.0)
    ).T
    key_columns = (late[:, LATENT:] + gain_columns).reshape(owners, shard, LANES)
    sub = lax.broadcasted_iota(jnp.int32, (LANES, LATENT), 0)
    latent_columns = jnp.where(sub == ROPE + 2, latent_gain_grad, 0.0).T.reshape(owners, short, LANES)
    grads4[:, :, queries : queries + LATENT] = (
        late[:, :LATENT].astype(BF16).reshape(owners, shard, LATENT)
    )
    grads4[:, :, queries + LATENT : edge] = key_columns.astype(BF16)
    grads4[:, :short, queries + LATENT : edge] = (key_columns[:, :short] + latent_columns).astype(BF16)
    scr_ref[:, edge:outer] = dot_tn(middle_low, attended_ref[...]).astype(BF16)
    scr_ref[:, :queries] = dot_tn(normed_ref[...], low[:, :queries]).astype(BF16)
    router_grad = dot_tn(mixed_ref[...], logits_low)
    scr_ref[:, outer + 2 * NOPE :] = router_grad[:, ROPE:].astype(BF16)
    halves = scr_ref.reshape(owners // 2, 2, shard, scr_ref.shape[1])
    core = core_ref[0]
    first = pltpu.make_async_copy(halves.at[:, 1 - core], pass_ref, sems.at[0])
    second = pltpu.make_async_copy(halves.at[:, core], keep_ref, sems.at[1])
    first.start()
    second.start()
    first.wait()
    second.wait()


def unpack_kernel(parts_ref, query_ref, late_ref, output_ref, up_ref, router_ref):
    heads = up_ref.shape[1] // (2 * NOPE)
    short = up_ref.shape[0]
    nope = heads * NOPE
    queries = nope + heads * ROPE
    edge = queries + LATENT + LANES
    outer = edge + heads * VDIM
    total = jnp.sum(parts_ref[...].astype(F32), axis=0)
    for head in range(heads):
        start = head * (NOPE + ROPE)
        query_ref[:, start : start + NOPE] = total[:, head * NOPE : (head + 1) * NOPE]
        query_ref[:, start + NOPE : start + NOPE + ROPE] = total[
            :, nope + head * ROPE : nope + (head + 1) * ROPE
        ]
        up_ref[:, head * 2 * NOPE : (head + 1) * 2 * NOPE] = total[
            head * short : (head + 1) * short, outer : outer + 2 * NOPE
        ]
    late_ref[...] = total[:, queries:edge]
    output_ref[...] = total[:, edge:outer]
    router_ref[...] = total[:, outer + 2 * NOPE :]


def late_kernel(own_ref, r1_ref, r2_ref, r3_ref, down_ref, gains_ref):
    total = own_ref[...] + r1_ref[...] + r2_ref[...] + r3_ref[...]
    down_ref[...] = total[:, : down_ref.shape[1]]
    columns = total[:, LATENT:]
    columns = jnp.concatenate([columns, jnp.zeros(columns.shape, F32)], axis=0)
    gains_ref[...] = columns.T[ROPE : ROPE + 8, :]


def stream_kernel(me_ref, middle_grad_ref, stream_ref, gains_ref, a0_ref, a1_ref, a2_ref, a3_ref, out_ref, wide_ref):
    piece = a0_ref.shape[1]
    count = stream_ref.shape[1] // piece
    for step, a_ref in enumerate((a0_ref, a1_ref, a2_ref, a3_ref)):
        wide_ref[:, block_at(me_ref[0], step, count, piece)] = a_ref[...].astype(F32)
    stream = stream_ref[...].astype(F32)
    norm_grad, _ = rms_back(stream, inverse_rms(stream), gains_ref[0:1, :], wide_ref[...])
    out_ref[...] = middle_grad_ref[...] + norm_grad


def routed_kernel(t0_ref, t1_ref, o_ref, own_ref, r1_ref, r2_ref, r3_ref, out_ref):
    owners, _, capacity, piece = o_ref.shape
    rows = owners * capacity
    total = own_ref[...]
    for r_ref in (r1_ref, r2_ref, r3_ref):
        total = total + r_ref[...].astype(F32)
    for index, t_ref in ((0, t0_ref), (1, t1_ref)):
        total = total + dot_nn(t_ref[...], o_ref[:, index].reshape(rows, piece))
    out_ref[...] = total.astype(BF16)


def result_kernel(me_ref, middle_ref, a0_ref, a1_ref, a2_ref, a3_ref, out_ref):
    piece = a0_ref.shape[1]
    count = middle_ref.shape[1] // piece
    for step, a_ref in enumerate((a0_ref, a1_ref, a2_ref, a3_ref)):
        place = block_at(me_ref[0], step, count, piece)
        out_ref[:, place] = middle_ref[:, place] + a_ref[...].astype(F32)


def shift(array, step):
    size = lax.axis_size("tensor")
    return lax.ppermute(array, "tensor", [(i, (i + step) % size) for i in range(size)])


def send_blocks(sends):
    return [shift(array, step + 1) for step, array in enumerate(sends)]


def share_small(low):
    size = lax.axis_size("tensor")
    return [low] + [shift(low, size - step) for step in range(1, size)]


def ring_first(rows):
    return shift(rows, 1), shift(rows, lax.axis_size("tensor") - 1)


def ring_second(rows, before, after):
    half = rows.shape[0] // 2
    across = [shift(before[:half], 1), shift(after[half:], lax.axis_size("tensor") - 1)]
    return [rows, after, jnp.concatenate(across, axis=0), before]


def after(array, *others):
    return lax.optimization_barrier((array, *others))[0]


def exchange(rows):
    shape = rows.shape
    return lax.all_to_all(
        rows.reshape(shape[0], -1, shape[-1]), "expert", split_axis=0, concat_axis=0, tiled=True
    ).reshape(shape)


def per_device(
    stream,
    segment_ids,
    expert_ids,
    first_gain,
    query_proj,
    latent_down,
    latent_gain,
    latent_up,
    output_proj,
    second_gain,
    router_proj,
    shared_gate,
    shared_up,
    shared_down,
    expert_gate,
    expert_up,
    expert_down,
    cotangent,
):
    tokens, width = stream.shape
    owners = lax.axis_size("expert")
    tensors = lax.axis_size("tensor")
    shard = query_proj.shape[0]
    heads = query_proj.shape[1] // (NOPE + ROPE)
    short = latent_up.shape[0]
    experts = router_proj.shape[1]
    hidden_columns = shared_gate.shape[1]
    local, _, expert_hidden = expert_gate.shape
    capacity = tokens * TOPK * 4 // (3 * experts)
    rows = owners * capacity
    piece = width // tensors
    nope = heads * NOPE
    queries = nope + heads * ROPE
    edge = queries + LATENT + LANES
    outer = edge + heads * VDIM
    me = lax.axis_index("tensor").astype(jnp.int32).reshape(1)
    base = (lax.axis_index("expert") * local).astype(jnp.int32).reshape(1)
    core = lax.rem(lax.axis_index("expert"), 2).astype(jnp.int32).reshape(1)
    smem = {0: pltpu.SMEM}

    gains = jnp.concatenate(
        [
            first_gain[:, None],
            second_gain[:, None],
            jnp.pad(latent_gain, (0, shard - short))[:, None],
            jnp.zeros((shard, ROPE - 3), BF16),
        ],
        axis=1,
    )
    by_head = query_proj.reshape(shard, heads, NOPE + ROPE)
    pack_one = jnp.concatenate(
        [
            by_head[:, :, :NOPE].reshape(shard, nope),
            by_head[:, :, NOPE:].reshape(shard, heads * ROPE),
            latent_down,
            router_proj,
            output_proj.T,
            latent_up.reshape(short, heads, 2 * NOPE).transpose(1, 0, 2).reshape(shard, 2 * NOPE),
            gains,
        ],
        axis=1,
    )
    pack_two = jnp.concatenate([shared_gate, shared_up, shared_down.T], axis=1)
    one = lax.all_gather(pack_one, "expert", axis=0, tiled=True)
    two = lax.all_gather(pack_two, "expert", axis=0, tiled=True)

    position = jnp.arange(tokens).astype(F32)
    exponent = jnp.arange(ROPE // 2).astype(F32) * (2.0 / ROPE)
    angles = position[:, None] * jnp.exp(-math.log(ROTARY_BASE) * exponent)[None, :]
    cosine = jnp.tile(jnp.cos(angles), (1, 2 * heads))
    sine = jnp.sin(angles)
    sine = jnp.tile(jnp.concatenate([-sine, sine], axis=1), (1, heads))

    t0, t1, cot_low, cot_out = run(
        routing_kernel,
        [
            ((tokens, rows), BF16),
            ((tokens, rows), BF16),
            ((tokens, width), BF16),
            ((owners, local, capacity, piece), BF16),
        ],
        [me, expert_ids.T, cotangent],
        2 * local * tokens * rows * (piece + experts),
        places=smem,
        name="routing",
    )

    cot_own = exchange(cot_out)
    cot_before, cot_after = ring_first(cot_own)
    (
        own,
        send1,
        send2,
        send3,
        normed,
        query,
        expanded,
        key,
        latent,
        compressed,
        probs,
        attended,
        gain_rows,
        latent_gain_rows,
    ) = run(
        attend_kernel,
        [
            ((tokens, piece), F32),
            ((tokens, piece), BF16),
            ((tokens, piece), BF16),
            ((tokens, piece), BF16),
            ((tokens, width), BF16),
            ((tokens, queries), BF16),
            ((tokens, heads * 2 * NOPE), BF16),
            ((tokens, LANES), BF16),
            ((tokens, LATENT), BF16),
            ((tokens, LATENT), F32),
            ((heads, tokens, tokens), F32),
            ((tokens, heads * VDIM), BF16),
            ((8, width), F32),
            ((8, LATENT), F32),
        ],
        [after(me, cot_own), stream, one, segment_ids, segment_ids.T, cosine, sine],
        2 * tokens * width * outer,
        places=smem,
        name="attend",
    )
    got = send_blocks([send1, send2, send3])
    attention = (own + got[0].astype(F32) + got[1].astype(F32) + got[2].astype(F32)).astype(BF16)
    attention = after(attention, cot_before, cot_after)
    middle, mixed, x_out = run(
        dispatch_kernel,
        [
            ((tokens, width), F32),
            ((tokens, width), BF16),
            ((owners, capacity, width + piece), BF16),
        ],
        [me, stream, *share_small(attention), gain_rows, t0, t1],
        2 * tokens * rows * (width + piece),
        places=smem,
        name="dispatch",
    )
    x_in = exchange(x_out)
    cots = ring_second(cot_own, cot_before, cot_after)
    x1s = x_in[:, :, width:]
    x1_before, x1_after = ring_first(x1s)
    x1s = [x_in] + ring_second(x1s, x1_before, x1_after)[1:]
    router_block = one[:, queries + LATENT : edge]
    (
        shared_own,
        shared1,
        shared2,
        shared3,
        shared_back,
        router_probs,
        shared_grads,
    ) = run(
        shared_kernel,
        [
            ((tokens, piece), F32),
            ((tokens, piece), BF16),
            ((tokens, piece), BF16),
            ((tokens, piece), BF16),
            ((tokens, width), F32),
            ((tokens, LANES), F32),
            ((width, 3 * hidden_columns), BF16),
        ],
        [me, mixed, cot_low, two, router_block],
        18 * tokens * width * hidden_columns,
        places=smem,
        name="shared",
    )
    base = after(base, shared_back)

    gate_t = expert_gate.transpose(0, 2, 1)
    up_t = expert_up.transpose(0, 2, 1)
    chunk = owners // 2
    back0, c0, hg0, gr0, ur0 = expert_back(
        False, me, base, [x_in], cots, gate_t, up_t, expert_down, one, edge // LANES - 1, chunk // 2
    )
    back0 = exchange(back0)
    back1, c1, hg1, gr1, ur1, x1 = expert_back(
        True, me, after(base, hg0), x1s, cots, gate_t, up_t, expert_down, one, edge // LANES - 1, chunk // 2
    )
    back1 = exchange(after(back1, back0))
    gr0 = after(gr0, back0)
    gate_grad, up_grad, down_grad = expert_grads(
        (x_in, c0, hg0, gr0, ur0), (x1, c1, hg1, gr1, ur1), tensors
    )
    out0 = expert_out(0, hg0, expert_down, owners, tensors, chunk)
    out1 = expert_out(1, after(hg1, out0), expert_down, owners, tensors, chunk)
    out_rows = [
        lax.psum_scatter(out, "tensor", scatter_dimension=0, tiled=True).reshape(owners, 1, capacity, piece)
        for out in (out0, out1)
    ]

    first_sum, first_probs = run(
        combine_first_kernel,
        [((tokens, width), F32), ((tokens, LANES), F32)],
        [t0, back0, shared_back],
        2 * tokens * rows * width,
        name="combine_first",
    )
    own, probs_own, send1, send2, send3 = run(
        combine_kernel,
        [
            ((tokens, piece), F32),
            ((tokens, LANES), F32),
            ((tokens, piece + LANES), BF16),
            ((tokens, piece + LANES), BF16),
            ((tokens, piece + LANES), BF16),
        ],
        [after(me, out1, gate_grad), t1, back1, first_sum, first_probs],
        2 * tokens * rows * width,
        places=smem,
        name="combine",
    )
    got = send_blocks([send1, send2, send3])
    out_rows = exchange(after(jnp.concatenate(out_rows, axis=1), own))
    shared_sum = lax.psum_scatter(
        after(shared_grads, own), "expert", scatter_dimension=0, tiled=True
    )
    mixed_sum = (
        own
        + got[0][:, :piece].astype(F32)
        + got[1][:, :piece].astype(F32)
        + got[2][:, :piece].astype(F32)
    ).astype(BF16)
    keep, passed, middle_grad, own, send1, send2, send3 = run(
        attend_back_kernel,
        [
            ((owners // 2, shard, outer + 2 * NOPE + experts), BF16),
            ((owners // 2, shard, outer + 2 * NOPE + experts), BF16),
            ((tokens, width), F32),
            ((tokens, piece), F32),
            ((tokens, piece), BF16),
            ((tokens, piece), BF16),
            ((tokens, piece), BF16),
        ],
        [
            me,
            core,
            stream,
            cotangent,
            middle,
            *share_small(mixed_sum),
            *got,
            probs_own,
            router_probs,
            one,
            router_block,
            mixed,
            normed,
            query,
            expanded,
            key,
            latent,
            compressed,
            probs,
            attended,
            gain_rows,
            latent_gain_rows,
            cosine,
            sine,
        ],
        2 * tokens * width * (3 * edge + 2 * outer),
        scratch=[
            pltpu.VMEM((width, outer + 2 * NOPE + experts), BF16),
            pltpu.VMEM((tokens, edge), BF16),
            pltpu.VMEM((tokens, width), F32),
            pltpu.SemaphoreType.DMA((2,)),
        ],
        places={0: pltpu.SMEM, 1: pltpu.SMEM},
        out_places={0: pl.ANY, 1: pl.ANY},
        name="attend_back",
    )
    paired = lax.ppermute(after(passed, out_rows), "expert", [(i, i ^ 1) for i in range(owners)])
    paired = (keep.astype(F32) + paired.astype(F32)).astype(BF16)
    parts = lax.all_to_all(
        paired,
        "expert",
        split_axis=0,
        concat_axis=0,
        tiled=True,
        axis_index_groups=[[2 * i + c for i in range(owners // 2)] for c in range(2)],
    )
    got = send_blocks([send1, send2, send3])
    first_sum = (own + got[0].astype(F32) + got[1].astype(F32) + got[2].astype(F32)).astype(BF16)
    (stream_grad,) = run(
        stream_kernel,
        [((tokens, width), F32)],
        [me, middle_grad, stream, gain_rows, *share_small(first_sum)],
        0,
        scratch=[pltpu.VMEM((tokens, width), F32)],
        places=smem,
        name="stream",
    )

    got = send_blocks([shared1, shared2, shared3])
    (branch,) = run(
        routed_kernel,
        [((tokens, piece), BF16)],
        [t0, t1, out_rows, shared_own, *got],
        4 * tokens * rows * piece,
        name="routed",
    )
    (result,) = run(
        result_kernel,
        [((tokens, width), F32)],
        [me, middle, *share_small(branch)],
        0,
        places=smem,
        name="result",
    )

    shared_sum = shared_sum.astype(F32)
    gate_sum = shared_sum[:, :hidden_columns]
    up_sum = shared_sum[:, hidden_columns : 2 * hidden_columns]
    down_sum = shared_sum[:, 2 * hidden_columns :]
    parts = after(parts, stream_grad, result, gate_sum, up_sum, down_sum)
    query_grad, late, output_grad, latent_up_grad, router_grad = run(
        unpack_kernel,
        [
            (query_proj.shape, F32),
            ((shard, edge - queries), F32),
            ((shard, heads * VDIM), F32),
            (latent_up.shape, F32),
            (router_proj.shape, F32),
        ],
        [parts],
        0,
        name="unpack",
    )
    latent_down_grad, gain_grads = run(
        late_kernel,
        [(latent_down.shape, F32), ((8, LANES), F32)],
        [late, *(shift(late, step) for step in range(1, tensors))],
        0,
        name="late",
    )
    return (
        result,
        stream_grad,
        gain_grads[0, :shard],
        query_grad,
        latent_down_grad,
        gain_grads[2, :short],
        latent_up_grad,
        output_grad.T,
        gain_grads[1, :shard],
        router_grad,
        gate_sum,
        up_sum,
        down_sum.T,
        gate_grad.transpose(0, 2, 1),
        up_grad.transpose(0, 2, 1),
        down_grad,
    )


def solution(mesh):
    placed = (
        P("expert", None),
        P("expert", None),
        P("expert", None),
        P("expert"),
        P("expert", "tensor"),
        P("expert", None),
        P("expert"),
        P("expert", "tensor"),
        P("tensor", "expert"),
        P("expert"),
        P("expert", None),
        P("expert", "tensor"),
        P("expert", "tensor"),
        P("tensor", "expert"),
        P("expert", None, "tensor"),
        P("expert", None, "tensor"),
        P("expert", "tensor", None),
        P("expert", None),
    )
    return jax.shard_map(
        per_device,
        mesh=mesh,
        in_specs=placed,
        out_specs=(
            P("expert", None),
            P("expert", None),
            P("expert"),
            P("expert", "tensor"),
            P("expert", None),
            P("expert"),
            P("expert", "tensor"),
            P("tensor", "expert"),
            P("expert"),
            P("expert", None),
            P("expert", "tensor"),
            P("expert", "tensor"),
            P("tensor", "expert"),
            P("expert", None, "tensor"),
            P("expert", None, "tensor"),
            P("expert", "tensor", None),
        ),
        check_vma=False,
    )
```

```python
import functools
import math

import jax
import jax.numpy as jnp
from jax import lax
from jax.experimental import pallas as pl
from jax.experimental.pallas import tpu as pltpu
from jax.sharding import PartitionSpec as P

NOPE = 128
ROPE = 64
VDIM = 128
LATENT = 512
TOPK = 6
EPSILON = 1e-06
ROTARY_BASE = 10000.0

BF16 = jnp.bfloat16
F32 = jnp.float32
VMEM_BYTES = 60 * 1024 * 1024
LANES = 128
COST_SCALE = 10


def dot_nn(left, right):
    return lax.dot_general(left, right, (((1,), (0,)), ((), ())), preferred_element_type=F32)


def dot_nt(left, right):
    return lax.dot_general(left, right, (((1,), (1,)), ((), ())), preferred_element_type=F32)


def dot_tn(left, right):
    return lax.dot_general(left, right, (((0,), (0,)), ((), ())), preferred_element_type=F32)


def silu_parts(pre_values):
    sigmoid_value = 1.0 / (1.0 + jnp.exp(-pre_values))
    return (pre_values * sigmoid_value, sigmoid_value * (1.0 + pre_values * (1.0 - sigmoid_value)))


def inverse_rms(values):
    return lax.rsqrt(jnp.mean(values * values, axis=-1, keepdims=True) + EPSILON)


def rms_back(values, scale, gain, grad):
    normed = values * scale
    weighted = grad * gain
    return (
        scale * (weighted - normed * jnp.mean(weighted * normed, axis=-1, keepdims=True)),
        grad * normed,
    )


def turned(values):
    width = values.shape[1]
    lane = lax.broadcasted_iota(jnp.int32, values.shape, 1) % ROPE
    half = ROPE // 2
    return jnp.where(
        lane < half, pltpu.roll(values, width - half, 1), pltpu.roll(values, half, 1)
    )


def rotated(values, cosine, sine):
    return values * cosine + turned(values) * sine


def block_at(me, step, count, width):
    return pl.ds(pl.multiple_of(lax.rem(me + step, count) * width, width), width)


def run(kernel, outs, args, flops, scratch=(), name=None, places=None, aliases=None, out_places=None):
    places = places or {}
    out_places = out_places or {}
    in_specs = [pl.BlockSpec(memory_space=places.get(i, pltpu.VMEM)) for i in range(len(args))]
    out_specs = [pl.BlockSpec(memory_space=out_places.get(i, pltpu.VMEM)) for i in range(len(outs))]
    moved = sum(a.size * a.dtype.itemsize for a in args) + sum(
        math.prod(shape) * jnp.dtype(dtype).itemsize for shape, dtype in outs
    )
    return pl.pallas_call(
        kernel,
        in_specs=in_specs,
        out_specs=out_specs,
        out_shape=[jax.ShapeDtypeStruct(shape, dtype) for shape, dtype in outs],
        scratch_shapes=list(scratch),
        input_output_aliases=aliases or {},
        compiler_params=pltpu.CompilerParams(vmem_limit_bytes=VMEM_BYTES),
        cost_estimate=pl.CostEstimate(
            flops=flops // COST_SCALE, bytes_accessed=moved // COST_SCALE, transcendentals=0
        ),
        name=name,
    )(*args)


def routing_kernel(me_ref, ids_ref, cot_ref, t0_ref, t1_ref, low_ref, out_ref):
    choices, tokens = ids_ref.shape
    owners, local, capacity, piece = out_ref.shape
    experts = owners * local
    rows = owners * capacity
    expert = lax.broadcasted_iota(jnp.int32, (experts, tokens), 0)
    chosen = jnp.zeros((experts, tokens), F32)
    for choice in range(choices):
        chosen += jnp.where(ids_ref[choice : choice + 1, :] == expert, 1.0, 0.0)
    before = jnp.where(
        lax.broadcasted_iota(jnp.int32, (tokens, tokens), 0)
        < lax.broadcasted_iota(jnp.int32, (tokens, tokens), 1),
        1.0,
        0.0,
    ).astype(BF16)
    place = dot_nn(chosen.astype(BF16), before)
    place = jnp.where(chosen > 0.5, place, -1.0).astype(BF16)
    low = cot_ref[...].astype(BF16)
    low_ref[...] = low
    mine = cot_ref[:, block_at(me_ref[0], 0, cot_ref.shape[1] // piece, piece)].astype(BF16)
    slot = (lax.broadcasted_iota(jnp.int32, (tokens, rows), 1) % capacity).astype(F32)
    for index, t_ref in ((0, t0_ref), (1, t1_ref)):
        spread = jnp.where(
            lax.broadcasted_iota(jnp.int32, (experts, rows), 0)
            == lax.broadcasted_iota(jnp.int32, (experts, rows), 1) // capacity * local + index,
            1.0,
            0.0,
        ).astype(BF16)
        wanted = dot_tn(place, spread)
        matrix = jnp.where(wanted == slot, 1.0, 0.0).astype(BF16)
        t_ref[...] = matrix
        out_ref[:, index] = dot_tn(matrix, mine).astype(BF16).reshape(owners, capacity, piece)


def attend_kernel(
    me_ref,
    stream_ref,
    w_ref,
    seg_row_ref,
    seg_col_ref,
    cos_ref,
    sin_ref,
    own_ref,
    send1_ref,
    send2_ref,
    send3_ref,
    normed_ref,
    query_ref,
    expanded_ref,
    key_ref,
    latent_ref,
    compressed_ref,
    probs_ref,
    attended_ref,
    gains_ref,
    latent_gain_ref,
):
    heads, tokens, _ = probs_ref.shape
    width = stream_ref.shape[1]
    piece = own_ref.shape[1]
    nope = heads * NOPE
    queries = nope + heads * ROPE
    edge = queries + LATENT + LANES
    outer = edge + heads * VDIM
    owners = 32
    columns = jnp.concatenate(
        [w_ref[:, outer + 2 * NOPE :].astype(F32), jnp.zeros((width, ROPE), F32)], axis=1
    )
    gains = columns.T[:8, :]
    gains_ref[...] = gains
    shard = width // owners
    short = LATENT // owners
    latent_gain = (
        columns.reshape(owners, shard, LANES)[:, :short, :].reshape(LATENT, LANES).T[:8, :]
    )
    latent_gain_ref[...] = latent_gain
    stream = stream_ref[...].astype(F32)
    normed = (stream * inverse_rms(stream) * gains[0:1, :]).astype(BF16)
    normed_ref[...] = normed
    projected = dot_nn(normed, w_ref[:, :edge])
    query_ref[:, :nope] = projected[:, :nope].astype(BF16)
    query_ref[:, nope:] = rotated(projected[:, nope:queries], cos_ref[...], sin_ref[...]).astype(BF16)
    compressed = projected[:, queries : queries + LATENT]
    compressed_ref[...] = compressed
    latent = (compressed * inverse_rms(compressed) * latent_gain[2:3, :]).astype(BF16)
    latent_ref[...] = latent
    raw_key = projected[:, queries + LATENT : edge]
    key = rotated(raw_key, cos_ref[:, :LANES], sin_ref[:, :LANES])
    lane = lax.broadcasted_iota(jnp.int32, key.shape, 1)
    key = jnp.where(lane < ROPE, key, 0.0)
    key_low = key.astype(BF16)
    key_odd = pltpu.roll(key, ROPE, 1).astype(BF16)
    key_ref[...] = key_low
    row = lax.broadcasted_iota(jnp.int32, (tokens, tokens), 0)
    column = lax.broadcasted_iota(jnp.int32, (tokens, tokens), 1)
    allowed = (seg_col_ref[...] == seg_row_ref[...]) & (column <= row)
    scale = (NOPE + ROPE) ** (-0.5)
    for head in range(heads):
        block = slice(head * 2 * NOPE, (head + 1) * 2 * NOPE)
        up = w_ref[:, outer : outer + 2 * NOPE].reshape(owners, heads, short, 2 * NOPE)[:, head]
        up = up.reshape(LATENT, 2 * NOPE)
        expanded = dot_nn(latent, up).astype(BF16)
        expanded_ref[:, block] = expanded
        pair = nope + head // 2 * LANES
        raw = dot_nt(query_ref[:, head * NOPE : (head + 1) * NOPE], expanded[:, :NOPE]) + dot_nt(
            query_ref[:, pair : pair + LANES], key_odd if head % 2 else key_low
        )
        scores = jnp.where(allowed, raw * scale, -1e30)
        weight = jnp.exp(scores - jnp.max(scores, axis=-1, keepdims=True))
        probs = weight / jnp.sum(weight, axis=-1, keepdims=True)
        probs_ref[head] = probs
        attended_ref[:, head * VDIM : (head + 1) * VDIM] = dot_nn(
            probs.astype(BF16), expanded[:, NOPE:]
        ).astype(BF16)
    attended = attended_ref[...]
    for step, out_ref in enumerate((own_ref, send1_ref, send2_ref, send3_ref)):
        part = dot_nt(attended, w_ref[block_at(me_ref[0], step, width // piece, piece), edge:outer])
        out_ref[...] = part.astype(out_ref.dtype)


def dispatch_kernel(
    me_ref, stream_ref, a0_ref, a1_ref, a2_ref, a3_ref, gains_ref, t0_ref, t1_ref, middle_ref, mixed_ref, out_ref
):
    piece = a0_ref.shape[1]
    width = stream_ref.shape[1]
    count = width // piece
    owners, capacity, _ = out_ref.shape
    for step, a_ref in enumerate((a0_ref, a1_ref, a2_ref, a3_ref)):
        place = block_at(me_ref[0], step, count, piece)
        middle_ref[:, place] = stream_ref[:, place].astype(F32) + a_ref[...].astype(F32)
    middle = middle_ref[...]
    mixed = (middle * inverse_rms(middle) * gains_ref[1:2, :]).astype(BF16)
    mixed_ref[...] = mixed
    mine = mixed_ref[:, block_at(me_ref[0], 0, count, piece)]
    out_ref[:, :, width:] = dot_tn(t1_ref[...], mine).astype(BF16).reshape(owners, capacity, piece)
    out_ref[:, :, :width] = dot_tn(t0_ref[...], mixed).astype(BF16).reshape(owners, capacity, width)


def shared_kernel(
    me_ref,
    mixed_ref,
    cot_ref,
    w_ref,
    router_ref,
    own_ref,
    send1_ref,
    send2_ref,
    send3_ref,
    back_ref,
    probs_ref,
    grads_ref,
):
    width = mixed_ref.shape[1]
    piece = own_ref.shape[1]
    hidden_columns = w_ref.shape[1] // 3
    mixed = mixed_ref[...]
    cot = cot_ref[...]
    pre = dot_nn(mixed, w_ref[:, : 2 * hidden_columns])
    gate_pre, up_pre = pre[:, :hidden_columns], pre[:, hidden_columns:]
    act, slope = silu_parts(gate_pre)
    hidden = (act * up_pre).astype(BF16)
    hidden_grad = dot_nn(cot, w_ref[:, 2 * hidden_columns :])
    pair = jnp.concatenate([hidden_grad * up_pre * slope, hidden_grad * act], axis=1).astype(BF16)
    grads_ref[:, : 2 * hidden_columns] = dot_tn(mixed, pair).astype(BF16)
    grads_ref[:, 2 * hidden_columns :] = dot_tn(cot, hidden).astype(BF16)
    back_ref[...] = dot_nt(pair, w_ref[:, : 2 * hidden_columns])
    logits = dot_nn(mixed, router_ref[...])
    lane = lax.broadcasted_iota(jnp.int32, logits.shape, 1)
    logits = jnp.where(lane >= ROPE, logits, -1e30)
    weight = jnp.exp(logits - jnp.max(logits, axis=-1, keepdims=True))
    probs_ref[...] = weight / jnp.sum(weight, axis=-1, keepdims=True)
    for step, out_ref in enumerate((own_ref, send1_ref, send2_ref, send3_ref)):
        place = block_at(me_ref[0], step, width // piece, piece)
        part = dot_nt(hidden, w_ref[place, 2 * hidden_columns :])
        out_ref[...] = part.astype(out_ref.dtype)


def expert_back_kernel(split, *refs):
    if split:
        me_ref, base_ref, x0_ref, x1_ref, x2_ref, x3_ref = refs[:6]
        refs = refs[6:]
    else:
        me_ref, base_ref, x_ref = refs[:3]
        refs = refs[3:]
    c0_ref, c1_ref, c2_ref, c3_ref, wg_ref, wu_ref, wd_ref, router_ref = refs[:8]
    refs = refs[8:]
    if split:
        back_ref, c_ref, hg_ref, gr_ref, ur_ref, x_ref, wide_ref, down_ref, tall_ref = refs
    else:
        back_ref, c_ref, hg_ref, gr_ref, ur_ref, wide_ref, down_ref, tall_ref = refs
    sources, capacity, width = c_ref.shape
    rows = sources * capacity
    piece = c0_ref.shape[-1]
    count = width // piece
    hidden_columns = wd_ref.shape[1]
    padded = down_ref.shape[1]
    me = me_ref[0]

    @pl.when(pl.program_id(0) == 0)
    def _():
        rest = jnp.zeros((padded - hidden_columns, width), BF16)
        gate_up = jnp.concatenate([wg_ref[0], rest, wu_ref[0], rest], axis=0)
        tall_ref[...] = gate_up
        wide_ref[...] = gate_up.T
        down_ref[...] = jnp.concatenate([wd_ref[0], rest], axis=0).T

    for step, p_ref in enumerate((c0_ref, c1_ref, c2_ref, c3_ref)):
        c_ref[:, :, block_at(me, step, count, piece)] = p_ref[:, 0]
    if split:
        for step, p_ref in enumerate((x0_ref, x1_ref, x2_ref, x3_ref)):
            x_ref[:, :, block_at(me, step, count, piece)] = p_ref[...]
    x = x_ref[...].reshape(rows, width)
    expert = base_ref[0] + (1 if split else 0) + ROPE
    logits = dot_nn(x, router_ref[...])
    lane = lax.broadcasted_iota(jnp.int32, logits.shape, 1)
    logits = jnp.where(lane >= ROPE, logits, -1e30)
    weight = jnp.exp(logits - jnp.max(logits, axis=-1, keepdims=True))
    gate = jnp.sum(jnp.where(lane == expert, weight, 0.0), axis=-1, keepdims=True) / jnp.sum(
        weight, axis=-1, keepdims=True
    )
    pre = dot_nn(x, wide_ref[...])
    gate_pre, up_pre = pre[:, :padded], pre[:, padded:]
    hidden_cot = dot_nn(c_ref[...].reshape(rows, width), down_ref[...])
    act, slope = silu_parts(gate_pre)
    hidden = (act * up_pre).astype(BF16).astype(F32)
    gate_grad = jnp.sum(hidden * hidden_cot, axis=-1, keepdims=True)
    hidden_grad = gate * hidden_cot
    gate_rows = (hidden_grad * up_pre * slope).astype(BF16)
    up_rows = (hidden_grad * act).astype(BF16)
    hg_ref[...] = (gate * hidden).astype(BF16)[:, :hidden_columns]
    gr_ref[...] = gate_rows[:, :hidden_columns]
    ur_ref[...] = up_rows[:, :hidden_columns]
    high = gate_grad.astype(BF16).astype(F32)
    low = gate_grad - high
    beside = jnp.where(lane == 0, high, 0.0) + jnp.where(lane == 1, low, 0.0)
    back = dot_nn(jnp.concatenate([gate_rows, up_rows], axis=1), tall_ref[...])
    back_ref[:, :, :width] = back.astype(BF16).reshape(sources, capacity, width)
    back_ref[:, :, width:] = beside.astype(BF16).reshape(sources, capacity, LANES)


def expert_back(split, me, base, xs, cs, wg, wu, wd, router, router_at, chunk):
    owners, local, capacity, piece = cs[0].shape
    hidden, width = wg.shape[1:]
    local_index = 1 if split else 0
    rows = owners * capacity
    padded = -(-hidden // LANES) * LANES
    scalar = pl.BlockSpec(memory_space=pltpu.SMEM)
    row_spec = pl.BlockSpec((chunk * capacity, hidden), lambda c: (c, 0))
    row_shape = jax.ShapeDtypeStruct((rows, hidden), BF16)
    wide_spec = pl.BlockSpec((chunk, capacity, width), lambda c: (c, 0, 0))
    wide_shape = jax.ShapeDtypeStruct((owners, capacity, width), BF16)
    narrow_spec = pl.BlockSpec((chunk, capacity, piece), lambda c: (c, 0, 0))
    own_spec = pl.BlockSpec((chunk, capacity, piece), lambda c: (c, 0, width // piece))
    cot_spec = pl.BlockSpec((chunk, 1, capacity, piece), lambda c: (c, local_index, 0, 0))
    weight_spec = pl.BlockSpec((1, hidden, width), lambda c: (local_index, 0, 0))
    in_specs = [scalar, scalar]
    in_specs += [own_spec] + [narrow_spec] * 3 if split else [wide_spec]
    in_specs += [cot_spec] * 4 + [weight_spec] * 3 + [pl.BlockSpec((width, LANES), lambda c: (0, router_at))]
    out_specs = [pl.BlockSpec((chunk, capacity, width + LANES), lambda c: (c, 0, 0)), wide_spec]
    out_shape = [jax.ShapeDtypeStruct((owners, capacity, width + LANES), BF16), wide_shape]
    last_spec, last_shape = ([wide_spec], [wide_shape]) if split else ([], [])
    return pl.pallas_call(
        functools.partial(expert_back_kernel, split),
        grid=(owners // chunk,),
        in_specs=in_specs,
        out_specs=out_specs + [row_spec] * 3 + last_spec,
        out_shape=out_shape + [row_shape] * 3 + last_shape,
        scratch_shapes=[
            pltpu.VMEM((width, 2 * padded), BF16),
            pltpu.VMEM((width, padded), BF16),
            pltpu.VMEM((2 * padded, width), BF16),
        ],
        compiler_params=pltpu.CompilerParams(vmem_limit_bytes=VMEM_BYTES),
        cost_estimate=pl.CostEstimate(
            flops=100 * rows * hidden * width, bytes_accessed=24 * 1024 * 1024, transcendentals=0
        ),
        name="expert_back",
    )(me, base, *xs, *cs, wg, wu, wd, router)


def expert_out_kernel(hg_ref, wd_ref, out_ref):
    pieces, sources, capacity, piece = out_ref.shape
    out = dot_nn(hg_ref[...], wd_ref[0]).astype(BF16)
    for index in range(pieces):
        out_ref[index] = out[:, index * piece : (index + 1) * piece].reshape(sources, capacity, piece)


def expert_out(expert, hg, wd, owners, pieces, chunk):
    rows, hidden = hg.shape
    width = wd.shape[2]
    capacity = rows // owners
    piece = width // pieces
    return pl.pallas_call(
        expert_out_kernel,
        grid=(owners // chunk,),
        in_specs=[
            pl.BlockSpec((chunk * capacity, hidden), lambda c: (c, 0)),
            pl.BlockSpec((1, hidden, width), lambda c: (expert, 0, 0)),
        ],
        out_specs=pl.BlockSpec((pieces, chunk, capacity, piece), lambda c: (0, c, 0, 0)),
        out_shape=jax.ShapeDtypeStruct((pieces, owners, capacity, piece), BF16),
        compiler_params=pltpu.CompilerParams(vmem_limit_bytes=VMEM_BYTES),
        cost_estimate=pl.CostEstimate(
            flops=rows * hidden * width // 5, bytes_accessed=6 * 1024 * 102, transcendentals=0
        ),
        name="expert_out",
    )(hg, wd)


def expert_grads_kernel(
    x0_ref, c0_ref, hg0_ref, gr0_ref, ur0_ref, x1_ref, c1_ref, hg1_ref, gr1_ref, ur1_ref, dg_ref, du_ref, dd_ref
):
    owners, capacity, piece = x0_ref.shape
    rows = owners * capacity

    def step(x_ref, c_ref, hg_ref, gr_ref, ur_ref):
        x = x_ref[...].reshape(rows, piece)
        dg_ref[0] = dot_tn(gr_ref[...], x)
        du_ref[0] = dot_tn(ur_ref[...], x)
        dd_ref[0] = dot_tn(hg_ref[...], c_ref[...].reshape(rows, piece))

    pl.when(pl.program_id(0) == 0)(lambda: step(x0_ref, c0_ref, hg0_ref, gr0_ref, ur0_ref))
    pl.when(pl.program_id(0) == 1)(lambda: step(x1_ref, c1_ref, hg1_ref, gr1_ref, ur1_ref))


def expert_grads(first, second, pieces):
    owners, capacity, width = first[1].shape
    rows, hidden = first[2].shape
    piece = width // pieces
    row_spec = pl.BlockSpec((rows, hidden), lambda e, j: (0, 0))

    def specs(expert):
        stay = 0 if expert else pieces - 1
        wide = pl.BlockSpec(
            (owners, capacity, piece), lambda e, j: (0, 0, jnp.where(e == expert, j, stay))
        )
        return [wide, wide, row_spec, row_spec, row_spec]

    out_spec = pl.BlockSpec((1, hidden, piece), lambda e, j: (e, 0, j))
    out_shape = jax.ShapeDtypeStruct((2, hidden, width), F32)
    return pl.pallas_call(
        expert_grads_kernel,
        grid=(2, pieces),
        in_specs=specs(0) + specs(1),
        out_specs=[out_spec] * 3,
        out_shape=[out_shape] * 3,
        compiler_params=pltpu.CompilerParams(vmem_limit_bytes=VMEM_BYTES),
        cost_estimate=pl.CostEstimate(
            flops=rows * hidden * width, bytes_accessed=40 * 1024 * 102, transcendentals=0
        ),
        name="expert_grads",
    )(*first, *second)


def slot_probs(t_ref, b_ref, index, width):
    owners, capacity, _ = b_ref.shape
    rows = owners * capacity
    beside = b_ref[:, :, width:].reshape(rows, LANES).astype(F32)
    lane = lax.broadcasted_iota(jnp.int32, (rows, LANES), 1)
    expert = 2 * (lax.broadcasted_iota(jnp.int32, (rows, LANES), 0) // capacity) + index
    spread = jnp.where(lane == expert + ROPE, beside[:, 0:1], 0.0) + jnp.where(
        lane == expert, beside[:, 1:2], 0.0
    )
    return dot_nn(t_ref[...], spread.astype(BF16))


def combine_first_kernel(t_ref, b_ref, shared_ref, sum_ref, probs_ref):
    owners, capacity, _ = b_ref.shape
    width = shared_ref.shape[1]
    probs_ref[...] = slot_probs(t_ref, b_ref, 0, width)
    sum_ref[...] = shared_ref[...] + dot_nn(t_ref[...], b_ref[:, :, :width].reshape(owners * capacity, width))


def combine_kernel(
    me_ref, t_ref, b_ref, sum_ref, first_probs_ref, own_ref, probs_ref, send1_ref, send2_ref, send3_ref
):
    owners, capacity, _ = b_ref.shape
    rows = owners * capacity
    width = sum_ref.shape[1]
    piece = own_ref.shape[1]
    probs = first_probs_ref[...] + slot_probs(t_ref, b_ref, 1, width)
    probs = probs + pltpu.roll(probs, ROPE, 1)
    probs_ref[...] = probs
    high = probs.astype(BF16)
    low = (probs - high.astype(F32)).astype(BF16)
    short = lax.broadcasted_iota(jnp.int32, probs.shape, 1)
    message = jnp.where(short >= ROPE, high.astype(F32), low.astype(F32)).astype(BF16)
    for step, out_ref in enumerate((own_ref, send1_ref, send2_ref, send3_ref)):
        place = block_at(me_ref[0], step, width // piece, piece)
        part = sum_ref[:, place] + dot_nn(t_ref[...], b_ref[:, :, place].reshape(rows, piece))
        if step == 0:
            own_ref[...] = part
        else:
            out_ref[:, :piece] = part.astype(BF16)
            out_ref[:, piece:] = message


def attend_back_kernel(
    me_ref,
    core_ref,
    stream_ref,
    cot_ref,
    middle_ref,
    a0_ref,
    a1_ref,
    a2_ref,
    a3_ref,
    r1_ref,
    r2_ref,
    r3_ref,
    probs_own_ref,
    router_probs_ref,
    w_ref,
    router_ref,
    mixed_ref,
    normed_ref,
    query_ref,
    expanded_ref,
    key_ref,
    latent_ref,
    compressed_ref,
    probs_ref,
    attended_ref,
    gains_ref,
    latent_gain_ref,
    cos_ref,
    sin_ref,
    keep_ref,
    pass_ref,
    middle_grad_ref,
    own_ref,
    send1_ref,
    send2_ref,
    send3_ref,
    scr_ref,
    low_ref,
    wide_ref,
    sems,
):
    heads, tokens, _ = probs_ref.shape
    width = stream_ref.shape[1]
    piece = own_ref.shape[1]
    nope = heads * NOPE
    queries = nope + heads * ROPE
    edge = queries + LATENT + LANES
    outer = edge + heads * VDIM
    owners = 32
    shard = width // owners
    short = LATENT // owners
    count = width // piece
    me = me_ref[0]
    probs_grad = probs_own_ref[...]
    for r_ref in (r1_ref, r2_ref, r3_ref):
        other = r_ref[:, piece:].astype(F32)
        probs_grad = probs_grad + other + pltpu.roll(other, ROPE, 1)
    router_probs = router_probs_ref[...]
    logits_low = (
        router_probs * (probs_grad - jnp.sum(router_probs * probs_grad, axis=-1, keepdims=True))
    ).astype(BF16)
    router_back = dot_nt(logits_low, router_ref[...])
    for step, a_ref in enumerate((a0_ref, a1_ref, a2_ref, a3_ref)):
        wide_ref[:, block_at(me, step, count, piece)] = a_ref[...].astype(F32)
    mixed_grad = wide_ref[...] + router_back
    middle = middle_ref[...]
    norm_grad, second_gain_rows = rms_back(middle, inverse_rms(middle), gains_ref[1:2, :], mixed_grad)
    second_gain_grad = jnp.sum(second_gain_rows, axis=0, keepdims=True)
    middle_grad = cot_ref[...] + norm_grad
    middle_grad_ref[...] = middle_grad
    middle_low = middle_grad.astype(BF16)
    attended_grad = dot_nn(middle_low, w_ref[:, edge:outer]).astype(BF16)
    scale = (NOPE + ROPE) ** (-0.5)
    key_low = key_ref[...]
    key_odd = pltpu.roll(key_low.astype(F32), ROPE, 1).astype(BF16)
    latent = latent_ref[...]
    latent_part = jnp.zeros((tokens, LATENT), F32)
    key_even_grad = jnp.zeros((tokens, LANES), F32)
    key_odd_grad = jnp.zeros((tokens, LANES), F32)
    rope_grads = []
    grads4 = scr_ref.reshape(owners, shard, scr_ref.shape[1])
    for head in range(heads):
        pair = nope + head // 2 * LANES
        expanded = expanded_ref[:, head * 2 * NOPE : (head + 1) * 2 * NOPE]
        probs = probs_ref[head]
        head_grad = attended_grad[:, head * VDIM : (head + 1) * VDIM]
        value_grad = dot_tn(probs.astype(BF16), head_grad)
        probs_att = dot_nt(head_grad, expanded[:, NOPE:])
        scores = probs * (probs_att - jnp.sum(probs * probs_att, axis=-1, keepdims=True))
        raw_low = (scores * scale).astype(BF16)
        low_ref[:, head * NOPE : (head + 1) * NOPE] = dot_nn(raw_low, expanded[:, :NOPE]).astype(BF16)
        turn_grad = dot_nn(raw_low, key_odd if head % 2 else key_low)
        if head % 2:
            rope_grads[-1] = rope_grads[-1] + turn_grad
            key_odd_grad += dot_tn(raw_low, query_ref[:, pair : pair + LANES])
        else:
            rope_grads.append(turn_grad)
            key_even_grad += dot_tn(raw_low, query_ref[:, pair : pair + LANES])
        key_grad = dot_tn(raw_low, query_ref[:, head * NOPE : (head + 1) * NOPE])
        expanded_low = jnp.concatenate([key_grad, value_grad], axis=1).astype(BF16)
        up = w_ref[:, outer : outer + 2 * NOPE].reshape(owners, heads, short, 2 * NOPE)[:, head]
        up = up.reshape(LATENT, 2 * NOPE)
        latent_part += dot_nt(expanded_low, up)
        grads4[:, head * short : (head + 1) * short, outer : outer + 2 * NOPE] = (
            dot_tn(latent, expanded_low).astype(BF16).reshape(owners, short, 2 * NOPE)
        )
    rope_grad = jnp.concatenate(rope_grads, axis=1)
    low_ref[:, nope:queries] = rotated(rope_grad, cos_ref[...], -sin_ref[...]).astype(BF16)
    compressed = compressed_ref[...]
    latent_grad, latent_gain_rows = rms_back(
        compressed, inverse_rms(compressed), latent_gain_ref[2:3, :], latent_part
    )
    latent_gain_grad = jnp.sum(latent_gain_rows, axis=0, keepdims=True)
    low_ref[:, queries : queries + LATENT] = latent_grad.astype(BF16)
    lane = lax.broadcasted_iota(jnp.int32, (tokens, LANES), 1)
    key_grad = jnp.where(lane < ROPE, key_even_grad + pltpu.roll(key_odd_grad, ROPE, 1), 0.0)
    key_grad = rotated(key_grad, cos_ref[:, :LANES], -sin_ref[:, :LANES])
    low_ref[:, queries + LATENT : edge] = jnp.where(lane < ROPE, key_grad, 0.0).astype(BF16)
    low = low_ref[...]
    for step, out_ref in enumerate((own_ref, send1_ref, send2_ref, send3_ref)):
        place = block_at(me, step, count, piece)
        part = dot_nt(low, w_ref[place, :edge])
        wide_ref[:, place] = part
        out_ref[...] = part.astype(out_ref.dtype)
    stream = stream_ref[...].astype(F32)
    first_gain_grad = jnp.sum(wide_ref[...] * (stream * inverse_rms(stream)), axis=0, keepdims=True)
    late = dot_tn(normed_ref[...], low[:, queries:])
    sub = lax.broadcasted_iota(jnp.int32, (LANES, width), 0)
    gain_columns = (
        jnp.where(sub == ROPE, first_gain_grad, 0.0)
        + jnp.where(sub == ROPE + 1, second_gain_grad * (1.0 / count), 0.0)
    ).T
    key_columns = (late[:, LATENT:] + gain_columns).reshape(owners, shard, LANES)
    sub = lax.broadcasted_iota(jnp.int32, (LANES, LATENT), 0)
    latent_columns = jnp.where(sub == ROPE + 2, latent_gain_grad, 0.0).T.reshape(owners, short, LANES)
    grads4[:, :, queries : queries + LATENT] = (
        late[:, :LATENT].astype(BF16).reshape(owners, shard, LATENT)
    )
    grads4[:, :, queries + LATENT : edge] = key_columns.astype(BF16)
    grads4[:, :short, queries + LATENT : edge] = (key_columns[:, :short] + latent_columns).astype(BF16)
    scr_ref[:, edge:outer] = dot_tn(middle_low, attended_ref[...]).astype(BF16)
    scr_ref[:, :queries] = dot_tn(normed_ref[...], low[:, :queries]).astype(BF16)
    router_grad = dot_tn(mixed_ref[...], logits_low)
    scr_ref[:, outer + 2 * NOPE :] = router_grad[:, ROPE:].astype(BF16)
    halves = scr_ref.reshape(owners // 2, 2, shard, scr_ref.shape[1])
    core = core_ref[0]
    first = pltpu.make_async_copy(halves.at[:, 1 - core], pass_ref, sems.at[0])
    second = pltpu.make_async_copy(halves.at[:, core], keep_ref, sems.at[1])
    first.start()
    second.start()
    first.wait()
    second.wait()


def pair_kernel(at_ref, keep_ref, got_ref, along_z_ref, *along_x_refs):
    side = len(along_x_refs)
    cut = along_x_refs[0].shape[2]

    def part(index, columns):
        return (keep_ref[index, :, columns].astype(F32) + got_ref[index, :, columns].astype(F32)).astype(BF16)

    for z in range(side):
        for x in range(side):
            along_z_ref[z, x] = part(x * side + z, slice(cut, None))
    for step, out_ref in enumerate(along_x_refs):
        peer = lax.rem(at_ref[0] + step, side)
        for other in range(side):
            out_ref[other] = part(peer * side + other, slice(0, cut))


def cross_kernel(group, at_ref, *refs):
    parts, out_refs = refs[:-4], refs[-4:]
    for step, out_ref in enumerate(out_refs):
        peer = lax.rem(at_ref[1 - group] + step, len(out_refs))
        if len(parts) == 1:
            rows = [parts[0][source, peer] for source in range(parts[0].shape[0])]
        else:
            rows = [r_ref[peer] for r_ref in parts]
        total = rows[0].astype(F32)
        for row in rows[1:]:
            total = total + row.astype(F32)
        out_ref[...] = total.astype(out_ref.dtype)


def unpack_kernel(*refs):
    query_ref, late_ref, output_ref, up_ref, router_ref, total_ref = refs[-6:]
    heads = up_ref.shape[1] // (2 * NOPE)
    short = up_ref.shape[0]
    nope = heads * NOPE
    queries = nope + heads * ROPE
    edge = queries + LATENT + LANES
    outer = edge + heads * VDIM
    start = 0
    for group in range(2):
        parts = refs[4 * group : 4 * group + 4]
        width = parts[0].shape[1]
        total = parts[0][...]
        for r_ref in parts[1:]:
            total = total + r_ref[...].astype(F32)
        total_ref[:, start : start + width] = total
        start += width
    total = total_ref[...]
    for head in range(heads):
        start = head * (NOPE + ROPE)
        query_ref[:, start : start + NOPE] = total[:, head * NOPE : (head + 1) * NOPE]
        query_ref[:, start + NOPE : start + NOPE + ROPE] = total[
            :, nope + head * ROPE : nope + (head + 1) * ROPE
        ]
        up_ref[:, head * 2 * NOPE : (head + 1) * 2 * NOPE] = total[
            head * short : (head + 1) * short, outer : outer + 2 * NOPE
        ]
    late_ref[...] = total[:, queries:edge]
    output_ref[...] = total[:, edge:outer]
    router_ref[...] = total[:, outer + 2 * NOPE :]


def late_kernel(own_ref, r1_ref, r2_ref, r3_ref, down_ref, gains_ref):
    total = own_ref[...] + r1_ref[...] + r2_ref[...] + r3_ref[...]
    down_ref[...] = total[:, : down_ref.shape[1]]
    columns = total[:, LATENT:]
    columns = jnp.concatenate([columns, jnp.zeros(columns.shape, F32)], axis=0)
    gains_ref[...] = columns.T[ROPE : ROPE + 8, :]


def stream_kernel(me_ref, middle_grad_ref, stream_ref, gains_ref, a0_ref, a1_ref, a2_ref, a3_ref, out_ref, wide_ref):
    piece = a0_ref.shape[1]
    count = stream_ref.shape[1] // piece
    for step, a_ref in enumerate((a0_ref, a1_ref, a2_ref, a3_ref)):
        wide_ref[:, block_at(me_ref[0], step, count, piece)] = a_ref[...].astype(F32)
    stream = stream_ref[...].astype(F32)
    norm_grad, _ = rms_back(stream, inverse_rms(stream), gains_ref[0:1, :], wide_ref[...])
    out_ref[...] = middle_grad_ref[...] + norm_grad


def routed_kernel(t0_ref, t1_ref, o_ref, own_ref, r1_ref, r2_ref, r3_ref, out_ref):
    owners, _, capacity, piece = o_ref.shape
    rows = owners * capacity
    total = own_ref[...]
    for r_ref in (r1_ref, r2_ref, r3_ref):
        total = total + r_ref[...].astype(F32)
    for index, t_ref in ((0, t0_ref), (1, t1_ref)):
        total = total + dot_nn(t_ref[...], o_ref[:, index].reshape(rows, piece))
    out_ref[...] = total.astype(BF16)


def result_kernel(me_ref, middle_ref, a0_ref, a1_ref, a2_ref, a3_ref, out_ref):
    piece = a0_ref.shape[1]
    count = middle_ref.shape[1] // piece
    for step, a_ref in enumerate((a0_ref, a1_ref, a2_ref, a3_ref)):
        place = block_at(me_ref[0], step, count, piece)
        out_ref[:, place] = middle_ref[:, place] + a_ref[...].astype(F32)


def shift(array, step):
    size = lax.axis_size("tensor")
    return lax.ppermute(array, "tensor", [(i, (i + step) % size) for i in range(size)])


def send_blocks(sends):
    return [shift(array, step + 1) for step, array in enumerate(sends)]


def share_small(low):
    size = lax.axis_size("tensor")
    return [low] + [shift(low, size - step) for step in range(1, size)]


def ring_first(rows):
    return shift(rows, 1), shift(rows, lax.axis_size("tensor") - 1)


def ring_second(rows, before, after):
    half = rows.shape[0] // 2
    across = [shift(before[:half], 1), shift(after[half:], lax.axis_size("tensor") - 1)]
    return [rows, after, jnp.concatenate(across, axis=0), before]


def after(array, *others):
    return lax.optimization_barrier((array, *others))[0]


def exchange(rows):
    shape = rows.shape
    return lax.all_to_all(
        rows.reshape(shape[0], -1, shape[-1]), "expert", split_axis=0, concat_axis=0, tiled=True
    ).reshape(shape)


def per_device(
    stream,
    segment_ids,
    expert_ids,
    first_gain,
    query_proj,
    latent_down,
    latent_gain,
    latent_up,
    output_proj,
    second_gain,
    router_proj,
    shared_gate,
    shared_up,
    shared_down,
    expert_gate,
    expert_up,
    expert_down,
    cotangent,
):
    tokens, width = stream.shape
    owners = lax.axis_size("expert")
    tensors = lax.axis_size("tensor")
    shard = query_proj.shape[0]
    heads = query_proj.shape[1] // (NOPE + ROPE)
    short = latent_up.shape[0]
    experts = router_proj.shape[1]
    hidden_columns = shared_gate.shape[1]
    local, _, expert_hidden = expert_gate.shape
    capacity = tokens * TOPK * 4 // (3 * experts)
    rows = owners * capacity
    piece = width // tensors
    nope = heads * NOPE
    queries = nope + heads * ROPE
    edge = queries + LATENT + LANES
    outer = edge + heads * VDIM
    me = lax.axis_index("tensor").astype(jnp.int32).reshape(1)
    base = (lax.axis_index("expert") * local).astype(jnp.int32).reshape(1)
    core = lax.rem(lax.axis_index("expert"), 2).astype(jnp.int32).reshape(1)
    smem = {0: pltpu.SMEM}

    gains = jnp.concatenate(
        [
            first_gain[:, None],
            second_gain[:, None],
            jnp.pad(latent_gain, (0, shard - short))[:, None],
            jnp.zeros((shard, ROPE - 3), BF16),
        ],
        axis=1,
    )
    by_head = query_proj.reshape(shard, heads, NOPE + ROPE)
    pack_one = jnp.concatenate(
        [
            by_head[:, :, :NOPE].reshape(shard, nope),
            by_head[:, :, NOPE:].reshape(shard, heads * ROPE),
            latent_down,
            router_proj,
            output_proj.T,
            latent_up.reshape(short, heads, 2 * NOPE).transpose(1, 0, 2).reshape(shard, 2 * NOPE),
            gains,
        ],
        axis=1,
    )
    pack_two = jnp.concatenate([shared_gate, shared_up, shared_down.T], axis=1)
    one = lax.all_gather(pack_one, "expert", axis=0, tiled=True)
    two = lax.all_gather(pack_two, "expert", axis=0, tiled=True)

    position = jnp.arange(tokens).astype(F32)
    exponent = jnp.arange(ROPE // 2).astype(F32) * (2.0 / ROPE)
    angles = position[:, None] * jnp.exp(-math.log(ROTARY_BASE) * exponent)[None, :]
    cosine = jnp.tile(jnp.cos(angles), (1, 2 * heads))
    sine = jnp.sin(angles)
    sine = jnp.tile(jnp.concatenate([-sine, sine], axis=1), (1, heads))

    t0, t1, cot_low, cot_out = run(
        routing_kernel,
        [
            ((tokens, rows), BF16),
            ((tokens, rows), BF16),
            ((tokens, width), BF16),
            ((owners, local, capacity, piece), BF16),
        ],
        [me, expert_ids.T, cotangent],
        2 * local * tokens * rows * (piece + experts),
        places=smem,
        name="routing",
    )

    cot_own = exchange(cot_out)
    cot_before, cot_after = ring_first(cot_own)
    (
        own,
        send1,
        send2,
        send3,
        normed,
        query,
        expanded,
        key,
        latent,
        compressed,
        probs,
        attended,
        gain_rows,
        latent_gain_rows,
    ) = run(
        attend_kernel,
        [
            ((tokens, piece), F32),
            ((tokens, piece), BF16),
            ((tokens, piece), BF16),
            ((tokens, piece), BF16),
            ((tokens, width), BF16),
            ((tokens, queries), BF16),
            ((tokens, heads * 2 * NOPE), BF16),
            ((tokens, LANES), BF16),
            ((tokens, LATENT), BF16),
            ((tokens, LATENT), F32),
            ((heads, tokens, tokens), F32),
            ((tokens, heads * VDIM), BF16),
            ((8, width), F32),
            ((8, LATENT), F32),
        ],
        [after(me, cot_own), stream, one, segment_ids, segment_ids.T, cosine, sine],
        2 * tokens * width * outer,
        places=smem,
        name="attend",
    )
    got = send_blocks([send1, send2, send3])
    attention = (own + got[0].astype(F32) + got[1].astype(F32) + got[2].astype(F32)).astype(BF16)
    attention = after(attention, cot_before, cot_after)
    middle, mixed, x_out = run(
        dispatch_kernel,
        [
            ((tokens, width), F32),
            ((tokens, width), BF16),
            ((owners, capacity, width + piece), BF16),
        ],
        [me, stream, *share_small(attention), gain_rows, t0, t1],
        2 * tokens * rows * (width + piece),
        places=smem,
        name="dispatch",
    )
    x_in = exchange(x_out)
    cots = ring_second(cot_own, cot_before, cot_after)
    x1s = x_in[:, :, width:]
    x1_before, x1_after = ring_first(x1s)
    x1s = [x_in] + ring_second(x1s, x1_before, x1_after)[1:]
    router_block = one[:, queries + LATENT : edge]
    (
        shared_own,
        shared1,
        shared2,
        shared3,
        shared_back,
        router_probs,
        shared_grads,
    ) = run(
        shared_kernel,
        [
            ((tokens, piece), F32),
            ((tokens, piece), BF16),
            ((tokens, piece), BF16),
            ((tokens, piece), BF16),
            ((tokens, width), F32),
            ((tokens, LANES), F32),
            ((width, 3 * hidden_columns), BF16),
        ],
        [me, mixed, cot_low, two, router_block],
        18 * tokens * width * hidden_columns,
        places=smem,
        name="shared",
    )
    base = after(base, shared_back)

    gate_t = expert_gate.transpose(0, 2, 1)
    up_t = expert_up.transpose(0, 2, 1)
    chunk = owners // 2
    back0, c0, hg0, gr0, ur0 = expert_back(
        False, me, base, [x_in], cots, gate_t, up_t, expert_down, one, edge // LANES - 1, chunk // 2
    )
    back0 = exchange(back0)
    back1, c1, hg1, gr1, ur1, x1 = expert_back(
        True, me, after(base, hg0), x1s, cots, gate_t, up_t, expert_down, one, edge // LANES - 1, chunk // 2
    )
    back1 = exchange(after(back1, back0))
    gr0 = after(gr0, back0)
    gate_grad, up_grad, down_grad = expert_grads(
        (x_in, c0, hg0, gr0, ur0), (x1, c1, hg1, gr1, ur1), tensors
    )
    out0 = expert_out(0, hg0, expert_down, owners, tensors, chunk)
    out1 = expert_out(1, after(hg1, out0), expert_down, owners, tensors, chunk)
    out_rows = [
        lax.psum_scatter(out, "tensor", scatter_dimension=0, tiled=True).reshape(owners, 1, capacity, piece)
        for out in (out0, out1)
    ]

    first_sum, first_probs = run(
        combine_first_kernel,
        [((tokens, width), F32), ((tokens, LANES), F32)],
        [t0, back0, shared_back],
        2 * tokens * rows * width,
        name="combine_first",
    )
    own, probs_own, send1, send2, send3 = run(
        combine_kernel,
        [
            ((tokens, piece), F32),
            ((tokens, LANES), F32),
            ((tokens, piece + LANES), BF16),
            ((tokens, piece + LANES), BF16),
            ((tokens, piece + LANES), BF16),
        ],
        [after(me, out1, gate_grad), t1, back1, first_sum, first_probs],
        2 * tokens * rows * width,
        places=smem,
        name="combine",
    )
    got = send_blocks([send1, send2, send3])
    out_rows = exchange(after(jnp.concatenate(out_rows, axis=1), own))
    shared_sum = lax.psum_scatter(
        after(shared_grads, own), "expert", scatter_dimension=0, tiled=True
    )
    mixed_sum = (
        own
        + got[0][:, :piece].astype(F32)
        + got[1][:, :piece].astype(F32)
        + got[2][:, :piece].astype(F32)
    ).astype(BF16)
    keep, passed, middle_grad, own, send1, send2, send3 = run(
        attend_back_kernel,
        [
            ((owners // 2, shard, outer + 2 * NOPE + experts), BF16),
            ((owners // 2, shard, outer + 2 * NOPE + experts), BF16),
            ((tokens, width), F32),
            ((tokens, piece), F32),
            ((tokens, piece), BF16),
            ((tokens, piece), BF16),
            ((tokens, piece), BF16),
        ],
        [
            me,
            core,
            stream,
            cotangent,
            middle,
            *share_small(mixed_sum),
            *got,
            probs_own,
            router_probs,
            one,
            router_block,
            mixed,
            normed,
            query,
            expanded,
            key,
            latent,
            compressed,
            probs,
            attended,
            gain_rows,
            latent_gain_rows,
            cosine,
            sine,
        ],
        2 * tokens * width * (3 * edge + 2 * outer),
        scratch=[
            pltpu.VMEM((width, outer + 2 * NOPE + experts), BF16),
            pltpu.VMEM((tokens, edge), BF16),
            pltpu.VMEM((tokens, width), F32),
            pltpu.SemaphoreType.DMA((2,)),
        ],
        places={0: pltpu.SMEM, 1: pltpu.SMEM},
        out_places={0: pl.ANY, 1: pl.ANY},
        name="attend_back",
    )
    paired = lax.ppermute(after(passed, out_rows), "expert", [(i, i ^ 1) for i in range(owners)])
    side = 4
    chip = lax.axis_index("expert") // 2
    at = jnp.stack([chip // side, lax.rem(chip, side)]).astype(jnp.int32)
    columns = outer + 2 * NOPE + experts
    cut = columns // 2 // LANES * LANES + LANES

    def along(group, array, step):
        def target(i):
            x, z, core = i // (2 * side), i // 2 % side, i % 2
            if group == 0:
                x = (x + step) % side
            else:
                z = (z + step) % side
            return (x * side + z) * 2 + core

        return lax.ppermute(array, "expert", [(i, target(i)) for i in range(owners)])

    widths = [cut, columns - cut]
    along_z, *along_x = run(
        pair_kernel,
        [((side, side, shard, widths[1]), BF16)] + [((side, shard, cut), BF16)] * side,
        [at, keep, paired],
        0,
        places=smem,
        name="pair",
    )
    came_z = lax.all_to_all(
        along_z.reshape(side, side * shard, widths[1]),
        "expert",
        split_axis=0,
        concat_axis=0,
        tiled=True,
        axis_index_groups=[[(x * side + z) * 2 + c for z in range(side)] for x in range(side) for c in range(2)],
    ).reshape(along_z.shape)
    came_x = [along_x[0]] + [along(0, along_x[step], step) for step in range(1, side)]
    parts = []
    for group, came in enumerate((came_x, [came_z])):
        crossed = run(
            functools.partial(cross_kernel, group),
            [((shard, widths[group]), F32)] + [((shard, widths[group]), BF16)] * (side - 1),
            [at, *came],
            0,
            places=smem,
            name="cross",
        )
        parts += [crossed[0]] + [along(1 - group, crossed[step], step) for step in range(1, side)]
    got = send_blocks([send1, send2, send3])
    first_sum = (own + got[0].astype(F32) + got[1].astype(F32) + got[2].astype(F32)).astype(BF16)
    (stream_grad,) = run(
        stream_kernel,
        [((tokens, width), F32)],
        [me, middle_grad, stream, gain_rows, *share_small(first_sum)],
        0,
        scratch=[pltpu.VMEM((tokens, width), F32)],
        places=smem,
        name="stream",
    )

    got = send_blocks([shared1, shared2, shared3])
    (branch,) = run(
        routed_kernel,
        [((tokens, piece), BF16)],
        [t0, t1, out_rows, shared_own, *got],
        4 * tokens * rows * piece,
        name="routed",
    )
    (result,) = run(
        result_kernel,
        [((tokens, width), F32)],
        [me, middle, *share_small(branch)],
        0,
        places=smem,
        name="result",
    )

    shared_sum = shared_sum.astype(F32)
    gate_sum = shared_sum[:, :hidden_columns]
    up_sum = shared_sum[:, hidden_columns : 2 * hidden_columns]
    down_sum = shared_sum[:, 2 * hidden_columns :]
    parts[0] = after(parts[0], stream_grad, result, gate_sum, up_sum, down_sum)
    query_grad, late, output_grad, latent_up_grad, router_grad = run(
        unpack_kernel,
        [
            (query_proj.shape, F32),
            ((shard, edge - queries), F32),
            ((shard, heads * VDIM), F32),
            (latent_up.shape, F32),
            (router_proj.shape, F32),
        ],
        parts,
        0,
        scratch=[pltpu.VMEM((shard, columns), F32)],
        name="unpack",
    )
    latent_down_grad, gain_grads = run(
        late_kernel,
        [(latent_down.shape, F32), ((8, LANES), F32)],
        [late, *(shift(late, step) for step in range(1, tensors))],
        0,
        name="late",
    )
    return (
        result,
        stream_grad,
        gain_grads[0, :shard],
        query_grad,
        latent_down_grad,
        gain_grads[2, :short],
        latent_up_grad,
        output_grad.T,
        gain_grads[1, :shard],
        router_grad,
        gate_sum,
        up_sum,
        down_sum.T,
        gate_grad.transpose(0, 2, 1),
        up_grad.transpose(0, 2, 1),
        down_grad,
    )


def solution(mesh):
    placed = (
        P("expert", None),
        P("expert", None),
        P("expert", None),
        P("expert"),
        P("expert", "tensor"),
        P("expert", None),
        P("expert"),
        P("expert", "tensor"),
        P("tensor", "expert"),
        P("expert"),
        P("expert", None),
        P("expert", "tensor"),
        P("expert", "tensor"),
        P("tensor", "expert"),
        P("expert", None, "tensor"),
        P("expert", None, "tensor"),
        P("expert", "tensor", None),
        P("expert", None),
    )
    return jax.shard_map(
        per_device,
        mesh=mesh,
        in_specs=placed,
        out_specs=(
            P("expert", None),
            P("expert", None),
            P("expert"),
            P("expert", "tensor"),
            P("expert", None),
            P("expert"),
            P("expert", "tensor"),
            P("tensor", "expert"),
            P("expert"),
            P("expert", None),
            P("expert", "tensor"),
            P("expert", "tensor"),
            P("tensor", "expert"),
            P("expert", None, "tensor"),
            P("expert", None, "tensor"),
            P("expert", "tensor", None),
        ),
        check_vma=False,
    )
```

```python
import functools
import math

import jax
import jax.numpy as jnp
from jax import lax
from jax.experimental import pallas as pl
from jax.experimental.pallas import tpu as pltpu
from jax.sharding import PartitionSpec as P

NOPE = 128
ROPE = 64
VDIM = 128
LATENT = 512
TOPK = 6
EPSILON = 1e-06
ROTARY_BASE = 10000.0

BF16 = jnp.bfloat16
F32 = jnp.float32
VMEM_BYTES = 60 * 1024 * 1024
LANES = 128
COST_SCALE = 10


def dot_nn(left, right):
    return lax.dot_general(left, right, (((1,), (0,)), ((), ())), preferred_element_type=F32)


def dot_nt(left, right):
    return lax.dot_general(left, right, (((1,), (1,)), ((), ())), preferred_element_type=F32)


def dot_tn(left, right):
    return lax.dot_general(left, right, (((0,), (0,)), ((), ())), preferred_element_type=F32)


def silu_parts(pre_values):
    sigmoid_value = 1.0 / (1.0 + jnp.exp(-pre_values))
    return (pre_values * sigmoid_value, sigmoid_value * (1.0 + pre_values * (1.0 - sigmoid_value)))


def inverse_rms(values):
    return lax.rsqrt(jnp.mean(values * values, axis=-1, keepdims=True) + EPSILON)


def rms_back(values, scale, gain, grad):
    normed = values * scale
    weighted = grad * gain
    return (
        scale * (weighted - normed * jnp.mean(weighted * normed, axis=-1, keepdims=True)),
        grad * normed,
    )


def turned(values):
    width = values.shape[1]
    lane = lax.broadcasted_iota(jnp.int32, values.shape, 1) % ROPE
    half = ROPE // 2
    return jnp.where(
        lane < half, pltpu.roll(values, width - half, 1), pltpu.roll(values, half, 1)
    )


def rotated(values, cosine, sine):
    return values * cosine + turned(values) * sine


def block_at(me, step, count, width):
    return pl.ds(pl.multiple_of(lax.rem(me + step, count) * width, width), width)


def run(kernel, outs, args, flops, scratch=(), name=None, places=None, aliases=None, out_places=None):
    places = places or {}
    out_places = out_places or {}
    in_specs = [pl.BlockSpec(memory_space=places.get(i, pltpu.VMEM)) for i in range(len(args))]
    out_specs = [pl.BlockSpec(memory_space=out_places.get(i, pltpu.VMEM)) for i in range(len(outs))]
    moved = sum(a.size * a.dtype.itemsize for a in args) + sum(
        math.prod(shape) * jnp.dtype(dtype).itemsize for shape, dtype in outs
    )
    return pl.pallas_call(
        kernel,
        in_specs=in_specs,
        out_specs=out_specs,
        out_shape=[jax.ShapeDtypeStruct(shape, dtype) for shape, dtype in outs],
        scratch_shapes=list(scratch),
        input_output_aliases=aliases or {},
        compiler_params=pltpu.CompilerParams(vmem_limit_bytes=VMEM_BYTES),
        cost_estimate=pl.CostEstimate(
            flops=flops // COST_SCALE, bytes_accessed=moved // COST_SCALE, transcendentals=0
        ),
        name=name,
    )(*args)


def routing_kernel(me_ref, ids_ref, cot_ref, t0_ref, t1_ref, s0_ref, s1_ref, low_ref, out_ref):
    choices, tokens = ids_ref.shape
    owners, local, capacity, piece = out_ref.shape
    experts = owners * local
    rows = owners * capacity
    expert = lax.broadcasted_iota(jnp.int32, (experts, tokens), 0)
    chosen = jnp.zeros((experts, tokens), F32)
    for choice in range(choices):
        chosen += jnp.where(ids_ref[choice : choice + 1, :] == expert, 1.0, 0.0)
    before = jnp.where(
        lax.broadcasted_iota(jnp.int32, (tokens, tokens), 0)
        < lax.broadcasted_iota(jnp.int32, (tokens, tokens), 1),
        1.0,
        0.0,
    ).astype(BF16)
    place = dot_nn(chosen.astype(BF16), before)
    place = jnp.where(chosen > 0.5, place, -1.0).astype(BF16)
    low = cot_ref[...].astype(BF16)
    low_ref[...] = low
    mine = cot_ref[:, block_at(me_ref[0], 0, cot_ref.shape[1] // piece, piece)].astype(BF16)
    slot = (lax.broadcasted_iota(jnp.int32, (tokens, rows), 1) % capacity).astype(F32)
    for index, (t_ref, s_ref) in enumerate(((t0_ref, s0_ref), (t1_ref, s1_ref))):
        spread = jnp.where(
            lax.broadcasted_iota(jnp.int32, (experts, rows), 0)
            == lax.broadcasted_iota(jnp.int32, (experts, rows), 1) // capacity * local + index,
            1.0,
            0.0,
        ).astype(BF16)
        wanted = dot_tn(place, spread)
        matrix = jnp.where(wanted == slot, 1.0, 0.0).astype(BF16)
        t_ref[...] = matrix
        by_slot = matrix.T
        s_ref[...] = by_slot
        out_ref[:, index] = dot_nn(by_slot, mine).astype(BF16).reshape(owners, capacity, piece)


def attend_kernel(
    me_ref,
    stream_ref,
    w_ref,
    seg_row_ref,
    seg_col_ref,
    cos_ref,
    sin_ref,
    own_ref,
    send1_ref,
    send2_ref,
    send3_ref,
    normed_ref,
    query_ref,
    expanded_ref,
    key_ref,
    latent_ref,
    compressed_ref,
    probs_ref,
    attended_ref,
    gains_ref,
    latent_gain_ref,
):
    heads, tokens, _ = probs_ref.shape
    width = stream_ref.shape[1]
    piece = own_ref.shape[1]
    nope = heads * NOPE
    queries = nope + heads * ROPE
    edge = queries + LATENT + LANES
    outer = edge + heads * VDIM
    owners = 32
    columns = jnp.concatenate(
        [w_ref[:, outer + 2 * NOPE :].astype(F32), jnp.zeros((width, ROPE), F32)], axis=1
    )
    gains = columns.T[:8, :]
    gains_ref[...] = gains
    shard = width // owners
    short = LATENT // owners
    latent_gain = (
        columns.reshape(owners, shard, LANES)[:, :short, :].reshape(LATENT, LANES).T[:8, :]
    )
    latent_gain_ref[...] = latent_gain
    stream = stream_ref[...].astype(F32)
    normed = (stream * inverse_rms(stream) * gains[0:1, :]).astype(BF16)
    normed_ref[...] = normed
    projected = dot_nn(normed, w_ref[:, :edge])
    query_ref[:, :nope] = projected[:, :nope].astype(BF16)
    query_ref[:, nope:] = rotated(projected[:, nope:queries], cos_ref[...], sin_ref[...]).astype(BF16)
    compressed = projected[:, queries : queries + LATENT]
    compressed_ref[...] = compressed
    latent = (compressed * inverse_rms(compressed) * latent_gain[2:3, :]).astype(BF16)
    latent_ref[...] = latent
    raw_key = projected[:, queries + LATENT : edge]
    key = rotated(raw_key, cos_ref[:, :LANES], sin_ref[:, :LANES])
    lane = lax.broadcasted_iota(jnp.int32, key.shape, 1)
    key = jnp.where(lane < ROPE, key, 0.0)
    key_low = key.astype(BF16)
    key_odd = pltpu.roll(key, ROPE, 1).astype(BF16)
    key_ref[...] = key_low
    row = lax.broadcasted_iota(jnp.int32, (tokens, tokens), 0)
    column = lax.broadcasted_iota(jnp.int32, (tokens, tokens), 1)
    allowed = (seg_col_ref[...] == seg_row_ref[...]) & (column <= row)
    scale = (NOPE + ROPE) ** (-0.5)
    for head in range(heads):
        block = slice(head * 2 * NOPE, (head + 1) * 2 * NOPE)
        up = w_ref[:, outer : outer + 2 * NOPE].reshape(owners, heads, short, 2 * NOPE)[:, head]
        up = up.reshape(LATENT, 2 * NOPE)
        expanded = dot_nn(latent, up).astype(BF16)
        expanded_ref[:, block] = expanded
        pair = nope + head // 2 * LANES
        raw = dot_nt(query_ref[:, head * NOPE : (head + 1) * NOPE], expanded[:, :NOPE]) + dot_nt(
            query_ref[:, pair : pair + LANES], key_odd if head % 2 else key_low
        )
        scores = jnp.where(allowed, raw * scale, -1e30)
        weight = jnp.exp(scores - jnp.max(scores, axis=-1, keepdims=True))
        probs = weight / jnp.sum(weight, axis=-1, keepdims=True)
        probs_ref[head] = probs
        attended_ref[:, head * VDIM : (head + 1) * VDIM] = dot_nn(
            probs.astype(BF16), expanded[:, NOPE:]
        ).astype(BF16)
    attended = attended_ref[...]
    for step, out_ref in enumerate((own_ref, send1_ref, send2_ref, send3_ref)):
        part = dot_nt(attended, w_ref[block_at(me_ref[0], step, width // piece, piece), edge:outer])
        out_ref[...] = part.astype(out_ref.dtype)


def dispatch_kernel(
    me_ref, stream_ref, a0_ref, a1_ref, a2_ref, a3_ref, gains_ref, s0_ref, s1_ref, middle_ref, mixed_ref, out_ref
):
    piece = a0_ref.shape[1]
    width = stream_ref.shape[1]
    count = width // piece
    owners, capacity, _ = out_ref.shape
    for step, a_ref in enumerate((a0_ref, a1_ref, a2_ref, a3_ref)):
        place = block_at(me_ref[0], step, count, piece)
        middle_ref[:, place] = stream_ref[:, place].astype(F32) + a_ref[...].astype(F32)
    middle = middle_ref[...]
    mixed = (middle * inverse_rms(middle) * gains_ref[1:2, :]).astype(BF16)
    mixed_ref[...] = mixed
    mine = mixed_ref[:, block_at(me_ref[0], 0, count, piece)]
    out_ref[:, :, width:] = dot_nn(s1_ref[...], mine).astype(BF16).reshape(owners, capacity, piece)
    out_ref[:, :, :width] = dot_nn(s0_ref[...], mixed).astype(BF16).reshape(owners, capacity, width)


def shared_kernel(
    me_ref,
    mixed_ref,
    cot_ref,
    w_ref,
    router_ref,
    own_ref,
    send1_ref,
    send2_ref,
    send3_ref,
    back_ref,
    probs_ref,
    grads_ref,
):
    width = mixed_ref.shape[1]
    piece = own_ref.shape[1]
    hidden_columns = w_ref.shape[1] // 3
    mixed = mixed_ref[...]
    cot = cot_ref[...]
    pre = dot_nn(mixed, w_ref[:, : 2 * hidden_columns])
    gate_pre, up_pre = pre[:, :hidden_columns], pre[:, hidden_columns:]
    act, slope = silu_parts(gate_pre)
    hidden = (act * up_pre).astype(BF16)
    hidden_grad = dot_nn(cot, w_ref[:, 2 * hidden_columns :])
    pair = jnp.concatenate([hidden_grad * up_pre * slope, hidden_grad * act], axis=1).astype(BF16)
    grads_ref[:, : 2 * hidden_columns] = dot_tn(mixed, pair).astype(BF16)
    grads_ref[:, 2 * hidden_columns :] = dot_tn(cot, hidden).astype(BF16)
    back_ref[...] = dot_nt(pair, w_ref[:, : 2 * hidden_columns])
    logits = dot_nn(mixed, router_ref[...])
    lane = lax.broadcasted_iota(jnp.int32, logits.shape, 1)
    logits = jnp.where(lane >= ROPE, logits, -1e30)
    weight = jnp.exp(logits - jnp.max(logits, axis=-1, keepdims=True))
    probs_ref[...] = weight / jnp.sum(weight, axis=-1, keepdims=True)
    for step, out_ref in enumerate((own_ref, send1_ref, send2_ref, send3_ref)):
        place = block_at(me_ref[0], step, width // piece, piece)
        part = dot_nt(hidden, w_ref[place, 2 * hidden_columns :])
        out_ref[...] = part.astype(out_ref.dtype)


def expert_back_kernel(split, *refs):
    if split:
        me_ref, base_ref, x0_ref, x1_ref, x2_ref, x3_ref = refs[:6]
        refs = refs[6:]
    else:
        me_ref, base_ref, x_ref = refs[:3]
        refs = refs[3:]
    c0_ref, c1_ref, c2_ref, c3_ref, wg_ref, wu_ref, wd_ref, router_ref = refs[:8]
    refs = refs[8:]
    if split:
        back_ref, c_ref, hg_ref, gr_ref, ur_ref, x_ref, wide_ref, down_ref, tall_ref = refs
    else:
        back_ref, c_ref, hg_ref, gr_ref, ur_ref, wide_ref, down_ref, tall_ref = refs
    sources, capacity, width = c_ref.shape
    rows = sources * capacity
    piece = c0_ref.shape[-1]
    count = width // piece
    hidden_columns = wd_ref.shape[1]
    padded = down_ref.shape[1]
    me = me_ref[0]

    @pl.when(pl.program_id(0) == 0)
    def _():
        rest = jnp.zeros((padded - hidden_columns, width), BF16)
        gate_up = jnp.concatenate([wg_ref[0], rest, wu_ref[0], rest], axis=0)
        tall_ref[...] = gate_up
        wide_ref[...] = gate_up.T
        down_ref[...] = jnp.concatenate([wd_ref[0], rest], axis=0).T

    for step, p_ref in enumerate((c0_ref, c1_ref, c2_ref, c3_ref)):
        c_ref[:, :, block_at(me, step, count, piece)] = p_ref[:, 0]
    if split:
        for step, p_ref in enumerate((x0_ref, x1_ref, x2_ref, x3_ref)):
            x_ref[:, :, block_at(me, step, count, piece)] = p_ref[...]
    x = x_ref[...].reshape(rows, width)
    expert = base_ref[0] + (1 if split else 0) + ROPE
    logits = dot_nn(x, router_ref[...])
    lane = lax.broadcasted_iota(jnp.int32, logits.shape, 1)
    logits = jnp.where(lane >= ROPE, logits, -1e30)
    weight = jnp.exp(logits - jnp.max(logits, axis=-1, keepdims=True))
    gate = jnp.sum(jnp.where(lane == expert, weight, 0.0), axis=-1, keepdims=True) / jnp.sum(
        weight, axis=-1, keepdims=True
    )
    pre = dot_nn(x, wide_ref[...])
    gate_pre, up_pre = pre[:, :padded], pre[:, padded:]
    hidden_cot = dot_nn(c_ref[...].reshape(rows, width), down_ref[...])
    act, slope = silu_parts(gate_pre)
    hidden = (act * up_pre).astype(BF16).astype(F32)
    gate_grad = jnp.sum(hidden * hidden_cot, axis=-1, keepdims=True)
    hidden_grad = gate * hidden_cot
    gate_rows = (hidden_grad * up_pre * slope).astype(BF16)
    up_rows = (hidden_grad * act).astype(BF16)
    hg_ref[...] = (gate * hidden).astype(BF16)[:, :hidden_columns]
    gr_ref[...] = gate_rows[:, :hidden_columns]
    ur_ref[...] = up_rows[:, :hidden_columns]
    high = gate_grad.astype(BF16).astype(F32)
    low = gate_grad - high
    beside = jnp.where(lane == 0, high, 0.0) + jnp.where(lane == 1, low, 0.0)
    back = dot_nn(jnp.concatenate([gate_rows, up_rows], axis=1), tall_ref[...])
    back_ref[:, :, :width] = back.astype(BF16).reshape(sources, capacity, width)
    back_ref[:, :, width:] = beside.astype(BF16).reshape(sources, capacity, LANES)


def expert_back(split, me, base, xs, cs, wg, wu, wd, router, router_at, chunk):
    owners, local, capacity, piece = cs[0].shape
    hidden, width = wg.shape[1:]
    local_index = 1 if split else 0
    rows = owners * capacity
    padded = -(-hidden // LANES) * LANES
    scalar = pl.BlockSpec(memory_space=pltpu.SMEM)
    row_spec = pl.BlockSpec((chunk * capacity, hidden), lambda c: (c, 0))
    row_shape = jax.ShapeDtypeStruct((rows, hidden), BF16)
    wide_spec = pl.BlockSpec((chunk, capacity, width), lambda c: (c, 0, 0))
    wide_shape = jax.ShapeDtypeStruct((owners, capacity, width), BF16)
    narrow_spec = pl.BlockSpec((chunk, capacity, piece), lambda c: (c, 0, 0))
    own_spec = pl.BlockSpec((chunk, capacity, piece), lambda c: (c, 0, width // piece))
    cot_spec = pl.BlockSpec((chunk, 1, capacity, piece), lambda c: (c, local_index, 0, 0))
    weight_spec = pl.BlockSpec((1, hidden, width), lambda c: (local_index, 0, 0))
    in_specs = [scalar, scalar]
    in_specs += [own_spec] + [narrow_spec] * 3 if split else [wide_spec]
    in_specs += [cot_spec] * 4 + [weight_spec] * 3 + [pl.BlockSpec((width, LANES), lambda c: (0, router_at))]
    out_specs = [pl.BlockSpec((chunk, capacity, width + LANES), lambda c: (c, 0, 0)), wide_spec]
    out_shape = [jax.ShapeDtypeStruct((owners, capacity, width + LANES), BF16), wide_shape]
    last_spec, last_shape = ([wide_spec], [wide_shape]) if split else ([], [])
    return pl.pallas_call(
        functools.partial(expert_back_kernel, split),
        grid=(owners // chunk,),
        in_specs=in_specs,
        out_specs=out_specs + [row_spec] * 3 + last_spec,
        out_shape=out_shape + [row_shape] * 3 + last_shape,
        scratch_shapes=[
            pltpu.VMEM((width, 2 * padded), BF16),
            pltpu.VMEM((width, padded), BF16),
            pltpu.VMEM((2 * padded, width), BF16),
        ],
        compiler_params=pltpu.CompilerParams(vmem_limit_bytes=VMEM_BYTES),
        cost_estimate=pl.CostEstimate(
            flops=100 * rows * hidden * width, bytes_accessed=24 * 1024 * 1024, transcendentals=0
        ),
        name="expert_back",
    )(me, base, *xs, *cs, wg, wu, wd, router)


def expert_out_kernel(hg_ref, wd_ref, out_ref):
    pieces, sources, capacity, piece = out_ref.shape
    out = dot_nn(hg_ref[...], wd_ref[0]).astype(BF16)
    for index in range(pieces):
        out_ref[index] = out[:, index * piece : (index + 1) * piece].reshape(sources, capacity, piece)


def expert_out(expert, hg, wd, owners, pieces, chunk):
    rows, hidden = hg.shape
    width = wd.shape[2]
    capacity = rows // owners
    piece = width // pieces
    return pl.pallas_call(
        expert_out_kernel,
        grid=(owners // chunk,),
        in_specs=[
            pl.BlockSpec((chunk * capacity, hidden), lambda c: (c, 0)),
            pl.BlockSpec((1, hidden, width), lambda c: (expert, 0, 0)),
        ],
        out_specs=pl.BlockSpec((pieces, chunk, capacity, piece), lambda c: (0, c, 0, 0)),
        out_shape=jax.ShapeDtypeStruct((pieces, owners, capacity, piece), BF16),
        compiler_params=pltpu.CompilerParams(vmem_limit_bytes=VMEM_BYTES),
        cost_estimate=pl.CostEstimate(
            flops=rows * hidden * width // 5, bytes_accessed=6 * 1024 * 102, transcendentals=0
        ),
        name="expert_out",
    )(hg, wd)


def expert_grads_kernel(
    x0_ref, c0_ref, hg0_ref, gr0_ref, ur0_ref, x1_ref, c1_ref, hg1_ref, gr1_ref, ur1_ref, dg_ref, du_ref, dd_ref
):
    owners, capacity, piece = x0_ref.shape
    rows = owners * capacity

    def step(x_ref, c_ref, hg_ref, gr_ref, ur_ref):
        x = x_ref[...].reshape(rows, piece)
        dg_ref[0] = dot_tn(gr_ref[...], x)
        du_ref[0] = dot_tn(ur_ref[...], x)
        dd_ref[0] = dot_tn(hg_ref[...], c_ref[...].reshape(rows, piece))

    pl.when(pl.program_id(0) == 0)(lambda: step(x0_ref, c0_ref, hg0_ref, gr0_ref, ur0_ref))
    pl.when(pl.program_id(0) == 1)(lambda: step(x1_ref, c1_ref, hg1_ref, gr1_ref, ur1_ref))


def expert_grads(first, second, pieces):
    owners, capacity, width = first[1].shape
    rows, hidden = first[2].shape
    piece = width // pieces
    row_spec = pl.BlockSpec((rows, hidden), lambda e, j: (0, 0))

    def specs(expert):
        stay = 0 if expert else pieces - 1
        wide = pl.BlockSpec(
            (owners, capacity, piece), lambda e, j: (0, 0, jnp.where(e == expert, j, stay))
        )
        return [wide, wide, row_spec, row_spec, row_spec]

    out_spec = pl.BlockSpec((1, hidden, piece), lambda e, j: (e, 0, j))
    out_shape = jax.ShapeDtypeStruct((2, hidden, width), F32)
    return pl.pallas_call(
        expert_grads_kernel,
        grid=(2, pieces),
        in_specs=specs(0) + specs(1),
        out_specs=[out_spec] * 3,
        out_shape=[out_shape] * 3,
        compiler_params=pltpu.CompilerParams(vmem_limit_bytes=VMEM_BYTES),
        cost_estimate=pl.CostEstimate(
            flops=rows * hidden * width, bytes_accessed=40 * 1024 * 102, transcendentals=0
        ),
        name="expert_grads",
    )(*first, *second)


def slot_probs(t_ref, b_ref, index, width):
    owners, capacity, _ = b_ref.shape
    rows = owners * capacity
    beside = b_ref[:, :, width:].reshape(rows, LANES).astype(F32)
    lane = lax.broadcasted_iota(jnp.int32, (rows, LANES), 1)
    expert = 2 * (lax.broadcasted_iota(jnp.int32, (rows, LANES), 0) // capacity) + index
    spread = jnp.where(lane == expert + ROPE, beside[:, 0:1], 0.0) + jnp.where(
        lane == expert, beside[:, 1:2], 0.0
    )
    return dot_nn(t_ref[...], spread.astype(BF16))


def combine_first_kernel(t_ref, b_ref, shared_ref, sum_ref, probs_ref):
    owners, capacity, _ = b_ref.shape
    width = shared_ref.shape[1]
    probs_ref[...] = slot_probs(t_ref, b_ref, 0, width)
    sum_ref[...] = shared_ref[...] + dot_nn(t_ref[...], b_ref[:, :, :width].reshape(owners * capacity, width))


def combine_kernel(
    me_ref, t_ref, b_ref, sum_ref, first_probs_ref, own_ref, probs_ref, send1_ref, send2_ref, send3_ref
):
    owners, capacity, _ = b_ref.shape
    rows = owners * capacity
    width = sum_ref.shape[1]
    piece = own_ref.shape[1]
    probs = first_probs_ref[...] + slot_probs(t_ref, b_ref, 1, width)
    probs = probs + pltpu.roll(probs, ROPE, 1)
    probs_ref[...] = probs
    high = probs.astype(BF16)
    low = (probs - high.astype(F32)).astype(BF16)
    short = lax.broadcasted_iota(jnp.int32, probs.shape, 1)
    message = jnp.where(short >= ROPE, high.astype(F32), low.astype(F32)).astype(BF16)
    for step, out_ref in enumerate((own_ref, send1_ref, send2_ref, send3_ref)):
        place = block_at(me_ref[0], step, width // piece, piece)
        part = sum_ref[:, place] + dot_nn(t_ref[...], b_ref[:, :, place].reshape(rows, piece))
        if step == 0:
            own_ref[...] = part
        else:
            out_ref[:, :piece] = part.astype(BF16)
            out_ref[:, piece:] = message


def attend_back_kernel(
    me_ref,
    core_ref,
    stream_ref,
    cot_ref,
    middle_ref,
    a0_ref,
    a1_ref,
    a2_ref,
    a3_ref,
    r1_ref,
    r2_ref,
    r3_ref,
    probs_own_ref,
    router_probs_ref,
    w_in,
    router_ref,
    mixed_ref,
    normed_in,
    query_in,
    expanded_in,
    key_ref,
    latent_ref,
    compressed_in,
    probs_in,
    attended_ref,
    gains_ref,
    latent_gain_ref,
    cos_ref,
    sin_ref,
    keep_ref,
    pass_ref,
    middle_grad_ref,
    own_ref,
    send1_ref,
    send2_ref,
    send3_ref,
    scr_ref,
    low_ref,
    wide_ref,
    w_ref,
    normed_ref,
    query_ref,
    expanded_ref,
    compressed_ref,
    probs_ref,
    sems,
    in_sems,
):
    heads, tokens, _ = probs_ref.shape
    width = stream_ref.shape[1]
    piece = own_ref.shape[1]
    nope = heads * NOPE
    queries = nope + heads * ROPE
    edge = queries + LATENT + LANES
    outer = edge + heads * VDIM
    owners = 32
    shard = width // owners
    short = LATENT // owners
    count = width // piece
    me = me_ref[0]
    copies = []
    for source, target in (
        (w_in.at[:, edge : outer + 2 * NOPE], w_ref.at[:, edge:]),
        (probs_in, probs_ref),
        (expanded_in, expanded_ref),
        (query_in, query_ref),
        (compressed_in, compressed_ref),
        (w_in.at[:, :edge], w_ref.at[:, :edge]),
        (normed_in, normed_ref),
    ):
        copies.append(pltpu.make_async_copy(source, target, in_sems.at[len(copies)]))
        copies[-1].start()
    probs_grad = probs_own_ref[...]
    for r_ref in (r1_ref, r2_ref, r3_ref):
        other = r_ref[:, piece:].astype(F32)
        probs_grad = probs_grad + other + pltpu.roll(other, ROPE, 1)
    router_probs = router_probs_ref[...]
    logits_low = (
        router_probs * (probs_grad - jnp.sum(router_probs * probs_grad, axis=-1, keepdims=True))
    ).astype(BF16)
    router_back = dot_nt(logits_low, router_ref[...])
    for step, a_ref in enumerate((a0_ref, a1_ref, a2_ref, a3_ref)):
        wide_ref[:, block_at(me, step, count, piece)] = a_ref[...].astype(F32)
    mixed_grad = wide_ref[...] + router_back
    middle = middle_ref[...]
    norm_grad, second_gain_rows = rms_back(middle, inverse_rms(middle), gains_ref[1:2, :], mixed_grad)
    second_gain_grad = jnp.sum(second_gain_rows, axis=0, keepdims=True)
    middle_grad = cot_ref[...] + norm_grad
    middle_grad_ref[...] = middle_grad
    middle_low = middle_grad.astype(BF16)
    core = core_ref[0]
    router_grad = dot_tn(mixed_ref[...], logits_low)
    scr_ref[:, outer + 2 * NOPE :] = pltpu.roll(router_grad, ROPE, 1).astype(BF16)
    scr_ref[:, edge:outer] = dot_tn(middle_low, attended_ref[...]).astype(BF16)
    copies[0].wait()
    attended_grad = dot_nn(middle_low, w_ref[:, edge:outer]).astype(BF16)
    for copy in copies[1:5]:
        copy.wait()
    scale = (NOPE + ROPE) ** (-0.5)
    key_low = key_ref[...]
    key_odd = pltpu.roll(key_low.astype(F32), ROPE, 1).astype(BF16)
    latent = latent_ref[...]
    latent_part = jnp.zeros((tokens, LATENT), F32)
    key_even_grad = jnp.zeros((tokens, LANES), F32)
    key_odd_grad = jnp.zeros((tokens, LANES), F32)
    rope_grads = []
    grads4 = scr_ref.reshape(owners, shard, scr_ref.shape[1])
    for head in range(heads):
        pair = nope + head // 2 * LANES
        expanded = expanded_ref[:, head * 2 * NOPE : (head + 1) * 2 * NOPE]
        probs = probs_ref[head]
        head_grad = attended_grad[:, head * VDIM : (head + 1) * VDIM]
        value_grad = dot_tn(probs.astype(BF16), head_grad)
        probs_att = dot_nt(head_grad, expanded[:, NOPE:])
        scores = probs * (probs_att - jnp.sum(probs * probs_att, axis=-1, keepdims=True))
        raw_low = (scores * scale).astype(BF16)
        low_ref[:, head * NOPE : (head + 1) * NOPE] = dot_nn(raw_low, expanded[:, :NOPE]).astype(BF16)
        turn_grad = dot_nn(raw_low, key_odd if head % 2 else key_low)
        if head % 2:
            rope_grads[-1] = rope_grads[-1] + turn_grad
            key_odd_grad += dot_tn(raw_low, query_ref[:, pair : pair + LANES])
        else:
            rope_grads.append(turn_grad)
            key_even_grad += dot_tn(raw_low, query_ref[:, pair : pair + LANES])
        key_grad = dot_tn(raw_low, query_ref[:, head * NOPE : (head + 1) * NOPE])
        expanded_low = jnp.concatenate([key_grad, value_grad], axis=1).astype(BF16)
        up = w_ref[:, outer : outer + 2 * NOPE].reshape(owners, heads, short, 2 * NOPE)[:, head]
        up = up.reshape(LATENT, 2 * NOPE)
        latent_part += dot_nt(expanded_low, up)
        grads4[:, head * short : (head + 1) * short, outer : outer + 2 * NOPE] = (
            dot_tn(latent, expanded_low).astype(BF16).reshape(owners, short, 2 * NOPE)
        )
    rope_grad = jnp.concatenate(rope_grads, axis=1)
    low_ref[:, nope:queries] = rotated(rope_grad, cos_ref[...], -sin_ref[...]).astype(BF16)
    compressed = compressed_ref[...]
    latent_grad, latent_gain_rows = rms_back(
        compressed, inverse_rms(compressed), latent_gain_ref[2:3, :], latent_part
    )
    latent_gain_grad = jnp.sum(latent_gain_rows, axis=0, keepdims=True)
    low_ref[:, queries : queries + LATENT] = latent_grad.astype(BF16)
    lane = lax.broadcasted_iota(jnp.int32, (tokens, LANES), 1)
    key_grad = jnp.where(lane < ROPE, key_even_grad + pltpu.roll(key_odd_grad, ROPE, 1), 0.0)
    key_grad = rotated(key_grad, cos_ref[:, :LANES], -sin_ref[:, :LANES])
    low_ref[:, queries + LATENT : edge] = jnp.where(lane < ROPE, key_grad, 0.0).astype(BF16)
    halves = scr_ref.reshape(owners // 2, 2, shard, scr_ref.shape[1])
    outgoing = [
        pltpu.make_async_copy(halves.at[:, 1 - core, :, edge:], pass_ref.at[:, :, edge:], sems.at[0]),
        pltpu.make_async_copy(halves.at[:, core, :, edge:], keep_ref.at[:, :, edge:], sems.at[1]),
    ]
    for copy in outgoing:
        copy.start()
    for copy in copies[5:]:
        copy.wait()
    low = low_ref[...]
    for step, out_ref in enumerate((own_ref, send1_ref, send2_ref, send3_ref)):
        place = block_at(me, step, count, piece)
        part = dot_nt(low, w_ref[place, :edge])
        wide_ref[:, place] = part
        out_ref[...] = part.astype(out_ref.dtype)
    stream = stream_ref[...].astype(F32)
    first_gain_grad = jnp.sum(wide_ref[...] * (stream * inverse_rms(stream)), axis=0, keepdims=True)
    late = dot_tn(normed_ref[...], low[:, queries:])
    sub = lax.broadcasted_iota(jnp.int32, (LANES, width), 0)
    gain_columns = (
        jnp.where(sub == ROPE, first_gain_grad, 0.0)
        + jnp.where(sub == ROPE + 1, second_gain_grad * (1.0 / count), 0.0)
    ).T
    key_columns = (late[:, LATENT:] + gain_columns).reshape(owners, shard, LANES)
    sub = lax.broadcasted_iota(jnp.int32, (LANES, LATENT), 0)
    latent_columns = jnp.where(sub == ROPE + 2, latent_gain_grad, 0.0).T.reshape(owners, short, LANES)
    grads4[:, :, queries : queries + LATENT] = (
        late[:, :LATENT].astype(BF16).reshape(owners, shard, LATENT)
    )
    grads4[:, :, queries + LATENT : edge] = key_columns.astype(BF16)
    grads4[:, :short, queries + LATENT : edge] = (key_columns[:, :short] + latent_columns).astype(BF16)
    scr_ref[:, :queries] = dot_tn(normed_ref[...], low[:, :queries]).astype(BF16)
    outgoing += [
        pltpu.make_async_copy(halves.at[:, 1 - core, :, :edge], pass_ref.at[:, :, :edge], sems.at[2]),
        pltpu.make_async_copy(halves.at[:, core, :, :edge], keep_ref.at[:, :, :edge], sems.at[3]),
    ]
    for copy in outgoing[2:]:
        copy.start()
    for copy in outgoing:
        copy.wait()


def pair_kernel(at_ref, keep_ref, got_ref, along_z_ref, *along_x_refs):
    side = len(along_x_refs)
    cut = along_x_refs[0].shape[2]

    def part(index, columns):
        return (keep_ref[index, :, columns].astype(F32) + got_ref[index, :, columns].astype(F32)).astype(BF16)

    for z in range(side):
        for x in range(side):
            along_z_ref[z, x] = part(x * side + z, slice(cut, None))
    for step, out_ref in enumerate(along_x_refs):
        peer = lax.rem(at_ref[0] + step, side)
        for other in range(side):
            out_ref[other] = part(peer * side + other, slice(0, cut))


def cross_kernel(group, at_ref, *refs):
    parts, out_refs = refs[:-4], refs[-4:]
    for step, out_ref in enumerate(out_refs):
        peer = lax.rem(at_ref[1 - group] + step, len(out_refs))
        if len(parts) == 1:
            rows = [parts[0][source, peer] for source in range(parts[0].shape[0])]
        else:
            rows = [r_ref[peer] for r_ref in parts]
        total = rows[0].astype(F32)
        for row in rows[1:]:
            total = total + row.astype(F32)
        out_ref[...] = total.astype(out_ref.dtype)


def unpack_kernel(*refs):
    query_ref, late_ref, output_ref, up_ref, router_ref, total_ref = refs[-6:]
    heads = up_ref.shape[1] // (2 * NOPE)
    short = up_ref.shape[0]
    nope = heads * NOPE
    queries = nope + heads * ROPE
    edge = queries + LATENT + LANES
    outer = edge + heads * VDIM
    start = 0
    for group in range(2):
        parts = refs[4 * group : 4 * group + 4]
        width = parts[0].shape[1]
        total = parts[0][...]
        for r_ref in parts[1:]:
            total = total + r_ref[...].astype(F32)
        total_ref[:, start : start + width] = total
        start += width
    total = total_ref[...]
    for head in range(heads):
        start = head * (NOPE + ROPE)
        query_ref[:, start : start + NOPE] = total[:, head * NOPE : (head + 1) * NOPE]
        query_ref[:, start + NOPE : start + NOPE + ROPE] = total[
            :, nope + head * ROPE : nope + (head + 1) * ROPE
        ]
        up_ref[:, head * 2 * NOPE : (head + 1) * 2 * NOPE] = total[
            head * short : (head + 1) * short, outer : outer + 2 * NOPE
        ]
    late_ref[...] = total[:, queries:edge]
    output_ref[...] = total[:, edge:outer]
    router_ref[...] = total[:, outer + 2 * NOPE : outer + 2 * NOPE + ROPE]


def late_kernel(own_ref, r1_ref, r2_ref, r3_ref, down_ref, gains_ref):
    total = own_ref[...]
    for r_ref in (r1_ref, r2_ref, r3_ref):
        total = total + r_ref[...].astype(F32)
    down_ref[...] = total[:, : down_ref.shape[1]]
    columns = total[:, LATENT:]
    columns = jnp.concatenate([columns, jnp.zeros(columns.shape, F32)], axis=0)
    gains_ref[...] = columns.T[ROPE : ROPE + 8, :]


def stream_kernel(me_ref, middle_grad_ref, stream_ref, gains_ref, a0_ref, a1_ref, a2_ref, a3_ref, out_ref, wide_ref):
    piece = a0_ref.shape[1]
    count = stream_ref.shape[1] // piece
    for step, a_ref in enumerate((a0_ref, a1_ref, a2_ref, a3_ref)):
        wide_ref[:, block_at(me_ref[0], step, count, piece)] = a_ref[...].astype(F32)
    stream = stream_ref[...].astype(F32)
    norm_grad, _ = rms_back(stream, inverse_rms(stream), gains_ref[0:1, :], wide_ref[...])
    out_ref[...] = middle_grad_ref[...] + norm_grad


def routed_kernel(t0_ref, t1_ref, o_ref, own_ref, r1_ref, r2_ref, r3_ref, out_ref):
    owners, _, capacity, piece = o_ref.shape
    rows = owners * capacity
    total = own_ref[...]
    for r_ref in (r1_ref, r2_ref, r3_ref):
        total = total + r_ref[...].astype(F32)
    for index, t_ref in ((0, t0_ref), (1, t1_ref)):
        total = total + dot_nn(t_ref[...], o_ref[:, index].reshape(rows, piece))
    out_ref[...] = total.astype(BF16)


def result_kernel(me_ref, middle_ref, a0_ref, a1_ref, a2_ref, a3_ref, out_ref):
    piece = a0_ref.shape[1]
    count = middle_ref.shape[1] // piece
    for step, a_ref in enumerate((a0_ref, a1_ref, a2_ref, a3_ref)):
        place = block_at(me_ref[0], step, count, piece)
        out_ref[:, place] = middle_ref[:, place] + a_ref[...].astype(F32)


def shift(array, step):
    size = lax.axis_size("tensor")
    return lax.ppermute(array, "tensor", [(i, (i + step) % size) for i in range(size)])


def send_blocks(sends):
    return [shift(array, step + 1) for step, array in enumerate(sends)]


def share_small(low):
    size = lax.axis_size("tensor")
    return [low] + [shift(low, size - step) for step in range(1, size)]


def ring_first(rows):
    return shift(rows, 1), shift(rows, lax.axis_size("tensor") - 1)


def ring_second(rows, before, after):
    half = rows.shape[0] // 2
    across = [shift(before[:half], 1), shift(after[half:], lax.axis_size("tensor") - 1)]
    return [rows, after, jnp.concatenate(across, axis=0), before]


def after(array, *others):
    return lax.optimization_barrier((array, *others))[0]


def exchange(rows):
    shape = rows.shape
    return lax.all_to_all(
        rows.reshape(shape[0], -1, shape[-1]), "expert", split_axis=0, concat_axis=0, tiled=True
    ).reshape(shape)


def per_device(
    stream,
    segment_ids,
    expert_ids,
    first_gain,
    query_proj,
    latent_down,
    latent_gain,
    latent_up,
    output_proj,
    second_gain,
    router_proj,
    shared_gate,
    shared_up,
    shared_down,
    expert_gate,
    expert_up,
    expert_down,
    cotangent,
):
    tokens, width = stream.shape
    owners = lax.axis_size("expert")
    tensors = lax.axis_size("tensor")
    shard = query_proj.shape[0]
    heads = query_proj.shape[1] // (NOPE + ROPE)
    short = latent_up.shape[0]
    experts = router_proj.shape[1]
    hidden_columns = shared_gate.shape[1]
    local, _, expert_hidden = expert_gate.shape
    capacity = tokens * TOPK * 4 // (3 * experts)
    rows = owners * capacity
    piece = width // tensors
    nope = heads * NOPE
    queries = nope + heads * ROPE
    edge = queries + LATENT + LANES
    outer = edge + heads * VDIM
    me = lax.axis_index("tensor").astype(jnp.int32).reshape(1)
    base = (lax.axis_index("expert") * local).astype(jnp.int32).reshape(1)
    core = lax.rem(lax.axis_index("expert"), 2).astype(jnp.int32).reshape(1)
    smem = {0: pltpu.SMEM}

    gains = jnp.concatenate(
        [
            first_gain[:, None],
            second_gain[:, None],
            jnp.pad(latent_gain, (0, shard - short))[:, None],
            jnp.zeros((shard, ROPE - 3), BF16),
        ],
        axis=1,
    )
    by_head = query_proj.reshape(shard, heads, NOPE + ROPE)
    pack_one = jnp.concatenate(
        [
            by_head[:, :, :NOPE].reshape(shard, nope),
            by_head[:, :, NOPE:].reshape(shard, heads * ROPE),
            latent_down,
            router_proj,
            output_proj.T,
            latent_up.reshape(short, heads, 2 * NOPE).transpose(1, 0, 2).reshape(shard, 2 * NOPE),
            gains,
        ],
        axis=1,
    )
    pack_two = jnp.concatenate([shared_gate, shared_up, shared_down.T], axis=1)
    one = lax.all_gather(pack_one, "expert", axis=0, tiled=True)
    two = lax.all_gather(pack_two, "expert", axis=0, tiled=True)

    position = jnp.arange(tokens).astype(F32)
    exponent = jnp.arange(ROPE // 2).astype(F32) * (2.0 / ROPE)
    angles = position[:, None] * jnp.exp(-math.log(ROTARY_BASE) * exponent)[None, :]
    cosine = jnp.tile(jnp.cos(angles), (1, 2 * heads))
    sine = jnp.sin(angles)
    sine = jnp.tile(jnp.concatenate([-sine, sine], axis=1), (1, heads))

    t0, t1, s0, s1, cot_low, cot_out = run(
        routing_kernel,
        [
            ((tokens, rows), BF16),
            ((tokens, rows), BF16),
            ((rows, tokens), BF16),
            ((rows, tokens), BF16),
            ((tokens, width), BF16),
            ((owners, local, capacity, piece), BF16),
        ],
        [me, expert_ids.T, cotangent],
        2 * local * tokens * rows * (piece + experts),
        places=smem,
        name="routing",
    )

    cot_own = exchange(cot_out)
    cot_before, cot_after = ring_first(cot_own)
    (
        own,
        send1,
        send2,
        send3,
        normed,
        query,
        expanded,
        key,
        latent,
        compressed,
        probs,
        attended,
        gain_rows,
        latent_gain_rows,
    ) = run(
        attend_kernel,
        [
            ((tokens, piece), F32),
            ((tokens, piece), BF16),
            ((tokens, piece), BF16),
            ((tokens, piece), BF16),
            ((tokens, width), BF16),
            ((tokens, queries), BF16),
            ((tokens, heads * 2 * NOPE), BF16),
            ((tokens, LANES), BF16),
            ((tokens, LATENT), BF16),
            ((tokens, LATENT), F32),
            ((heads, tokens, tokens), F32),
            ((tokens, heads * VDIM), BF16),
            ((8, width), F32),
            ((8, LATENT), F32),
        ],
        [after(me, cot_own), stream, one, segment_ids, segment_ids.T, cosine, sine],
        2 * tokens * width * outer,
        places=smem,
        name="attend",
    )
    got = send_blocks([send1, send2, send3])
    attention = (own + got[0].astype(F32) + got[1].astype(F32) + got[2].astype(F32)).astype(BF16)
    attention = after(attention, cot_before, cot_after)
    middle, mixed, x_out = run(
        dispatch_kernel,
        [
            ((tokens, width), F32),
            ((tokens, width), BF16),
            ((owners, capacity, width + piece), BF16),
        ],
        [me, stream, *share_small(attention), gain_rows, s0, s1],
        2 * tokens * rows * (width + piece),
        places=smem,
        name="dispatch",
    )
    x_in = exchange(x_out)
    cots = ring_second(cot_own, cot_before, cot_after)
    x1s = x_in[:, :, width:]
    x1_before, x1_after = ring_first(x1s)
    x1s = [x_in] + ring_second(x1s, x1_before, x1_after)[1:]
    router_block = one[:, queries + LATENT : edge]
    (
        shared_own,
        shared1,
        shared2,
        shared3,
        shared_back,
        router_probs,
        shared_grads,
    ) = run(
        shared_kernel,
        [
            ((tokens, piece), F32),
            ((tokens, piece), BF16),
            ((tokens, piece), BF16),
            ((tokens, piece), BF16),
            ((tokens, width), F32),
            ((tokens, LANES), F32),
            ((width, 3 * hidden_columns), BF16),
        ],
        [me, mixed, cot_low, two, router_block],
        18 * tokens * width * hidden_columns,
        places=smem,
        name="shared",
    )
    base = after(base, shared_back)

    gate_t = expert_gate.transpose(0, 2, 1)
    up_t = expert_up.transpose(0, 2, 1)
    chunk = owners // 2
    back0, c0, hg0, gr0, ur0 = expert_back(
        False, me, base, [x_in], cots, gate_t, up_t, expert_down, one, edge // LANES - 1, chunk // 2
    )
    back0 = exchange(back0)
    back1, c1, hg1, gr1, ur1, x1 = expert_back(
        True, me, after(base, hg0), x1s, cots, gate_t, up_t, expert_down, one, edge // LANES - 1, chunk // 2
    )
    back1 = exchange(after(back1, back0))
    gr0 = after(gr0, back0)
    gate_grad, up_grad, down_grad = expert_grads(
        (x_in, c0, hg0, gr0, ur0), (x1, c1, hg1, gr1, ur1), tensors
    )
    out0 = expert_out(0, hg0, expert_down, owners, tensors, chunk)
    out1 = expert_out(1, after(hg1, out0), expert_down, owners, tensors, chunk)
    out_rows = [
        lax.psum_scatter(out, "tensor", scatter_dimension=0, tiled=True).reshape(owners, 1, capacity, piece)
        for out in (out0, out1)
    ]

    first_sum, first_probs = run(
        combine_first_kernel,
        [((tokens, width), F32), ((tokens, LANES), F32)],
        [t0, back0, shared_back],
        2 * tokens * rows * width,
        name="combine_first",
    )
    own, probs_own, send1, send2, send3 = run(
        combine_kernel,
        [
            ((tokens, piece), F32),
            ((tokens, LANES), F32),
            ((tokens, piece + LANES), BF16),
            ((tokens, piece + LANES), BF16),
            ((tokens, piece + LANES), BF16),
        ],
        [after(me, out1, gate_grad), t1, back1, first_sum, first_probs],
        2 * tokens * rows * width,
        places=smem,
        name="combine",
    )
    got = send_blocks([send1, send2, send3])
    out_rows = exchange(after(jnp.concatenate(out_rows, axis=1), own))
    shared_sum = lax.psum_scatter(
        after(shared_grads, own), "expert", scatter_dimension=0, tiled=True
    )
    mixed_sum = (
        own
        + got[0][:, :piece].astype(F32)
        + got[1][:, :piece].astype(F32)
        + got[2][:, :piece].astype(F32)
    ).astype(BF16)
    keep, passed, middle_grad, own, send1, send2, send3 = run(
        attend_back_kernel,
        [
            ((owners // 2, shard, outer + 2 * NOPE + LANES), BF16),
            ((owners // 2, shard, outer + 2 * NOPE + LANES), BF16),
            ((tokens, width), F32),
            ((tokens, piece), F32),
            ((tokens, piece), BF16),
            ((tokens, piece), BF16),
            ((tokens, piece), BF16),
        ],
        [
            me,
            core,
            stream,
            cotangent,
            middle,
            *share_small(mixed_sum),
            *got,
            probs_own,
            router_probs,
            one,
            router_block,
            mixed,
            normed,
            query,
            expanded,
            key,
            latent,
            compressed,
            probs,
            attended,
            gain_rows,
            latent_gain_rows,
            cosine,
            sine,
        ],
        2 * tokens * width * (3 * edge + 2 * outer),
        scratch=[
            pltpu.VMEM((width, outer + 2 * NOPE + LANES), BF16),
            pltpu.VMEM((tokens, edge), BF16),
            pltpu.VMEM((tokens, width), F32),
            pltpu.VMEM((width, outer + 2 * NOPE), BF16),
            pltpu.VMEM(normed.shape, BF16),
            pltpu.VMEM(query.shape, BF16),
            pltpu.VMEM(expanded.shape, BF16),
            pltpu.VMEM(compressed.shape, F32),
            pltpu.VMEM(probs.shape, F32),
            pltpu.SemaphoreType.DMA((4,)),
            pltpu.SemaphoreType.DMA((7,)),
        ],
        places={0: pltpu.SMEM, 1: pltpu.SMEM} | {i: pl.ANY for i in (14, 17, 18, 19, 22, 23)},
        out_places={0: pl.ANY, 1: pl.ANY},
        name="attend_back",
    )
    paired = lax.ppermute(after(passed, out_rows), "expert", [(i, i ^ 1) for i in range(owners)])
    side = 4
    chip = lax.axis_index("expert") // 2
    at = jnp.stack([chip // side, lax.rem(chip, side)]).astype(jnp.int32)
    columns = outer + 2 * NOPE + LANES
    cut = columns // 2

    def along(group, array, step):
        def target(i):
            x, z, core = i // (2 * side), i // 2 % side, i % 2
            if group == 0:
                x = (x + step) % side
            else:
                z = (z + step) % side
            return (x * side + z) * 2 + core

        return lax.ppermute(array, "expert", [(i, target(i)) for i in range(owners)])

    widths = [cut, columns - cut]
    along_z, *along_x = run(
        pair_kernel,
        [((side, side, shard, widths[1]), BF16)] + [((side, shard, cut), BF16)] * side,
        [at, keep, paired],
        0,
        places=smem,
        name="pair",
    )
    came_z = lax.all_to_all(
        along_z.reshape(side, side * shard, widths[1]),
        "expert",
        split_axis=0,
        concat_axis=0,
        tiled=True,
        axis_index_groups=[[(x * side + z) * 2 + c for z in range(side)] for x in range(side) for c in range(2)],
    ).reshape(along_z.shape)
    came_x = [along_x[0]] + [along(0, along_x[step], step) for step in range(1, side)]
    parts = []
    for group, came in enumerate((came_x, [came_z])):
        crossed = run(
            functools.partial(cross_kernel, group),
            [((shard, widths[group]), F32)] + [((shard, widths[group]), BF16)] * (side - 1),
            [at, *came],
            0,
            places=smem,
            name="cross",
        )
        parts += [crossed[0]] + [along(1 - group, crossed[step], step) for step in range(1, side)]
    got = send_blocks([send1, send2, send3])
    first_sum = (own + got[0].astype(F32) + got[1].astype(F32) + got[2].astype(F32)).astype(BF16)
    (stream_grad,) = run(
        stream_kernel,
        [((tokens, width), F32)],
        [after(me, parts[0], parts[4]), middle_grad, stream, gain_rows, *share_small(first_sum)],
        0,
        scratch=[pltpu.VMEM((tokens, width), F32)],
        places=smem,
        name="stream",
    )

    got = send_blocks([shared1, shared2, shared3])
    (branch,) = run(
        routed_kernel,
        [((tokens, piece), BF16)],
        [t0, t1, out_rows, shared_own, *got],
        4 * tokens * rows * piece,
        name="routed",
    )
    (result,) = run(
        result_kernel,
        [((tokens, width), F32)],
        [after(me, parts[0], parts[4]), middle, *share_small(branch)],
        0,
        places=smem,
        name="result",
    )

    shared_sum = shared_sum.astype(F32)
    gate_sum = shared_sum[:, :hidden_columns]
    up_sum = shared_sum[:, hidden_columns : 2 * hidden_columns]
    down_sum = shared_sum[:, 2 * hidden_columns :]
    parts[0] = after(parts[0], stream_grad, result, gate_sum, up_sum, down_sum)
    query_grad, late, output_grad, latent_up_grad, router_grad = run(
        unpack_kernel,
        [
            (query_proj.shape, F32),
            ((shard, edge - queries), F32),
            ((shard, heads * VDIM), F32),
            (latent_up.shape, F32),
            (router_proj.shape, F32),
        ],
        parts,
        0,
        scratch=[pltpu.VMEM((shard, columns), F32)],
        name="unpack",
    )
    latent_down_grad, gain_grads = run(
        late_kernel,
        [(latent_down.shape, F32), ((8, LANES), F32)],
        [late, *(shift(late.astype(BF16), step) for step in range(1, tensors))],
        0,
        name="late",
    )
    return (
        result,
        stream_grad,
        gain_grads[0, :shard],
        query_grad,
        latent_down_grad,
        gain_grads[2, :short],
        latent_up_grad,
        output_grad.T,
        gain_grads[1, :shard],
        router_grad,
        gate_sum,
        up_sum,
        down_sum.T,
        gate_grad.transpose(0, 2, 1),
        up_grad.transpose(0, 2, 1),
        down_grad,
    )


def solution(mesh):
    placed = (
        P("expert", None),
        P("expert", None),
        P("expert", None),
        P("expert"),
        P("expert", "tensor"),
        P("expert", None),
        P("expert"),
        P("expert", "tensor"),
        P("tensor", "expert"),
        P("expert"),
        P("expert", None),
        P("expert", "tensor"),
        P("expert", "tensor"),
        P("tensor", "expert"),
        P("expert", None, "tensor"),
        P("expert", None, "tensor"),
        P("expert", "tensor", None),
        P("expert", None),
    )
    return jax.shard_map(
        per_device,
        mesh=mesh,
        in_specs=placed,
        out_specs=(
            P("expert", None),
            P("expert", None),
            P("expert"),
            P("expert", "tensor"),
            P("expert", None),
            P("expert"),
            P("expert", "tensor"),
            P("tensor", "expert"),
            P("expert"),
            P("expert", None),
            P("expert", "tensor"),
            P("expert", "tensor"),
            P("tensor", "expert"),
            P("expert", None, "tensor"),
            P("expert", None, "tensor"),
            P("expert", "tensor", None),
        ),
        check_vma=False,
    )
```

```python
import functools
import math

import jax
import jax.numpy as jnp
from jax import lax
from jax.experimental import pallas as pl
from jax.experimental.pallas import tpu as pltpu
from jax.sharding import PartitionSpec as P

NOPE = 128
ROPE = 64
VDIM = 128
LATENT = 512
TOPK = 6
EPSILON = 1e-06
ROTARY_BASE = 10000.0

BF16 = jnp.bfloat16
F32 = jnp.float32
VMEM_BYTES = 60 * 1024 * 1024
LANES = 128
COST_SCALE = 10


def dot_nn(left, right):
    return lax.dot_general(left, right, (((1,), (0,)), ((), ())), preferred_element_type=F32)


def dot_nt(left, right):
    return lax.dot_general(left, right, (((1,), (1,)), ((), ())), preferred_element_type=F32)


def dot_tn(left, right):
    return lax.dot_general(left, right, (((0,), (0,)), ((), ())), preferred_element_type=F32)


def silu_parts(pre_values):
    sigmoid_value = 1.0 / (1.0 + jnp.exp(-pre_values))
    return (pre_values * sigmoid_value, sigmoid_value * (1.0 + pre_values * (1.0 - sigmoid_value)))


def inverse_rms(values):
    return lax.rsqrt(jnp.mean(values * values, axis=-1, keepdims=True) + EPSILON)


def rms_back(values, scale, gain, grad):
    normed = values * scale
    weighted = grad * gain
    return (
        scale * (weighted - normed * jnp.mean(weighted * normed, axis=-1, keepdims=True)),
        grad * normed,
    )


def turned(values):
    width = values.shape[1]
    lane = lax.broadcasted_iota(jnp.int32, values.shape, 1) % ROPE
    half = ROPE // 2
    return jnp.where(
        lane < half, pltpu.roll(values, width - half, 1), pltpu.roll(values, half, 1)
    )


def rotated(values, cosine, sine):
    return values * cosine + turned(values) * sine


def block_at(me, step, count, width):
    return pl.ds(pl.multiple_of(lax.rem(me + step, count) * width, width), width)


def run(kernel, outs, args, flops, scratch=(), name=None, places=None, aliases=None, out_places=None):
    places = places or {}
    out_places = out_places or {}
    in_specs = [pl.BlockSpec(memory_space=places.get(i, pltpu.VMEM)) for i in range(len(args))]
    out_specs = [pl.BlockSpec(memory_space=out_places.get(i, pltpu.VMEM)) for i in range(len(outs))]
    moved = sum(a.size * a.dtype.itemsize for a in args) + sum(
        math.prod(shape) * jnp.dtype(dtype).itemsize for shape, dtype in outs
    )
    return pl.pallas_call(
        kernel,
        in_specs=in_specs,
        out_specs=out_specs,
        out_shape=[jax.ShapeDtypeStruct(shape, dtype) for shape, dtype in outs],
        scratch_shapes=list(scratch),
        input_output_aliases=aliases or {},
        compiler_params=pltpu.CompilerParams(vmem_limit_bytes=VMEM_BYTES),
        cost_estimate=pl.CostEstimate(
            flops=flops // COST_SCALE, bytes_accessed=moved // COST_SCALE, transcendentals=0
        ),
        name=name,
    )(*args)


def pack_kernel(
    first_ref, second_ref, latent_gain_ref, query_ref, down_ref, router_ref, output_ref, up_ref, out_ref
):
    shard = query_ref.shape[0]
    short = up_ref.shape[0]
    heads = up_ref.shape[1] // (2 * NOPE)
    nope = heads * NOPE
    queries = nope + heads * ROPE
    edge = queries + LATENT + LANES
    outer = edge + output_ref.shape[1]
    for head in range(heads):
        start = head * (NOPE + ROPE)
        out_ref[:, head * NOPE : (head + 1) * NOPE] = query_ref[:, start : start + NOPE]
        out_ref[:, nope + head * ROPE : nope + (head + 1) * ROPE] = query_ref[
            :, start + NOPE : start + NOPE + ROPE
        ]
        out_ref[head * short : (head + 1) * short, outer : outer + 2 * NOPE] = up_ref[
            :, head * 2 * NOPE : (head + 1) * 2 * NOPE
        ]
    out_ref[:, queries : queries + LATENT + ROPE] = down_ref[...]
    out_ref[:, queries + LATENT + ROPE : edge] = router_ref[...]
    out_ref[:, edge:outer] = output_ref[...]
    sub = lax.broadcasted_iota(jnp.int32, (LANES, LANES), 0)
    lane = lax.broadcasted_iota(jnp.int32, (LANES, LANES), 1)
    rows = jnp.zeros((LANES, LANES), F32)
    for index, g_ref in enumerate((first_ref, second_ref, latent_gain_ref)):
        gain = jnp.concatenate([g_ref[...].astype(F32), jnp.zeros((1, LANES - shard), F32)], axis=1)
        rows = jnp.where((sub == index) & (lane < shard), gain, rows)
    out_ref[:, outer + 2 * NOPE :] = rows.T[:shard, : out_ref.shape[1] - outer - 2 * NOPE].astype(BF16)


def routing_kernel(me_ref, ids_ref, cot_ref, t0_ref, t1_ref, s0_ref, s1_ref, low_ref, out_ref):
    choices, tokens = ids_ref.shape
    owners, local, capacity, piece = out_ref.shape
    experts = owners * local
    rows = owners * capacity
    expert = lax.broadcasted_iota(jnp.int32, (experts, tokens), 0)
    chosen = jnp.zeros((experts, tokens), F32)
    for choice in range(choices):
        chosen += jnp.where(ids_ref[choice : choice + 1, :] == expert, 1.0, 0.0)
    before = jnp.where(
        lax.broadcasted_iota(jnp.int32, (tokens, tokens), 0)
        < lax.broadcasted_iota(jnp.int32, (tokens, tokens), 1),
        1.0,
        0.0,
    ).astype(BF16)
    place = dot_nn(chosen.astype(BF16), before)
    place = jnp.where(chosen > 0.5, place, -1.0).astype(BF16)
    low = cot_ref[...].astype(BF16)
    low_ref[...] = low
    mine = cot_ref[:, block_at(me_ref[0], 0, cot_ref.shape[1] // piece, piece)].astype(BF16)
    slot = (lax.broadcasted_iota(jnp.int32, (tokens, rows), 1) % capacity).astype(F32)
    for index, (t_ref, s_ref) in enumerate(((t0_ref, s0_ref), (t1_ref, s1_ref))):
        spread = jnp.where(
            lax.broadcasted_iota(jnp.int32, (experts, rows), 0)
            == lax.broadcasted_iota(jnp.int32, (experts, rows), 1) // capacity * local + index,
            1.0,
            0.0,
        ).astype(BF16)
        wanted = dot_tn(place, spread)
        matrix = jnp.where(wanted == slot, 1.0, 0.0).astype(BF16)
        t_ref[...] = matrix
        by_slot = matrix.T
        s_ref[...] = by_slot
        out_ref[:, index] = dot_nn(by_slot, mine).astype(BF16).reshape(owners, capacity, piece)


def attend_kernel(
    me_ref,
    stream_ref,
    w_ref,
    seg_row_ref,
    seg_col_ref,
    cos_ref,
    sin_ref,
    own_ref,
    send1_ref,
    send2_ref,
    send3_ref,
    normed_ref,
    query_ref,
    expanded_ref,
    key_ref,
    latent_ref,
    compressed_ref,
    probs_ref,
    attended_ref,
    gains_ref,
    latent_gain_ref,
):
    heads, tokens, _ = probs_ref.shape
    width = stream_ref.shape[1]
    piece = own_ref.shape[1]
    nope = heads * NOPE
    queries = nope + heads * ROPE
    edge = queries + LATENT + LANES
    outer = edge + heads * VDIM
    owners = 32
    columns = jnp.concatenate(
        [w_ref[:, outer + 2 * NOPE :].astype(F32), jnp.zeros((width, ROPE), F32)], axis=1
    )
    gains = columns.T[:8, :]
    gains_ref[...] = gains
    shard = width // owners
    short = LATENT // owners
    latent_gain = (
        columns.reshape(owners, shard, LANES)[:, :short, :].reshape(LATENT, LANES).T[:8, :]
    )
    latent_gain_ref[...] = latent_gain
    stream = stream_ref[...].astype(F32)
    normed = (stream * inverse_rms(stream) * gains[0:1, :]).astype(BF16)
    normed_ref[...] = normed
    projected = dot_nn(normed, w_ref[:, :edge])
    query_ref[:, :nope] = projected[:, :nope].astype(BF16)
    query_ref[:, nope:] = rotated(projected[:, nope:queries], cos_ref[...], sin_ref[...]).astype(BF16)
    compressed = projected[:, queries : queries + LATENT]
    compressed_ref[...] = compressed
    latent = (compressed * inverse_rms(compressed) * latent_gain[2:3, :]).astype(BF16)
    latent_ref[...] = latent
    raw_key = projected[:, queries + LATENT : edge]
    key = rotated(raw_key, cos_ref[:, :LANES], sin_ref[:, :LANES])
    lane = lax.broadcasted_iota(jnp.int32, key.shape, 1)
    key = jnp.where(lane < ROPE, key, 0.0)
    key_low = key.astype(BF16)
    key_odd = pltpu.roll(key, ROPE, 1).astype(BF16)
    key_ref[...] = key_low
    row = lax.broadcasted_iota(jnp.int32, (tokens, tokens), 0)
    column = lax.broadcasted_iota(jnp.int32, (tokens, tokens), 1)
    allowed = (seg_col_ref[...] == seg_row_ref[...]) & (column <= row)
    scale = (NOPE + ROPE) ** (-0.5)
    for head in range(heads):
        block = slice(head * 2 * NOPE, (head + 1) * 2 * NOPE)
        up = w_ref[:, outer : outer + 2 * NOPE].reshape(owners, heads, short, 2 * NOPE)[:, head]
        up = up.reshape(LATENT, 2 * NOPE)
        expanded = dot_nn(latent, up).astype(BF16)
        expanded_ref[:, block] = expanded
        pair = nope + head // 2 * LANES
        raw = dot_nt(query_ref[:, head * NOPE : (head + 1) * NOPE], expanded[:, :NOPE]) + dot_nt(
            query_ref[:, pair : pair + LANES], key_odd if head % 2 else key_low
        )
        scores = jnp.where(allowed, raw * scale, -1e30)
        weight = jnp.exp(scores - jnp.max(scores, axis=-1, keepdims=True))
        probs = weight / jnp.sum(weight, axis=-1, keepdims=True)
        probs_ref[head] = probs
        attended_ref[:, head * VDIM : (head + 1) * VDIM] = dot_nn(
            probs.astype(BF16), expanded[:, NOPE:]
        ).astype(BF16)
    attended = attended_ref[...]
    for step, out_ref in enumerate((own_ref, send1_ref, send2_ref, send3_ref)):
        part = dot_nt(attended, w_ref[block_at(me_ref[0], step, width // piece, piece), edge:outer])
        out_ref[...] = part.astype(out_ref.dtype)


def dispatch_kernel(
    me_ref, stream_ref, a0_ref, a1_ref, a2_ref, a3_ref, gains_ref, s0_ref, s1_ref, middle_ref, mixed_ref, out_ref
):
    piece = a0_ref.shape[1]
    width = stream_ref.shape[1]
    count = width // piece
    owners, capacity, _ = out_ref.shape
    for step, a_ref in enumerate((a0_ref, a1_ref, a2_ref, a3_ref)):
        place = block_at(me_ref[0], step, count, piece)
        middle_ref[:, place] = stream_ref[:, place].astype(F32) + a_ref[...].astype(F32)
    middle = middle_ref[...]
    mixed = (middle * inverse_rms(middle) * gains_ref[1:2, :]).astype(BF16)
    mixed_ref[...] = mixed
    mine = mixed_ref[:, block_at(me_ref[0], 0, count, piece)]
    out_ref[:, :, width:] = dot_nn(s1_ref[...], mine).astype(BF16).reshape(owners, capacity, piece)
    out_ref[:, :, :width] = dot_nn(s0_ref[...], mixed).astype(BF16).reshape(owners, capacity, width)


def shared_kernel(
    me_ref,
    mixed_ref,
    cot_ref,
    w_ref,
    router_ref,
    own_ref,
    send1_ref,
    send2_ref,
    send3_ref,
    back_ref,
    probs_ref,
    grads_ref,
):
    width = mixed_ref.shape[1]
    piece = own_ref.shape[1]
    hidden_columns = w_ref.shape[1] // 3
    mixed = mixed_ref[...]
    cot = cot_ref[...]
    pre = dot_nn(mixed, w_ref[:, : 2 * hidden_columns])
    gate_pre, up_pre = pre[:, :hidden_columns], pre[:, hidden_columns:]
    act, slope = silu_parts(gate_pre)
    hidden = (act * up_pre).astype(BF16)
    hidden_grad = dot_nn(cot, w_ref[:, 2 * hidden_columns :])
    pair = jnp.concatenate([hidden_grad * up_pre * slope, hidden_grad * act], axis=1).astype(BF16)
    grads_ref[:, : 2 * hidden_columns] = dot_tn(mixed, pair).astype(BF16)
    grads_ref[:, 2 * hidden_columns :] = dot_tn(cot, hidden).astype(BF16)
    back_ref[...] = dot_nt(pair, w_ref[:, : 2 * hidden_columns])
    logits = dot_nn(mixed, router_ref[...])
    lane = lax.broadcasted_iota(jnp.int32, logits.shape, 1)
    logits = jnp.where(lane >= ROPE, logits, -1e30)
    weight = jnp.exp(logits - jnp.max(logits, axis=-1, keepdims=True))
    probs_ref[...] = weight / jnp.sum(weight, axis=-1, keepdims=True)
    for step, out_ref in enumerate((own_ref, send1_ref, send2_ref, send3_ref)):
        place = block_at(me_ref[0], step, width // piece, piece)
        part = dot_nt(hidden, w_ref[place, 2 * hidden_columns :])
        out_ref[...] = part.astype(out_ref.dtype)


def expert_back_kernel(split, *refs):
    if split:
        me_ref, base_ref, x0_ref, x1_ref, x2_ref, x3_ref = refs[:6]
        refs = refs[6:]
    else:
        me_ref, base_ref, x_ref = refs[:3]
        refs = refs[3:]
    c0_ref, c1_ref, c2_ref, c3_ref, wg_ref, wu_ref, wd_ref, router_ref = refs[:8]
    refs = refs[8:]
    if split:
        back_ref, c_ref, hg_ref, gr_ref, ur_ref, x_ref, wide_ref, down_ref, tall_ref = refs
    else:
        back_ref, c_ref, hg_ref, gr_ref, ur_ref, wide_ref, down_ref, tall_ref = refs
    sources, capacity, width = c_ref.shape
    rows = sources * capacity
    piece = c0_ref.shape[-1]
    count = width // piece
    hidden_columns = wd_ref.shape[1]
    padded = down_ref.shape[1]
    me = me_ref[0]

    @pl.when(pl.program_id(0) == 0)
    def _():
        rest = jnp.zeros((padded - hidden_columns, width), BF16)
        gate_up = jnp.concatenate([wg_ref[0], rest, wu_ref[0], rest], axis=0)
        tall_ref[...] = gate_up
        wide_ref[...] = gate_up.T
        down_ref[...] = jnp.concatenate([wd_ref[0], rest], axis=0).T

    for step, p_ref in enumerate((c0_ref, c1_ref, c2_ref, c3_ref)):
        c_ref[:, :, block_at(me, step, count, piece)] = p_ref[:, 0]
    if split:
        for step, p_ref in enumerate((x0_ref, x1_ref, x2_ref, x3_ref)):
            x_ref[:, :, block_at(me, step, count, piece)] = p_ref[...]
    x = x_ref[...].reshape(rows, width)
    expert = base_ref[0] + (1 if split else 0) + ROPE
    logits = dot_nn(x, router_ref[...])
    lane = lax.broadcasted_iota(jnp.int32, logits.shape, 1)
    logits = jnp.where(lane >= ROPE, logits, -1e30)
    weight = jnp.exp(logits - jnp.max(logits, axis=-1, keepdims=True))
    gate = jnp.sum(jnp.where(lane == expert, weight, 0.0), axis=-1, keepdims=True) / jnp.sum(
        weight, axis=-1, keepdims=True
    )
    pre = dot_nn(x, wide_ref[...])
    gate_pre, up_pre = pre[:, :padded], pre[:, padded:]
    hidden_cot = dot_nn(c_ref[...].reshape(rows, width), down_ref[...])
    act, slope = silu_parts(gate_pre)
    hidden = (act * up_pre).astype(BF16).astype(F32)
    gate_grad = jnp.sum(hidden * hidden_cot, axis=-1, keepdims=True)
    hidden_grad = gate * hidden_cot
    gate_rows = (hidden_grad * up_pre * slope).astype(BF16)
    up_rows = (hidden_grad * act).astype(BF16)
    hg_ref[...] = (gate * hidden).astype(BF16)[:, :hidden_columns]
    gr_ref[...] = gate_rows[:, :hidden_columns]
    ur_ref[...] = up_rows[:, :hidden_columns]
    high = gate_grad.astype(BF16).astype(F32)
    low = gate_grad - high
    beside = jnp.where(lane == 0, high, 0.0) + jnp.where(lane == 1, low, 0.0)
    back = dot_nn(jnp.concatenate([gate_rows, up_rows], axis=1), tall_ref[...])
    back_ref[:, :, :width] = back.astype(BF16).reshape(sources, capacity, width)
    back_ref[:, :, width:] = beside.astype(BF16).reshape(sources, capacity, LANES)


def expert_back(split, me, base, xs, cs, wg, wu, wd, router, router_at, chunk):
    owners, local, capacity, piece = cs[0].shape
    hidden, width = wg.shape[1:]
    local_index = 1 if split else 0
    rows = owners * capacity
    padded = -(-hidden // LANES) * LANES
    scalar = pl.BlockSpec(memory_space=pltpu.SMEM)
    row_spec = pl.BlockSpec((chunk * capacity, hidden), lambda c: (c, 0))
    row_shape = jax.ShapeDtypeStruct((rows, hidden), BF16)
    wide_spec = pl.BlockSpec((chunk, capacity, width), lambda c: (c, 0, 0))
    wide_shape = jax.ShapeDtypeStruct((owners, capacity, width), BF16)
    narrow_spec = pl.BlockSpec((chunk, capacity, piece), lambda c: (c, 0, 0))
    own_spec = pl.BlockSpec((chunk, capacity, piece), lambda c: (c, 0, width // piece))
    cot_spec = pl.BlockSpec((chunk, 1, capacity, piece), lambda c: (c, local_index, 0, 0))
    weight_spec = pl.BlockSpec((1, hidden, width), lambda c: (local_index, 0, 0))
    in_specs = [scalar, scalar]
    in_specs += [own_spec] + [narrow_spec] * 3 if split else [wide_spec]
    in_specs += [cot_spec] * 4 + [weight_spec] * 3 + [pl.BlockSpec((width, LANES), lambda c: (0, router_at))]
    out_specs = [pl.BlockSpec((chunk, capacity, width + LANES), lambda c: (c, 0, 0)), wide_spec]
    out_shape = [jax.ShapeDtypeStruct((owners, capacity, width + LANES), BF16), wide_shape]
    last_spec, last_shape = ([wide_spec], [wide_shape]) if split else ([], [])
    return pl.pallas_call(
        functools.partial(expert_back_kernel, split),
        grid=(owners // chunk,),
        in_specs=in_specs,
        out_specs=out_specs + [row_spec] * 3 + last_spec,
        out_shape=out_shape + [row_shape] * 3 + last_shape,
        scratch_shapes=[
            pltpu.VMEM((width, 2 * padded), BF16),
            pltpu.VMEM((width, padded), BF16),
            pltpu.VMEM((2 * padded, width), BF16),
        ],
        compiler_params=pltpu.CompilerParams(vmem_limit_bytes=VMEM_BYTES),
        cost_estimate=pl.CostEstimate(
            flops=100 * rows * hidden * width, bytes_accessed=24 * 1024 * 1024, transcendentals=0
        ),
        name="expert_back",
    )(me, base, *xs, *cs, wg, wu, wd, router)


def expert_out_kernel(hg_ref, wd_ref, out_ref):
    pieces, sources, capacity, piece = out_ref.shape
    out = dot_nn(hg_ref[...], wd_ref[0]).astype(BF16)
    for index in range(pieces):
        out_ref[index] = out[:, index * piece : (index + 1) * piece].reshape(sources, capacity, piece)


def expert_out(expert, hg, wd, owners, pieces, chunk):
    rows, hidden = hg.shape
    width = wd.shape[2]
    capacity = rows // owners
    piece = width // pieces
    return pl.pallas_call(
        expert_out_kernel,
        grid=(owners // chunk,),
        in_specs=[
            pl.BlockSpec((chunk * capacity, hidden), lambda c: (c, 0)),
            pl.BlockSpec((1, hidden, width), lambda c: (expert, 0, 0)),
        ],
        out_specs=pl.BlockSpec((pieces, chunk, capacity, piece), lambda c: (0, c, 0, 0)),
        out_shape=jax.ShapeDtypeStruct((pieces, owners, capacity, piece), BF16),
        compiler_params=pltpu.CompilerParams(vmem_limit_bytes=VMEM_BYTES),
        cost_estimate=pl.CostEstimate(
            flops=rows * hidden * width // 5, bytes_accessed=6 * 1024 * 102, transcendentals=0
        ),
        name="expert_out",
    )(hg, wd)


def expert_grads_kernel(
    x0_ref, c0_ref, hg0_ref, gr0_ref, ur0_ref, x1_ref, c1_ref, hg1_ref, gr1_ref, ur1_ref, dg_ref, du_ref, dd_ref
):
    owners, capacity, piece = x0_ref.shape
    rows = owners * capacity

    def step(x_ref, c_ref, hg_ref, gr_ref, ur_ref):
        x = x_ref[...].reshape(rows, piece)
        dg_ref[0] = dot_tn(gr_ref[...], x)
        du_ref[0] = dot_tn(ur_ref[...], x)
        dd_ref[0] = dot_tn(hg_ref[...], c_ref[...].reshape(rows, piece))

    pl.when(pl.program_id(0) == 0)(lambda: step(x0_ref, c0_ref, hg0_ref, gr0_ref, ur0_ref))
    pl.when(pl.program_id(0) == 1)(lambda: step(x1_ref, c1_ref, hg1_ref, gr1_ref, ur1_ref))


def expert_grads(first, second, pieces):
    owners, capacity, width = first[1].shape
    rows, hidden = first[2].shape
    piece = width // pieces
    row_spec = pl.BlockSpec((rows, hidden), lambda e, j: (0, 0))

    def specs(expert):
        stay = 0 if expert else pieces - 1
        wide = pl.BlockSpec(
            (owners, capacity, piece), lambda e, j: (0, 0, jnp.where(e == expert, j, stay))
        )
        return [wide, wide, row_spec, row_spec, row_spec]

    out_spec = pl.BlockSpec((1, hidden, piece), lambda e, j: (e, 0, j))
    out_shape = jax.ShapeDtypeStruct((2, hidden, width), F32)
    return pl.pallas_call(
        expert_grads_kernel,
        grid=(2, pieces),
        in_specs=specs(0) + specs(1),
        out_specs=[out_spec] * 3,
        out_shape=[out_shape] * 3,
        compiler_params=pltpu.CompilerParams(vmem_limit_bytes=VMEM_BYTES),
        cost_estimate=pl.CostEstimate(
            flops=rows * hidden * width, bytes_accessed=40 * 1024 * 102, transcendentals=0
        ),
        name="expert_grads",
    )(*first, *second)


def slot_probs(t_ref, b_ref, index, width):
    owners, capacity, _ = b_ref.shape
    rows = owners * capacity
    beside = b_ref[:, :, width:].reshape(rows, LANES).astype(F32)
    lane = lax.broadcasted_iota(jnp.int32, (rows, LANES), 1)
    expert = 2 * (lax.broadcasted_iota(jnp.int32, (rows, LANES), 0) // capacity) + index
    spread = jnp.where(lane == expert + ROPE, beside[:, 0:1], 0.0) + jnp.where(
        lane == expert, beside[:, 1:2], 0.0
    )
    return dot_nn(t_ref[...], spread.astype(BF16))


def combine_first_kernel(t_ref, b_ref, shared_ref, sum_ref, probs_ref):
    owners, capacity, _ = b_ref.shape
    width = shared_ref.shape[1]
    probs_ref[...] = slot_probs(t_ref, b_ref, 0, width)
    sum_ref[...] = shared_ref[...] + dot_nn(t_ref[...], b_ref[:, :, :width].reshape(owners * capacity, width))


def combine_kernel(
    me_ref, t_ref, b_ref, sum_ref, first_probs_ref, own_ref, probs_ref, send1_ref, send2_ref, send3_ref
):
    owners, capacity, _ = b_ref.shape
    rows = owners * capacity
    width = sum_ref.shape[1]
    piece = own_ref.shape[1]
    probs = first_probs_ref[...] + slot_probs(t_ref, b_ref, 1, width)
    probs = probs + pltpu.roll(probs, ROPE, 1)
    probs_ref[...] = probs
    high = probs.astype(BF16)
    low = (probs - high.astype(F32)).astype(BF16)
    short = lax.broadcasted_iota(jnp.int32, probs.shape, 1)
    message = jnp.where(short >= ROPE, high.astype(F32), low.astype(F32)).astype(BF16)
    for step, out_ref in enumerate((own_ref, send1_ref, send2_ref, send3_ref)):
        place = block_at(me_ref[0], step, width // piece, piece)
        part = sum_ref[:, place] + dot_nn(t_ref[...], b_ref[:, :, place].reshape(rows, piece))
        if step == 0:
            own_ref[...] = part
        else:
            out_ref[:, :piece] = part.astype(BF16)
            out_ref[:, piece:] = message


def attend_back_kernel(
    me_ref,
    core_ref,
    stream_ref,
    cot_ref,
    middle_ref,
    a0_ref,
    a1_ref,
    a2_ref,
    a3_ref,
    r1_ref,
    r2_ref,
    r3_ref,
    probs_own_ref,
    router_probs_ref,
    w_in,
    router_ref,
    mixed_ref,
    normed_in,
    query_in,
    expanded_in,
    key_ref,
    latent_ref,
    compressed_in,
    probs_in,
    attended_ref,
    gains_ref,
    latent_gain_ref,
    cos_ref,
    sin_ref,
    keep_ref,
    pass_ref,
    middle_grad_ref,
    own_ref,
    send1_ref,
    send2_ref,
    send3_ref,
    scr_ref,
    low_ref,
    wide_ref,
    w_ref,
    normed_ref,
    query_ref,
    expanded_ref,
    compressed_ref,
    probs_ref,
    sems,
    in_sems,
):
    heads, tokens, _ = probs_ref.shape
    width = stream_ref.shape[1]
    piece = own_ref.shape[1]
    nope = heads * NOPE
    queries = nope + heads * ROPE
    edge = queries + LATENT + LANES
    outer = edge + heads * VDIM
    owners = 32
    shard = width // owners
    short = LATENT // owners
    count = width // piece
    me = me_ref[0]
    copies = []
    for source, target in (
        (w_in.at[:, edge : outer + 2 * NOPE], w_ref.at[:, edge:]),
        (probs_in, probs_ref),
        (expanded_in, expanded_ref),
        (query_in, query_ref),
        (compressed_in, compressed_ref),
        (w_in.at[:, :edge], w_ref.at[:, :edge]),
        (normed_in, normed_ref),
    ):
        copies.append(pltpu.make_async_copy(source, target, in_sems.at[len(copies)]))
        copies[-1].start()
    probs_grad = probs_own_ref[...]
    for r_ref in (r1_ref, r2_ref, r3_ref):
        other = r_ref[:, piece:].astype(F32)
        probs_grad = probs_grad + other + pltpu.roll(other, ROPE, 1)
    router_probs = router_probs_ref[...]
    logits_low = (
        router_probs * (probs_grad - jnp.sum(router_probs * probs_grad, axis=-1, keepdims=True))
    ).astype(BF16)
    router_back = dot_nt(logits_low, router_ref[...])
    for step, a_ref in enumerate((a0_ref, a1_ref, a2_ref, a3_ref)):
        wide_ref[:, block_at(me, step, count, piece)] = a_ref[...].astype(F32)
    mixed_grad = wide_ref[...] + router_back
    middle = middle_ref[...]
    norm_grad, second_gain_rows = rms_back(middle, inverse_rms(middle), gains_ref[1:2, :], mixed_grad)
    second_gain_grad = jnp.sum(second_gain_rows, axis=0, keepdims=True)
    middle_grad = cot_ref[...] + norm_grad
    middle_grad_ref[...] = middle_grad
    middle_low = middle_grad.astype(BF16)
    core = core_ref[0]
    router_grad = dot_tn(mixed_ref[...], logits_low)
    scr_ref[:, outer + 2 * NOPE :] = pltpu.roll(router_grad, ROPE, 1).astype(BF16)
    scr_ref[:, edge:outer] = dot_tn(middle_low, attended_ref[...]).astype(BF16)
    copies[0].wait()
    attended_grad = dot_nn(middle_low, w_ref[:, edge:outer]).astype(BF16)
    for copy in copies[1:5]:
        copy.wait()
    scale = (NOPE + ROPE) ** (-0.5)
    key_low = key_ref[...]
    key_odd = pltpu.roll(key_low.astype(F32), ROPE, 1).astype(BF16)
    latent = latent_ref[...]
    latent_part = jnp.zeros((tokens, LATENT), F32)
    key_even_grad = jnp.zeros((tokens, LANES), F32)
    key_odd_grad = jnp.zeros((tokens, LANES), F32)
    rope_grads = []
    grads4 = scr_ref.reshape(owners, shard, scr_ref.shape[1])
    for head in range(heads):
        pair = nope + head // 2 * LANES
        expanded = expanded_ref[:, head * 2 * NOPE : (head + 1) * 2 * NOPE]
        probs = probs_ref[head]
        head_grad = attended_grad[:, head * VDIM : (head + 1) * VDIM]
        value_grad = dot_tn(probs.astype(BF16), head_grad)
        probs_att = dot_nt(head_grad, expanded[:, NOPE:])
        scores = probs * (probs_att - jnp.sum(probs * probs_att, axis=-1, keepdims=True))
        raw_low = (scores * scale).astype(BF16)
        low_ref[:, head * NOPE : (head + 1) * NOPE] = dot_nn(raw_low, expanded[:, :NOPE]).astype(BF16)
        turn_grad = dot_nn(raw_low, key_odd if head % 2 else key_low)
        if head % 2:
            rope_grads[-1] = rope_grads[-1] + turn_grad
            key_odd_grad += dot_tn(raw_low, query_ref[:, pair : pair + LANES])
        else:
            rope_grads.append(turn_grad)
            key_even_grad += dot_tn(raw_low, query_ref[:, pair : pair + LANES])
        key_grad = dot_tn(raw_low, query_ref[:, head * NOPE : (head + 1) * NOPE])
        expanded_low = jnp.concatenate([key_grad, value_grad], axis=1).astype(BF16)
        up = w_ref[:, outer : outer + 2 * NOPE].reshape(owners, heads, short, 2 * NOPE)[:, head]
        up = up.reshape(LATENT, 2 * NOPE)
        latent_part += dot_nt(expanded_low, up)
        grads4[:, head * short : (head + 1) * short, outer : outer + 2 * NOPE] = (
            dot_tn(latent, expanded_low).astype(BF16).reshape(owners, short, 2 * NOPE)
        )
    rope_grad = jnp.concatenate(rope_grads, axis=1)
    low_ref[:, nope:queries] = rotated(rope_grad, cos_ref[...], -sin_ref[...]).astype(BF16)
    compressed = compressed_ref[...]
    latent_grad, latent_gain_rows = rms_back(
        compressed, inverse_rms(compressed), latent_gain_ref[2:3, :], latent_part
    )
    latent_gain_grad = jnp.sum(latent_gain_rows, axis=0, keepdims=True)
    low_ref[:, queries : queries + LATENT] = latent_grad.astype(BF16)
    lane = lax.broadcasted_iota(jnp.int32, (tokens, LANES), 1)
    key_grad = jnp.where(lane < ROPE, key_even_grad + pltpu.roll(key_odd_grad, ROPE, 1), 0.0)
    key_grad = rotated(key_grad, cos_ref[:, :LANES], -sin_ref[:, :LANES])
    low_ref[:, queries + LATENT : edge] = jnp.where(lane < ROPE, key_grad, 0.0).astype(BF16)
    halves = scr_ref.reshape(owners // 2, 2, shard, scr_ref.shape[1])
    outgoing = [
        pltpu.make_async_copy(halves.at[:, 1 - core, :, edge:], pass_ref.at[:, :, edge:], sems.at[0]),
        pltpu.make_async_copy(halves.at[:, core, :, edge:], keep_ref.at[:, :, edge:], sems.at[1]),
    ]
    for copy in outgoing:
        copy.start()
    for copy in copies[5:]:
        copy.wait()
    low = low_ref[...]
    for step, out_ref in enumerate((own_ref, send1_ref, send2_ref, send3_ref)):
        place = block_at(me, step, count, piece)
        part = dot_nt(low, w_ref[place, :edge])
        wide_ref[:, place] = part
        out_ref[...] = part.astype(out_ref.dtype)
    stream = stream_ref[...].astype(F32)
    first_gain_grad = jnp.sum(wide_ref[...] * (stream * inverse_rms(stream)), axis=0, keepdims=True)
    late = dot_tn(normed_ref[...], low[:, queries:])
    sub = lax.broadcasted_iota(jnp.int32, (LANES, width), 0)
    gain_columns = (
        jnp.where(sub == ROPE, first_gain_grad, 0.0)
        + jnp.where(sub == ROPE + 1, second_gain_grad * (1.0 / count), 0.0)
    ).T
    key_columns = (late[:, LATENT:] + gain_columns).reshape(owners, shard, LANES)
    sub = lax.broadcasted_iota(jnp.int32, (LANES, LATENT), 0)
    latent_columns = jnp.where(sub == ROPE + 2, latent_gain_grad, 0.0).T.reshape(owners, short, LANES)
    grads4[:, :, queries : queries + LATENT] = (
        late[:, :LATENT].astype(BF16).reshape(owners, shard, LATENT)
    )
    grads4[:, :, queries + LATENT : edge] = key_columns.astype(BF16)
    grads4[:, :short, queries + LATENT : edge] = (key_columns[:, :short] + latent_columns).astype(BF16)
    scr_ref[:, :queries] = dot_tn(normed_ref[...], low[:, :queries]).astype(BF16)
    outgoing += [
        pltpu.make_async_copy(halves.at[:, 1 - core, :, :edge], pass_ref.at[:, :, :edge], sems.at[2]),
        pltpu.make_async_copy(halves.at[:, core, :, :edge], keep_ref.at[:, :, :edge], sems.at[3]),
    ]
    for copy in outgoing[2:]:
        copy.start()
    for copy in outgoing:
        copy.wait()


def pair_kernel(at_ref, keep_ref, got_ref, along_z_ref, *along_x_refs):
    side = len(along_x_refs)
    cut = along_x_refs[0].shape[2]

    def part(index, columns):
        return (keep_ref[index, :, columns].astype(F32) + got_ref[index, :, columns].astype(F32)).astype(BF16)

    for z in range(side):
        for x in range(side):
            along_z_ref[z, x] = part(x * side + z, slice(cut, None))
    for step, out_ref in enumerate(along_x_refs):
        peer = lax.rem(at_ref[0] + step, side)
        for other in range(side):
            out_ref[other] = part(peer * side + other, slice(0, cut))


def cross_kernel(group, at_ref, *refs):
    parts, out_refs = refs[:-4], refs[-4:]
    for step, out_ref in enumerate(out_refs):
        peer = lax.rem(at_ref[1 - group] + step, len(out_refs))
        if len(parts) == 1:
            rows = [parts[0][source, peer] for source in range(parts[0].shape[0])]
        else:
            rows = [r_ref[peer] for r_ref in parts]
        total = rows[0].astype(F32)
        for row in rows[1:]:
            total = total + row.astype(F32)
        out_ref[...] = total.astype(out_ref.dtype)


def unpack_kernel(*refs):
    query_ref, late_ref, output_ref, up_ref, router_ref, total_ref = refs[-6:]
    heads = up_ref.shape[1] // (2 * NOPE)
    short = up_ref.shape[0]
    nope = heads * NOPE
    queries = nope + heads * ROPE
    edge = queries + LATENT + LANES
    outer = edge + heads * VDIM
    start = 0
    for group in range(2):
        parts = refs[4 * group : 4 * group + 4]
        width = parts[0].shape[1]
        total = parts[0][...]
        for r_ref in parts[1:]:
            total = total + r_ref[...].astype(F32)
        total_ref[:, start : start + width] = total
        start += width
    total = total_ref[...]
    for head in range(heads):
        start = head * (NOPE + ROPE)
        query_ref[:, start : start + NOPE] = total[:, head * NOPE : (head + 1) * NOPE]
        query_ref[:, start + NOPE : start + NOPE + ROPE] = total[
            :, nope + head * ROPE : nope + (head + 1) * ROPE
        ]
        up_ref[:, head * 2 * NOPE : (head + 1) * 2 * NOPE] = total[
            head * short : (head + 1) * short, outer : outer + 2 * NOPE
        ]
    late_ref[...] = total[:, queries:edge]
    output_ref[...] = total[:, edge:outer]
    router_ref[...] = total[:, outer + 2 * NOPE : outer + 2 * NOPE + ROPE]


def late_kernel(own_ref, r1_ref, r2_ref, r3_ref, down_ref, gains_ref):
    total = own_ref[...]
    for r_ref in (r1_ref, r2_ref, r3_ref):
        total = total + r_ref[...].astype(F32)
    down_ref[...] = total[:, : down_ref.shape[1]]
    columns = total[:, LATENT:]
    columns = jnp.concatenate([columns, jnp.zeros(columns.shape, F32)], axis=0)
    gains_ref[...] = columns.T[ROPE : ROPE + 8, :]


def stream_kernel(me_ref, middle_grad_ref, stream_ref, gains_ref, a0_ref, a1_ref, a2_ref, a3_ref, out_ref, wide_ref):
    piece = a0_ref.shape[1]
    count = stream_ref.shape[1] // piece
    for step, a_ref in enumerate((a0_ref, a1_ref, a2_ref, a3_ref)):
        wide_ref[:, block_at(me_ref[0], step, count, piece)] = a_ref[...].astype(F32)
    stream = stream_ref[...].astype(F32)
    norm_grad, _ = rms_back(stream, inverse_rms(stream), gains_ref[0:1, :], wide_ref[...])
    out_ref[...] = middle_grad_ref[...] + norm_grad


def routed_kernel(t0_ref, t1_ref, o_ref, own_ref, r1_ref, r2_ref, r3_ref, out_ref):
    owners, _, capacity, piece = o_ref.shape
    rows = owners * capacity
    total = own_ref[...]
    for r_ref in (r1_ref, r2_ref, r3_ref):
        total = total + r_ref[...].astype(F32)
    for index, t_ref in ((0, t0_ref), (1, t1_ref)):
        total = total + dot_nn(t_ref[...], o_ref[:, index].reshape(rows, piece))
    out_ref[...] = total.astype(BF16)


def result_kernel(me_ref, middle_ref, a0_ref, a1_ref, a2_ref, a3_ref, out_ref):
    piece = a0_ref.shape[1]
    count = middle_ref.shape[1] // piece
    for step, a_ref in enumerate((a0_ref, a1_ref, a2_ref, a3_ref)):
        place = block_at(me_ref[0], step, count, piece)
        out_ref[:, place] = middle_ref[:, place] + a_ref[...].astype(F32)


def shift(array, step):
    size = lax.axis_size("tensor")
    return lax.ppermute(array, "tensor", [(i, (i + step) % size) for i in range(size)])


def send_blocks(sends):
    return [shift(array, step + 1) for step, array in enumerate(sends)]


def share_small(low):
    size = lax.axis_size("tensor")
    return [low] + [shift(low, size - step) for step in range(1, size)]


def ring_first(rows):
    return shift(rows, 1), shift(rows, lax.axis_size("tensor") - 1)


def ring_second(rows, before, after):
    half = rows.shape[0] // 2
    across = [shift(before[:half], 1), shift(after[half:], lax.axis_size("tensor") - 1)]
    return [rows, after, jnp.concatenate(across, axis=0), before]


def after(array, *others):
    return lax.optimization_barrier((array, *others))[0]


def exchange(rows):
    shape = rows.shape
    return lax.all_to_all(
        rows.reshape(shape[0], -1, shape[-1]), "expert", split_axis=0, concat_axis=0, tiled=True
    ).reshape(shape)


def per_device(
    stream,
    segment_ids,
    expert_ids,
    first_gain,
    query_proj,
    latent_down,
    latent_gain,
    latent_up,
    output_proj,
    second_gain,
    router_proj,
    shared_gate,
    shared_up,
    shared_down,
    expert_gate,
    expert_up,
    expert_down,
    cotangent,
):
    tokens, width = stream.shape
    owners = lax.axis_size("expert")
    tensors = lax.axis_size("tensor")
    shard = query_proj.shape[0]
    heads = query_proj.shape[1] // (NOPE + ROPE)
    short = latent_up.shape[0]
    experts = router_proj.shape[1]
    hidden_columns = shared_gate.shape[1]
    local, _, expert_hidden = expert_gate.shape
    capacity = tokens * TOPK * 4 // (3 * experts)
    rows = owners * capacity
    piece = width // tensors
    nope = heads * NOPE
    queries = nope + heads * ROPE
    edge = queries + LATENT + LANES
    outer = edge + heads * VDIM
    me = lax.axis_index("tensor").astype(jnp.int32).reshape(1)
    base = (lax.axis_index("expert") * local).astype(jnp.int32).reshape(1)
    core = lax.rem(lax.axis_index("expert"), 2).astype(jnp.int32).reshape(1)
    smem = {0: pltpu.SMEM}

    (pack_one,) = run(
        pack_kernel,
        [((shard, outer + 2 * NOPE + ROPE), BF16)],
        [
            first_gain.reshape(1, shard),
            second_gain.reshape(1, shard),
            jnp.pad(latent_gain, (0, shard - short)).reshape(1, shard),
            query_proj,
            latent_down,
            router_proj,
            output_proj.T,
            latent_up,
        ],
        0,
        name="pack",
    )
    pack_two = jnp.concatenate([shared_gate, shared_up, shared_down.T], axis=1)
    one = lax.all_gather(pack_one, "expert", axis=0, tiled=True)
    two = lax.all_gather(pack_two, "expert", axis=0, tiled=True)

    position = jnp.arange(tokens).astype(F32)
    exponent = jnp.arange(ROPE // 2).astype(F32) * (2.0 / ROPE)
    angles = position[:, None] * jnp.exp(-math.log(ROTARY_BASE) * exponent)[None, :]
    cosine = jnp.tile(jnp.cos(angles), (1, 2 * heads))
    sine = jnp.sin(angles)
    sine = jnp.tile(jnp.concatenate([-sine, sine], axis=1), (1, heads))

    t0, t1, s0, s1, cot_low, cot_out = run(
        routing_kernel,
        [
            ((tokens, rows), BF16),
            ((tokens, rows), BF16),
            ((rows, tokens), BF16),
            ((rows, tokens), BF16),
            ((tokens, width), BF16),
            ((owners, local, capacity, piece), BF16),
        ],
        [me, expert_ids.T, cotangent],
        2 * local * tokens * rows * (piece + experts),
        places=smem,
        name="routing",
    )

    cot_own = exchange(cot_out)
    cot_before, cot_after = ring_first(cot_own)
    (
        own,
        send1,
        send2,
        send3,
        normed,
        query,
        expanded,
        key,
        latent,
        compressed,
        probs,
        attended,
        gain_rows,
        latent_gain_rows,
    ) = run(
        attend_kernel,
        [
            ((tokens, piece), F32),
            ((tokens, piece), BF16),
            ((tokens, piece), BF16),
            ((tokens, piece), BF16),
            ((tokens, width), BF16),
            ((tokens, queries), BF16),
            ((tokens, heads * 2 * NOPE), BF16),
            ((tokens, LANES), BF16),
            ((tokens, LATENT), BF16),
            ((tokens, LATENT), F32),
            ((heads, tokens, tokens), F32),
            ((tokens, heads * VDIM), BF16),
            ((8, width), F32),
            ((8, LATENT), F32),
        ],
        [after(me, cot_own), stream, one, segment_ids, segment_ids.T, cosine, sine],
        2 * tokens * width * outer,
        places=smem,
        name="attend",
    )
    got = send_blocks([send1, send2, send3])
    attention = (own + got[0].astype(F32) + got[1].astype(F32) + got[2].astype(F32)).astype(BF16)
    attention = after(attention, cot_before, cot_after)
    middle, mixed, x_out = run(
        dispatch_kernel,
        [
            ((tokens, width), F32),
            ((tokens, width), BF16),
            ((owners, capacity, width + piece), BF16),
        ],
        [me, stream, *share_small(attention), gain_rows, s0, s1],
        2 * tokens * rows * (width + piece),
        places=smem,
        name="dispatch",
    )
    x_in = exchange(x_out)
    cots = ring_second(cot_own, cot_before, cot_after)
    x1s = x_in[:, :, width:]
    x1_before, x1_after = ring_first(x1s)
    x1s = [x_in] + ring_second(x1s, x1_before, x1_after)[1:]
    router_block = one[:, queries + LATENT : edge]
    (
        shared_own,
        shared1,
        shared2,
        shared3,
        shared_back,
        router_probs,
        shared_grads,
    ) = run(
        shared_kernel,
        [
            ((tokens, piece), F32),
            ((tokens, piece), BF16),
            ((tokens, piece), BF16),
            ((tokens, piece), BF16),
            ((tokens, width), F32),
            ((tokens, LANES), F32),
            ((width, 3 * hidden_columns), BF16),
        ],
        [me, mixed, cot_low, two, router_block],
        18 * tokens * width * hidden_columns,
        places=smem,
        name="shared",
    )
    base = after(base, shared_back)

    gate_t = expert_gate.transpose(0, 2, 1)
    up_t = expert_up.transpose(0, 2, 1)
    chunk = owners // 2
    back0, c0, hg0, gr0, ur0 = expert_back(
        False, me, base, [x_in], cots, gate_t, up_t, expert_down, one, edge // LANES - 1, chunk // 2
    )
    back0 = exchange(back0)
    back1, c1, hg1, gr1, ur1, x1 = expert_back(
        True, me, after(base, hg0), x1s, cots, gate_t, up_t, expert_down, one, edge // LANES - 1, chunk // 2
    )
    back1 = exchange(after(back1, back0))
    gr0 = after(gr0, back0)
    gate_grad, up_grad, down_grad = expert_grads(
        (x_in, c0, hg0, gr0, ur0), (x1, c1, hg1, gr1, ur1), tensors
    )
    out0 = expert_out(0, hg0, expert_down, owners, tensors, chunk)
    out1 = expert_out(1, after(hg1, out0), expert_down, owners, tensors, chunk)
    out_rows = [
        lax.psum_scatter(out, "tensor", scatter_dimension=0, tiled=True).reshape(owners, 1, capacity, piece)
        for out in (out0, out1)
    ]

    out_cat = jnp.concatenate(out_rows, axis=1)
    shared_got = send_blocks([after(shared1, back0), shared2, shared3])
    first_sum, first_probs = run(
        combine_first_kernel,
        [((tokens, width), F32), ((tokens, LANES), F32)],
        [t0, back0, shared_back],
        2 * tokens * rows * width,
        name="combine_first",
    )
    own, probs_own, send1, send2, send3 = run(
        combine_kernel,
        [
            ((tokens, piece), F32),
            ((tokens, LANES), F32),
            ((tokens, piece + LANES), BF16),
            ((tokens, piece + LANES), BF16),
            ((tokens, piece + LANES), BF16),
        ],
        [after(me, out_cat, gate_grad, *shared_got), t1, back1, first_sum, first_probs],
        2 * tokens * rows * width,
        places=smem,
        name="combine",
    )
    got = send_blocks([send1, send2, send3])
    out_rows = exchange(after(out_cat, own))
    shared_sum = lax.psum_scatter(
        after(shared_grads, own), "expert", scatter_dimension=0, tiled=True
    )
    mixed_sum = (
        own
        + got[0][:, :piece].astype(F32)
        + got[1][:, :piece].astype(F32)
        + got[2][:, :piece].astype(F32)
    ).astype(BF16)
    keep, passed, middle_grad, own, send1, send2, send3 = run(
        attend_back_kernel,
        [
            ((owners // 2, shard, outer + 2 * NOPE + LANES), BF16),
            ((owners // 2, shard, outer + 2 * NOPE + LANES), BF16),
            ((tokens, width), F32),
            ((tokens, piece), F32),
            ((tokens, piece), BF16),
            ((tokens, piece), BF16),
            ((tokens, piece), BF16),
        ],
        [
            me,
            core,
            stream,
            cotangent,
            middle,
            *share_small(mixed_sum),
            *got,
            probs_own,
            router_probs,
            one,
            router_block,
            mixed,
            normed,
            query,
            expanded,
            key,
            latent,
            compressed,
            probs,
            attended,
            gain_rows,
            latent_gain_rows,
            cosine,
            sine,
        ],
        2 * tokens * width * (3 * edge + 2 * outer),
        scratch=[
            pltpu.VMEM((width, outer + 2 * NOPE + LANES), BF16),
            pltpu.VMEM((tokens, edge), BF16),
            pltpu.VMEM((tokens, width), F32),
            pltpu.VMEM((width, outer + 2 * NOPE), BF16),
            pltpu.VMEM(normed.shape, BF16),
            pltpu.VMEM(query.shape, BF16),
            pltpu.VMEM(expanded.shape, BF16),
            pltpu.VMEM(compressed.shape, F32),
            pltpu.VMEM(probs.shape, F32),
            pltpu.SemaphoreType.DMA((4,)),
            pltpu.SemaphoreType.DMA((7,)),
        ],
        places={0: pltpu.SMEM, 1: pltpu.SMEM} | {i: pl.ANY for i in (14, 17, 18, 19, 22, 23)},
        out_places={0: pl.ANY, 1: pl.ANY},
        name="attend_back",
    )
    paired = lax.ppermute(after(passed, out_rows), "expert", [(i, i ^ 1) for i in range(owners)])
    side = 4
    chip = lax.axis_index("expert") // 2
    at = jnp.stack([chip // side, lax.rem(chip, side)]).astype(jnp.int32)
    columns = outer + 2 * NOPE + LANES
    cut = columns // 2

    def along(group, array, step):
        def target(i):
            x, z, core = i // (2 * side), i // 2 % side, i % 2
            if group == 0:
                x = (x + step) % side
            else:
                z = (z + step) % side
            return (x * side + z) * 2 + core

        return lax.ppermute(array, "expert", [(i, target(i)) for i in range(owners)])

    widths = [cut, columns - cut]
    along_z, *along_x = run(
        pair_kernel,
        [((side, side, shard, widths[1]), BF16)] + [((side, shard, cut), BF16)] * side,
        [at, keep, paired],
        0,
        places=smem,
        name="pair",
    )
    came_z = lax.all_to_all(
        along_z.reshape(side, side * shard, widths[1]),
        "expert",
        split_axis=0,
        concat_axis=0,
        tiled=True,
        axis_index_groups=[[(x * side + z) * 2 + c for z in range(side)] for x in range(side) for c in range(2)],
    ).reshape(along_z.shape)
    came_x = [along_x[0]] + [along(0, along_x[step], step) for step in range(1, side)]
    parts = []
    for group, came in enumerate((came_x, [came_z])):
        crossed = run(
            functools.partial(cross_kernel, group),
            [((shard, widths[group]), F32)] + [((shard, widths[group]), BF16)] * (side - 1),
            [at, *came],
            0,
            places=smem,
            name="cross",
        )
        parts += [crossed[0]] + [along(1 - group, crossed[step], step) for step in range(1, side)]
    shared_sum = shared_sum.astype(F32)
    gate_sum = shared_sum[:, :hidden_columns]
    up_sum = shared_sum[:, hidden_columns : 2 * hidden_columns]
    down_sum = shared_sum[:, 2 * hidden_columns :]
    parts[0] = after(parts[0], gate_sum, up_sum, down_sum)
    query_grad, late, output_grad, latent_up_grad, router_grad = run(
        unpack_kernel,
        [
            (query_proj.shape, F32),
            ((shard, edge - queries), F32),
            ((shard, heads * VDIM), F32),
            (latent_up.shape, F32),
            (router_proj.shape, F32),
        ],
        parts,
        0,
        scratch=[pltpu.VMEM((shard, columns), F32)],
        name="unpack",
    )
    got = send_blocks([send1, send2, send3])
    first_sum = (own + got[0].astype(F32) + got[1].astype(F32) + got[2].astype(F32)).astype(BF16)
    (stream_grad,) = run(
        stream_kernel,
        [((tokens, width), F32)],
        [after(me, late), middle_grad, stream, gain_rows, *share_small(first_sum)],
        0,
        scratch=[pltpu.VMEM((tokens, width), F32)],
        places=smem,
        name="stream",
    )

    (branch,) = run(
        routed_kernel,
        [((tokens, piece), BF16)],
        [t0, t1, out_rows, shared_own, *shared_got],
        4 * tokens * rows * piece,
        name="routed",
    )
    (result,) = run(
        result_kernel,
        [((tokens, width), F32)],
        [after(me, late), middle, *share_small(branch)],
        0,
        places=smem,
        name="result",
    )

    latent_down_grad, gain_grads = run(
        late_kernel,
        [(latent_down.shape, F32), ((8, LANES), F32)],
        [late, *(shift(late.astype(BF16), step) for step in range(1, tensors))],
        0,
        name="late",
    )
    return (
        result,
        stream_grad,
        gain_grads[0, :shard],
        query_grad,
        latent_down_grad,
        gain_grads[2, :short],
        latent_up_grad,
        output_grad.T,
        gain_grads[1, :shard],
        router_grad,
        gate_sum,
        up_sum,
        down_sum.T,
        gate_grad.transpose(0, 2, 1),
        up_grad.transpose(0, 2, 1),
        down_grad,
    )


def solution(mesh):
    placed = (
        P("expert", None),
        P("expert", None),
        P("expert", None),
        P("expert"),
        P("expert", "tensor"),
        P("expert", None),
        P("expert"),
        P("expert", "tensor"),
        P("tensor", "expert"),
        P("expert"),
        P("expert", None),
        P("expert", "tensor"),
        P("expert", "tensor"),
        P("tensor", "expert"),
        P("expert", None, "tensor"),
        P("expert", None, "tensor"),
        P("expert", "tensor", None),
        P("expert", None),
    )
    return jax.shard_map(
        per_device,
        mesh=mesh,
        in_specs=placed,
        out_specs=(
            P("expert", None),
            P("expert", None),
            P("expert"),
            P("expert", "tensor"),
            P("expert", None),
            P("expert"),
            P("expert", "tensor"),
            P("tensor", "expert"),
            P("expert"),
            P("expert", None),
            P("expert", "tensor"),
            P("expert", "tensor"),
            P("tensor", "expert"),
            P("expert", None, "tensor"),
            P("expert", None, "tensor"),
            P("expert", "tensor", None),
        ),
        check_vma=False,
    )
```

```python
import functools
import math

import jax
import jax.numpy as jnp
from jax import lax
from jax.experimental import pallas as pl
from jax.experimental.pallas import tpu as pltpu
from jax.sharding import PartitionSpec as P

NOPE = 128
ROPE = 64
VDIM = 128
LATENT = 512
TOPK = 6
EPSILON = 1e-06
ROTARY_BASE = 10000.0

BF16 = jnp.bfloat16
F32 = jnp.float32
VMEM_BYTES = 60 * 1024 * 1024
LANES = 128
COST_SCALE = 10


def dot_nn(left, right):
    return lax.dot_general(left, right, (((1,), (0,)), ((), ())), preferred_element_type=F32)


def dot_nt(left, right):
    return lax.dot_general(left, right, (((1,), (1,)), ((), ())), preferred_element_type=F32)


def dot_tn(left, right):
    return lax.dot_general(left, right, (((0,), (0,)), ((), ())), preferred_element_type=F32)


def silu_parts(pre_values):
    sigmoid_value = 1.0 / (1.0 + jnp.exp(-pre_values))
    return (pre_values * sigmoid_value, sigmoid_value * (1.0 + pre_values * (1.0 - sigmoid_value)))


def inverse_rms(values):
    return lax.rsqrt(jnp.mean(values * values, axis=-1, keepdims=True) + EPSILON)


def rms_back(values, scale, gain, grad):
    normed = values * scale
    weighted = grad * gain
    return (
        scale * (weighted - normed * jnp.mean(weighted * normed, axis=-1, keepdims=True)),
        grad * normed,
    )


def turned(values):
    width = values.shape[1]
    lane = lax.broadcasted_iota(jnp.int32, values.shape, 1) % ROPE
    half = ROPE // 2
    return jnp.where(
        lane < half, pltpu.roll(values, width - half, 1), pltpu.roll(values, half, 1)
    )


def rotated(values, cosine, sine):
    return values * cosine + turned(values) * sine


def block_at(me, step, count, width):
    return pl.ds(pl.multiple_of(lax.rem(me + step, count) * width, width), width)


def run(kernel, outs, args, flops, scratch=(), name=None, places=None, aliases=None, out_places=None):
    places = places or {}
    out_places = out_places or {}
    in_specs = [pl.BlockSpec(memory_space=places.get(i, pltpu.VMEM)) for i in range(len(args))]
    out_specs = [pl.BlockSpec(memory_space=out_places.get(i, pltpu.VMEM)) for i in range(len(outs))]
    moved = sum(a.size * a.dtype.itemsize for a in args) + sum(
        math.prod(shape) * jnp.dtype(dtype).itemsize for shape, dtype in outs
    )
    return pl.pallas_call(
        kernel,
        in_specs=in_specs,
        out_specs=out_specs,
        out_shape=[jax.ShapeDtypeStruct(shape, dtype) for shape, dtype in outs],
        scratch_shapes=list(scratch),
        input_output_aliases=aliases or {},
        compiler_params=pltpu.CompilerParams(vmem_limit_bytes=VMEM_BYTES),
        cost_estimate=pl.CostEstimate(
            flops=flops // COST_SCALE, bytes_accessed=moved // COST_SCALE, transcendentals=0
        ),
        name=name,
    )(*args)


def pack_kernel(
    first_ref, second_ref, latent_gain_ref, query_ref, down_ref, router_ref, output_ref, up_ref, out_ref
):
    shard = query_ref.shape[0]
    short = up_ref.shape[0]
    heads = up_ref.shape[1] // (2 * NOPE)
    nope = heads * NOPE
    queries = nope + heads * ROPE
    edge = queries + LATENT + LANES
    outer = edge + output_ref.shape[1]
    for head in range(heads):
        start = head * (NOPE + ROPE)
        out_ref[:, head * NOPE : (head + 1) * NOPE] = query_ref[:, start : start + NOPE]
        out_ref[:, nope + head * ROPE : nope + (head + 1) * ROPE] = query_ref[
            :, start + NOPE : start + NOPE + ROPE
        ]
        out_ref[head * short : (head + 1) * short, outer : outer + 2 * NOPE] = up_ref[
            :, head * 2 * NOPE : (head + 1) * 2 * NOPE
        ]
    out_ref[:, queries : queries + LATENT + ROPE] = down_ref[...]
    out_ref[:, queries + LATENT + ROPE : edge] = router_ref[...]
    out_ref[:, edge:outer] = output_ref[...]
    sub = lax.broadcasted_iota(jnp.int32, (LANES, LANES), 0)
    lane = lax.broadcasted_iota(jnp.int32, (LANES, LANES), 1)
    rows = jnp.zeros((LANES, LANES), F32)
    for index, g_ref in enumerate((first_ref, second_ref, latent_gain_ref)):
        gain = jnp.concatenate([g_ref[...].astype(F32), jnp.zeros((1, LANES - shard), F32)], axis=1)
        rows = jnp.where((sub == index) & (lane < shard), gain, rows)
    out_ref[:, outer + 2 * NOPE :] = rows.T[:shard, : out_ref.shape[1] - outer - 2 * NOPE].astype(BF16)


def routing_kernel(me_ref, ids_ref, cot_ref, t0_ref, t1_ref, s0_ref, s1_ref, low_ref, out_ref):
    choices, tokens = ids_ref.shape
    owners, local, capacity, piece = out_ref.shape
    experts = owners * local
    rows = owners * capacity
    expert = lax.broadcasted_iota(jnp.int32, (experts, tokens), 0)
    chosen = jnp.zeros((experts, tokens), F32)
    for choice in range(choices):
        chosen += jnp.where(ids_ref[choice : choice + 1, :] == expert, 1.0, 0.0)
    before = jnp.where(
        lax.broadcasted_iota(jnp.int32, (tokens, tokens), 0)
        < lax.broadcasted_iota(jnp.int32, (tokens, tokens), 1),
        1.0,
        0.0,
    ).astype(BF16)
    place = dot_nn(chosen.astype(BF16), before)
    place = jnp.where(chosen > 0.5, place, -1.0).astype(BF16)
    low = cot_ref[...].astype(BF16)
    low_ref[...] = low
    mine = cot_ref[:, block_at(me_ref[0], 0, cot_ref.shape[1] // piece, piece)].astype(BF16)
    slot = (lax.broadcasted_iota(jnp.int32, (tokens, rows), 1) % capacity).astype(F32)
    for index, (t_ref, s_ref) in enumerate(((t0_ref, s0_ref), (t1_ref, s1_ref))):
        spread = jnp.where(
            lax.broadcasted_iota(jnp.int32, (experts, rows), 0)
            == lax.broadcasted_iota(jnp.int32, (experts, rows), 1) // capacity * local + index,
            1.0,
            0.0,
        ).astype(BF16)
        wanted = dot_tn(place, spread)
        matrix = jnp.where(wanted == slot, 1.0, 0.0).astype(BF16)
        t_ref[...] = matrix
        by_slot = matrix.T
        s_ref[...] = by_slot
        out_ref[:, index] = dot_nn(by_slot, mine).astype(BF16).reshape(owners, capacity, piece)


def attend_kernel(
    me_ref,
    stream_ref,
    w_ref,
    seg_row_ref,
    seg_col_ref,
    cos_ref,
    sin_ref,
    own_ref,
    send1_ref,
    send2_ref,
    send3_ref,
    normed_ref,
    query_ref,
    expanded_ref,
    key_ref,
    latent_ref,
    compressed_ref,
    probs_ref,
    attended_ref,
    gains_ref,
    latent_gain_ref,
):
    heads, tokens, _ = probs_ref.shape
    width = stream_ref.shape[1]
    piece = own_ref.shape[1]
    nope = heads * NOPE
    queries = nope + heads * ROPE
    edge = queries + LATENT + LANES
    outer = edge + heads * VDIM
    owners = 32
    columns = jnp.concatenate(
        [w_ref[:, outer + 2 * NOPE :].astype(F32), jnp.zeros((width, ROPE), F32)], axis=1
    )
    gains = columns.T[:8, :]
    gains_ref[...] = gains
    shard = width // owners
    short = LATENT // owners
    latent_gain = (
        columns.reshape(owners, shard, LANES)[:, :short, :].reshape(LATENT, LANES).T[:8, :]
    )
    latent_gain_ref[...] = latent_gain
    stream = stream_ref[...].astype(F32)
    normed = (stream * inverse_rms(stream) * gains[0:1, :]).astype(BF16)
    normed_ref[...] = normed
    projected = dot_nn(normed, w_ref[:, :edge])
    query_ref[:, :nope] = projected[:, :nope].astype(BF16)
    query_ref[:, nope:] = rotated(projected[:, nope:queries], cos_ref[...], sin_ref[...]).astype(BF16)
    compressed = projected[:, queries : queries + LATENT]
    compressed_ref[...] = compressed
    latent = (compressed * inverse_rms(compressed) * latent_gain[2:3, :]).astype(BF16)
    latent_ref[...] = latent
    raw_key = projected[:, queries + LATENT : edge]
    key = rotated(raw_key, cos_ref[:, :LANES], sin_ref[:, :LANES])
    lane = lax.broadcasted_iota(jnp.int32, key.shape, 1)
    key = jnp.where(lane < ROPE, key, 0.0)
    key_low = key.astype(BF16)
    key_odd = pltpu.roll(key, ROPE, 1).astype(BF16)
    key_ref[...] = key_low
    row = lax.broadcasted_iota(jnp.int32, (tokens, tokens), 0)
    column = lax.broadcasted_iota(jnp.int32, (tokens, tokens), 1)
    allowed = (seg_col_ref[...] == seg_row_ref[...]) & (column <= row)
    scale = (NOPE + ROPE) ** (-0.5)
    for head in range(heads):
        block = slice(head * 2 * NOPE, (head + 1) * 2 * NOPE)
        up = w_ref[:, outer : outer + 2 * NOPE].reshape(owners, heads, short, 2 * NOPE)[:, head]
        up = up.reshape(LATENT, 2 * NOPE)
        expanded = dot_nn(latent, up).astype(BF16)
        expanded_ref[:, block] = expanded
        pair = nope + head // 2 * LANES
        raw = dot_nt(query_ref[:, head * NOPE : (head + 1) * NOPE], expanded[:, :NOPE]) + dot_nt(
            query_ref[:, pair : pair + LANES], key_odd if head % 2 else key_low
        )
        scores = jnp.where(allowed, raw * scale, -1e30)
        weight = jnp.exp(scores - jnp.max(scores, axis=-1, keepdims=True))
        probs = weight / jnp.sum(weight, axis=-1, keepdims=True)
        probs_ref[head] = probs
        attended_ref[:, head * VDIM : (head + 1) * VDIM] = dot_nn(
            probs.astype(BF16), expanded[:, NOPE:]
        ).astype(BF16)
    attended = attended_ref[...]
    for step, out_ref in enumerate((own_ref, send1_ref, send2_ref, send3_ref)):
        part = dot_nt(attended, w_ref[block_at(me_ref[0], step, width // piece, piece), edge:outer])
        out_ref[...] = part.astype(out_ref.dtype)


def dispatch_kernel(
    me_ref, stream_ref, a0_ref, a1_ref, a2_ref, a3_ref, gains_ref, s0_ref, s1_ref, middle_ref, mixed_ref, out_ref
):
    piece = a0_ref.shape[1]
    width = stream_ref.shape[1]
    count = width // piece
    owners, capacity, _ = out_ref.shape
    for step, a_ref in enumerate((a0_ref, a1_ref, a2_ref, a3_ref)):
        place = block_at(me_ref[0], step, count, piece)
        middle_ref[:, place] = stream_ref[:, place].astype(F32) + a_ref[...].astype(F32)
    middle = middle_ref[...]
    mixed = (middle * inverse_rms(middle) * gains_ref[1:2, :]).astype(BF16)
    mixed_ref[...] = mixed
    mine = mixed_ref[:, block_at(me_ref[0], 0, count, piece)]
    out_ref[:, :, width:] = dot_nn(s1_ref[...], mine).astype(BF16).reshape(owners, capacity, piece)
    out_ref[:, :, :width] = dot_nn(s0_ref[...], mixed).astype(BF16).reshape(owners, capacity, width)


def shared_kernel(
    me_ref,
    mixed_ref,
    cot_ref,
    w_ref,
    router_ref,
    own_ref,
    send1_ref,
    send2_ref,
    send3_ref,
    back_ref,
    probs_ref,
    grads_ref,
):
    width = mixed_ref.shape[1]
    piece = own_ref.shape[1]
    hidden_columns = w_ref.shape[1] // 3
    mixed = mixed_ref[...]
    cot = cot_ref[...]
    pre = dot_nn(mixed, w_ref[:, : 2 * hidden_columns])
    gate_pre, up_pre = pre[:, :hidden_columns], pre[:, hidden_columns:]
    act, slope = silu_parts(gate_pre)
    hidden = (act * up_pre).astype(BF16)
    hidden_grad = dot_nn(cot, w_ref[:, 2 * hidden_columns :])
    pair = jnp.concatenate([hidden_grad * up_pre * slope, hidden_grad * act], axis=1).astype(BF16)
    grads_ref[:, : 2 * hidden_columns] = dot_tn(mixed, pair).astype(BF16)
    grads_ref[:, 2 * hidden_columns :] = dot_tn(cot, hidden).astype(BF16)
    back_ref[...] = dot_nt(pair, w_ref[:, : 2 * hidden_columns])
    logits = dot_nn(mixed, router_ref[...])
    lane = lax.broadcasted_iota(jnp.int32, logits.shape, 1)
    logits = jnp.where(lane >= ROPE, logits, -1e30)
    weight = jnp.exp(logits - jnp.max(logits, axis=-1, keepdims=True))
    probs_ref[...] = weight / jnp.sum(weight, axis=-1, keepdims=True)
    for step, out_ref in enumerate((own_ref, send1_ref, send2_ref, send3_ref)):
        place = block_at(me_ref[0], step, width // piece, piece)
        part = dot_nt(hidden, w_ref[place, 2 * hidden_columns :])
        out_ref[...] = part.astype(out_ref.dtype)


def expert_back_kernel(split, *refs):
    if split:
        me_ref, base_ref, x0_ref, x1_ref, x2_ref, x3_ref = refs[:6]
        refs = refs[6:]
    else:
        me_ref, base_ref, x_ref = refs[:3]
        refs = refs[3:]
    c0_ref, c1_ref, c2_ref, c3_ref, wg_ref, wu_ref, wd_ref, router_ref = refs[:8]
    refs = refs[8:]
    if split:
        back_ref, c_ref, hg_ref, gr_ref, ur_ref, x_ref, wide_ref, down_ref, tall_ref = refs
    else:
        back_ref, c_ref, hg_ref, gr_ref, ur_ref, wide_ref, down_ref, tall_ref = refs
    sources, capacity, width = c_ref.shape
    rows = sources * capacity
    piece = c0_ref.shape[-1]
    count = width // piece
    hidden_columns = wd_ref.shape[1]
    padded = down_ref.shape[1]
    me = me_ref[0]

    @pl.when(pl.program_id(0) == 0)
    def _():
        rest = jnp.zeros((padded - hidden_columns, width), BF16)
        gate_up = jnp.concatenate([wg_ref[0], rest, wu_ref[0], rest], axis=0)
        tall_ref[...] = gate_up
        wide_ref[...] = gate_up.T
        down_ref[...] = jnp.concatenate([wd_ref[0], rest], axis=0).T

    for step, p_ref in enumerate((c0_ref, c1_ref, c2_ref, c3_ref)):
        c_ref[:, :, block_at(me, step, count, piece)] = p_ref[:, 0]
    if split:
        for step, p_ref in enumerate((x0_ref, x1_ref, x2_ref, x3_ref)):
            x_ref[:, :, block_at(me, step, count, piece)] = p_ref[...]
    x = x_ref[...].reshape(rows, width)
    expert = base_ref[0] + (1 if split else 0) + ROPE
    logits = dot_nn(x, router_ref[...])
    lane = lax.broadcasted_iota(jnp.int32, logits.shape, 1)
    logits = jnp.where(lane >= ROPE, logits, -1e30)
    weight = jnp.exp(logits - jnp.max(logits, axis=-1, keepdims=True))
    gate = jnp.sum(jnp.where(lane == expert, weight, 0.0), axis=-1, keepdims=True) / jnp.sum(
        weight, axis=-1, keepdims=True
    )
    pre = dot_nn(x, wide_ref[...])
    gate_pre, up_pre = pre[:, :padded], pre[:, padded:]
    hidden_cot = dot_nn(c_ref[...].reshape(rows, width), down_ref[...])
    act, slope = silu_parts(gate_pre)
    hidden = (act * up_pre).astype(BF16).astype(F32)
    gate_grad = jnp.sum(hidden * hidden_cot, axis=-1, keepdims=True)
    hidden_grad = gate * hidden_cot
    gate_rows = (hidden_grad * up_pre * slope).astype(BF16)
    up_rows = (hidden_grad * act).astype(BF16)
    hg_ref[...] = (gate * hidden).astype(BF16)[:, :hidden_columns]
    gr_ref[...] = gate_rows[:, :hidden_columns]
    ur_ref[...] = up_rows[:, :hidden_columns]
    high = gate_grad.astype(BF16).astype(F32)
    low = gate_grad - high
    beside = jnp.where(lane == 0, high, 0.0) + jnp.where(lane == 1, low, 0.0)
    back = dot_nn(jnp.concatenate([gate_rows, up_rows], axis=1), tall_ref[...])
    back_ref[:, :, :width] = back.astype(BF16).reshape(sources, capacity, width)
    back_ref[:, :, width:] = beside.astype(BF16).reshape(sources, capacity, LANES)


def expert_back(split, me, base, xs, cs, wg, wu, wd, router, router_at, chunk):
    owners, local, capacity, piece = cs[0].shape
    hidden, width = wg.shape[1:]
    local_index = 1 if split else 0
    rows = owners * capacity
    padded = -(-hidden // LANES) * LANES
    scalar = pl.BlockSpec(memory_space=pltpu.SMEM)
    row_spec = pl.BlockSpec((chunk * capacity, hidden), lambda c: (c, 0))
    row_shape = jax.ShapeDtypeStruct((rows, hidden), BF16)
    wide_spec = pl.BlockSpec((chunk, capacity, width), lambda c: (c, 0, 0))
    wide_shape = jax.ShapeDtypeStruct((owners, capacity, width), BF16)
    narrow_spec = pl.BlockSpec((chunk, capacity, piece), lambda c: (c, 0, 0))
    own_spec = pl.BlockSpec((chunk, capacity, piece), lambda c: (c, 0, width // piece))
    cot_spec = pl.BlockSpec((chunk, 1, capacity, piece), lambda c: (c, local_index, 0, 0))
    weight_spec = pl.BlockSpec((1, hidden, width), lambda c: (local_index, 0, 0))
    in_specs = [scalar, scalar]
    in_specs += [own_spec] + [narrow_spec] * 3 if split else [wide_spec]
    in_specs += [cot_spec] * 4 + [weight_spec] * 3 + [pl.BlockSpec((width, LANES), lambda c: (0, router_at))]
    out_specs = [pl.BlockSpec((chunk, capacity, width + LANES), lambda c: (c, 0, 0)), wide_spec]
    out_shape = [jax.ShapeDtypeStruct((owners, capacity, width + LANES), BF16), wide_shape]
    last_spec, last_shape = ([wide_spec], [wide_shape]) if split else ([], [])
    return pl.pallas_call(
        functools.partial(expert_back_kernel, split),
        grid=(owners // chunk,),
        in_specs=in_specs,
        out_specs=out_specs + [row_spec] * 3 + last_spec,
        out_shape=out_shape + [row_shape] * 3 + last_shape,
        scratch_shapes=[
            pltpu.VMEM((width, 2 * padded), BF16),
            pltpu.VMEM((width, padded), BF16),
            pltpu.VMEM((2 * padded, width), BF16),
        ],
        compiler_params=pltpu.CompilerParams(vmem_limit_bytes=VMEM_BYTES),
        cost_estimate=pl.CostEstimate(
            flops=100 * rows * hidden * width, bytes_accessed=24 * 1024 * 1024, transcendentals=0
        ),
        name="expert_back",
    )(me, base, *xs, *cs, wg, wu, wd, router)


def expert_out_kernel(hg_ref, wd_ref, out_ref):
    pieces, sources, capacity, piece = out_ref.shape
    out = dot_nn(hg_ref[...], wd_ref[0]).astype(BF16)
    for index in range(pieces):
        out_ref[index] = out[:, index * piece : (index + 1) * piece].reshape(sources, capacity, piece)


def expert_out(expert, hg, wd, owners, pieces, chunk):
    rows, hidden = hg.shape
    width = wd.shape[2]
    capacity = rows // owners
    piece = width // pieces
    return pl.pallas_call(
        expert_out_kernel,
        grid=(owners // chunk,),
        in_specs=[
            pl.BlockSpec((chunk * capacity, hidden), lambda c: (c, 0)),
            pl.BlockSpec((1, hidden, width), lambda c: (expert, 0, 0)),
        ],
        out_specs=pl.BlockSpec((pieces, chunk, capacity, piece), lambda c: (0, c, 0, 0)),
        out_shape=jax.ShapeDtypeStruct((pieces, owners, capacity, piece), BF16),
        compiler_params=pltpu.CompilerParams(vmem_limit_bytes=VMEM_BYTES),
        cost_estimate=pl.CostEstimate(
            flops=rows * hidden * width // 5, bytes_accessed=6 * 1024 * 102, transcendentals=0
        ),
        name="expert_out",
    )(hg, wd)


def expert_grads_kernel(
    x0_ref, c0_ref, hg0_ref, gr0_ref, ur0_ref, x1_ref, c1_ref, hg1_ref, gr1_ref, ur1_ref, dg_ref, du_ref, dd_ref
):
    owners, capacity, piece = x0_ref.shape
    rows = owners * capacity

    def step(x_ref, c_ref, hg_ref, gr_ref, ur_ref):
        x = x_ref[...].reshape(rows, piece)
        dg_ref[0] = dot_tn(gr_ref[...], x)
        du_ref[0] = dot_tn(ur_ref[...], x)
        dd_ref[0] = dot_tn(hg_ref[...], c_ref[...].reshape(rows, piece))

    pl.when(pl.program_id(0) == 0)(lambda: step(x0_ref, c0_ref, hg0_ref, gr0_ref, ur0_ref))
    pl.when(pl.program_id(0) == 1)(lambda: step(x1_ref, c1_ref, hg1_ref, gr1_ref, ur1_ref))


def expert_grads(first, second, pieces):
    owners, capacity, width = first[1].shape
    rows, hidden = first[2].shape
    piece = width // pieces
    row_spec = pl.BlockSpec((rows, hidden), lambda e, j: (0, 0))

    def specs(expert):
        stay = 0 if expert else pieces - 1
        wide = pl.BlockSpec(
            (owners, capacity, piece), lambda e, j: (0, 0, jnp.where(e == expert, j, stay))
        )
        return [wide, wide, row_spec, row_spec, row_spec]

    out_spec = pl.BlockSpec((1, hidden, piece), lambda e, j: (e, 0, j))
    out_shape = jax.ShapeDtypeStruct((2, hidden, width), F32)
    return pl.pallas_call(
        expert_grads_kernel,
        grid=(2, pieces),
        in_specs=specs(0) + specs(1),
        out_specs=[out_spec] * 3,
        out_shape=[out_shape] * 3,
        compiler_params=pltpu.CompilerParams(vmem_limit_bytes=VMEM_BYTES),
        cost_estimate=pl.CostEstimate(
            flops=rows * hidden * width, bytes_accessed=40 * 1024 * 102, transcendentals=0
        ),
        name="expert_grads",
    )(*first, *second)


def slot_probs(t_ref, b_ref, index, width):
    owners, capacity, _ = b_ref.shape
    rows = owners * capacity
    beside = b_ref[:, :, width:].reshape(rows, LANES).astype(F32)
    lane = lax.broadcasted_iota(jnp.int32, (rows, LANES), 1)
    expert = 2 * (lax.broadcasted_iota(jnp.int32, (rows, LANES), 0) // capacity) + index
    spread = jnp.where(lane == expert + ROPE, beside[:, 0:1], 0.0) + jnp.where(
        lane == expert, beside[:, 1:2], 0.0
    )
    return dot_nn(t_ref[...], spread.astype(BF16))


def combine_first_kernel(t_ref, b_ref, shared_ref, sum_ref, probs_ref):
    owners, capacity, _ = b_ref.shape
    width = shared_ref.shape[1]
    probs_ref[...] = slot_probs(t_ref, b_ref, 0, width)
    sum_ref[...] = shared_ref[...] + dot_nn(t_ref[...], b_ref[:, :, :width].reshape(owners * capacity, width))


def combine_kernel(
    me_ref, t_ref, b_ref, sum_ref, first_probs_ref, own_ref, probs_ref, send1_ref, send2_ref, send3_ref
):
    owners, capacity, _ = b_ref.shape
    rows = owners * capacity
    width = sum_ref.shape[1]
    piece = own_ref.shape[1]
    probs = first_probs_ref[...] + slot_probs(t_ref, b_ref, 1, width)
    probs = probs + pltpu.roll(probs, ROPE, 1)
    probs_ref[...] = probs
    high = probs.astype(BF16)
    low = (probs - high.astype(F32)).astype(BF16)
    short = lax.broadcasted_iota(jnp.int32, probs.shape, 1)
    message = jnp.where(short >= ROPE, high.astype(F32), low.astype(F32)).astype(BF16)
    for step, out_ref in enumerate((own_ref, send1_ref, send2_ref, send3_ref)):
        place = block_at(me_ref[0], step, width // piece, piece)
        part = sum_ref[:, place] + dot_nn(t_ref[...], b_ref[:, :, place].reshape(rows, piece))
        if step == 0:
            own_ref[...] = part
        else:
            out_ref[:, :piece] = part.astype(BF16)
            out_ref[:, piece:] = message


def attend_back_kernel(
    me_ref,
    core_ref,
    stream_ref,
    cot_ref,
    middle_ref,
    a0_ref,
    a1_ref,
    a2_ref,
    a3_ref,
    r1_ref,
    r2_ref,
    r3_ref,
    probs_own_ref,
    router_probs_ref,
    w_in,
    router_ref,
    mixed_ref,
    normed_in,
    query_in,
    expanded_in,
    key_ref,
    latent_ref,
    compressed_in,
    probs_in,
    attended_ref,
    gains_ref,
    latent_gain_ref,
    cos_ref,
    sin_ref,
    keep_ref,
    pass_ref,
    middle_grad_ref,
    own_ref,
    send1_ref,
    send2_ref,
    send3_ref,
    scr_ref,
    low_ref,
    wide_ref,
    w_ref,
    normed_ref,
    query_ref,
    expanded_ref,
    compressed_ref,
    probs_ref,
    sems,
    in_sems,
):
    heads, tokens, _ = probs_ref.shape
    width = stream_ref.shape[1]
    piece = own_ref.shape[1]
    nope = heads * NOPE
    queries = nope + heads * ROPE
    edge = queries + LATENT + LANES
    outer = edge + heads * VDIM
    owners = 32
    shard = width // owners
    short = LATENT // owners
    count = width // piece
    me = me_ref[0]
    copies = []
    for source, target in (
        (w_in.at[:, edge : outer + 2 * NOPE], w_ref.at[:, edge:]),
        (probs_in, probs_ref),
        (expanded_in, expanded_ref),
        (query_in, query_ref),
        (compressed_in, compressed_ref),
        (w_in.at[:, :edge], w_ref.at[:, :edge]),
        (normed_in, normed_ref),
    ):
        copies.append(pltpu.make_async_copy(source, target, in_sems.at[len(copies)]))
        copies[-1].start()
    probs_grad = probs_own_ref[...]
    for r_ref in (r1_ref, r2_ref, r3_ref):
        other = r_ref[:, piece:].astype(F32)
        probs_grad = probs_grad + other + pltpu.roll(other, ROPE, 1)
    router_probs = router_probs_ref[...]
    logits_low = (
        router_probs * (probs_grad - jnp.sum(router_probs * probs_grad, axis=-1, keepdims=True))
    ).astype(BF16)
    router_back = dot_nt(logits_low, router_ref[...])
    for step, a_ref in enumerate((a0_ref, a1_ref, a2_ref, a3_ref)):
        wide_ref[:, block_at(me, step, count, piece)] = a_ref[...].astype(F32)
    mixed_grad = wide_ref[...] + router_back
    middle = middle_ref[...]
    norm_grad, second_gain_rows = rms_back(middle, inverse_rms(middle), gains_ref[1:2, :], mixed_grad)
    second_gain_grad = jnp.sum(second_gain_rows, axis=0, keepdims=True)
    middle_grad = cot_ref[...] + norm_grad
    middle_grad_ref[...] = middle_grad
    middle_low = middle_grad.astype(BF16)
    core = core_ref[0]
    router_grad = dot_tn(mixed_ref[...], logits_low)
    scr_ref[:, outer + 2 * NOPE :] = pltpu.roll(router_grad, ROPE, 1).astype(BF16)
    scr_ref[:, edge:outer] = dot_tn(middle_low, attended_ref[...]).astype(BF16)
    copies[0].wait()
    attended_grad = dot_nn(middle_low, w_ref[:, edge:outer]).astype(BF16)
    for copy in copies[1:5]:
        copy.wait()
    scale = (NOPE + ROPE) ** (-0.5)
    key_low = key_ref[...]
    key_odd = pltpu.roll(key_low.astype(F32), ROPE, 1).astype(BF16)
    latent = latent_ref[...]
    latent_part = jnp.zeros((tokens, LATENT), F32)
    key_even_grad = jnp.zeros((tokens, LANES), F32)
    key_odd_grad = jnp.zeros((tokens, LANES), F32)
    rope_grads = []
    grads4 = scr_ref.reshape(owners, shard, scr_ref.shape[1])
    for head in range(heads):
        pair = nope + head // 2 * LANES
        expanded = expanded_ref[:, head * 2 * NOPE : (head + 1) * 2 * NOPE]
        probs = probs_ref[head]
        head_grad = attended_grad[:, head * VDIM : (head + 1) * VDIM]
        value_grad = dot_tn(probs.astype(BF16), head_grad)
        probs_att = dot_nt(head_grad, expanded[:, NOPE:])
        scores = probs * (probs_att - jnp.sum(probs * probs_att, axis=-1, keepdims=True))
        raw_low = (scores * scale).astype(BF16)
        low_ref[:, head * NOPE : (head + 1) * NOPE] = dot_nn(raw_low, expanded[:, :NOPE]).astype(BF16)
        turn_grad = dot_nn(raw_low, key_odd if head % 2 else key_low)
        if head % 2:
            rope_grads[-1] = rope_grads[-1] + turn_grad
            key_odd_grad += dot_tn(raw_low, query_ref[:, pair : pair + LANES])
        else:
            rope_grads.append(turn_grad)
            key_even_grad += dot_tn(raw_low, query_ref[:, pair : pair + LANES])
        key_grad = dot_tn(raw_low, query_ref[:, head * NOPE : (head + 1) * NOPE])
        expanded_low = jnp.concatenate([key_grad, value_grad], axis=1).astype(BF16)
        up = w_ref[:, outer : outer + 2 * NOPE].reshape(owners, heads, short, 2 * NOPE)[:, head]
        up = up.reshape(LATENT, 2 * NOPE)
        latent_part += dot_nt(expanded_low, up)
        grads4[:, head * short : (head + 1) * short, outer : outer + 2 * NOPE] = (
            dot_tn(latent, expanded_low).astype(BF16).reshape(owners, short, 2 * NOPE)
        )
    rope_grad = jnp.concatenate(rope_grads, axis=1)
    low_ref[:, nope:queries] = rotated(rope_grad, cos_ref[...], -sin_ref[...]).astype(BF16)
    compressed = compressed_ref[...]
    latent_grad, latent_gain_rows = rms_back(
        compressed, inverse_rms(compressed), latent_gain_ref[2:3, :], latent_part
    )
    latent_gain_grad = jnp.sum(latent_gain_rows, axis=0, keepdims=True)
    low_ref[:, queries : queries + LATENT] = latent_grad.astype(BF16)
    lane = lax.broadcasted_iota(jnp.int32, (tokens, LANES), 1)
    key_grad = jnp.where(lane < ROPE, key_even_grad + pltpu.roll(key_odd_grad, ROPE, 1), 0.0)
    key_grad = rotated(key_grad, cos_ref[:, :LANES], -sin_ref[:, :LANES])
    low_ref[:, queries + LATENT : edge] = jnp.where(lane < ROPE, key_grad, 0.0).astype(BF16)
    halves = scr_ref.reshape(owners // 2, 2, shard, scr_ref.shape[1])
    outgoing = [
        pltpu.make_async_copy(halves.at[:, 1 - core, :, edge:], pass_ref.at[:, :, edge:], sems.at[0]),
        pltpu.make_async_copy(halves.at[:, core, :, edge:], keep_ref.at[:, :, edge:], sems.at[1]),
    ]
    for copy in outgoing:
        copy.start()
    for copy in copies[5:]:
        copy.wait()
    low = low_ref[...]
    for step, out_ref in enumerate((own_ref, send1_ref, send2_ref, send3_ref)):
        place = block_at(me, step, count, piece)
        part = dot_nt(low, w_ref[place, :edge])
        wide_ref[:, place] = part
        out_ref[...] = part.astype(out_ref.dtype)
    stream = stream_ref[...].astype(F32)
    first_gain_grad = jnp.sum(wide_ref[...] * (stream * inverse_rms(stream)), axis=0, keepdims=True)
    late = dot_tn(normed_ref[...], low[:, queries:])
    sub = lax.broadcasted_iota(jnp.int32, (LANES, width), 0)
    gain_columns = (
        jnp.where(sub == ROPE, first_gain_grad, 0.0)
        + jnp.where(sub == ROPE + 1, second_gain_grad * (1.0 / count), 0.0)
    ).T
    key_columns = (late[:, LATENT:] + gain_columns).reshape(owners, shard, LANES)
    sub = lax.broadcasted_iota(jnp.int32, (LANES, LATENT), 0)
    latent_columns = jnp.where(sub == ROPE + 2, latent_gain_grad, 0.0).T.reshape(owners, short, LANES)
    grads4[:, :, queries : queries + LATENT] = (
        late[:, :LATENT].astype(BF16).reshape(owners, shard, LATENT)
    )
    grads4[:, :, queries + LATENT : edge] = key_columns.astype(BF16)
    grads4[:, :short, queries + LATENT : edge] = (key_columns[:, :short] + latent_columns).astype(BF16)
    scr_ref[:, :queries] = dot_tn(normed_ref[...], low[:, :queries]).astype(BF16)
    outgoing += [
        pltpu.make_async_copy(halves.at[:, 1 - core, :, :edge], pass_ref.at[:, :, :edge], sems.at[2]),
        pltpu.make_async_copy(halves.at[:, core, :, :edge], keep_ref.at[:, :, :edge], sems.at[3]),
    ]
    for copy in outgoing[2:]:
        copy.start()
    for copy in outgoing:
        copy.wait()


def pair_kernel(at_ref, keep_ref, got_ref, along_z_ref, *along_x_refs):
    side = len(along_x_refs)
    cut = along_x_refs[0].shape[2]

    def part(index, columns):
        return (keep_ref[index, :, columns].astype(F32) + got_ref[index, :, columns].astype(F32)).astype(BF16)

    for z in range(side):
        for x in range(side):
            along_z_ref[z, x] = part(x * side + z, slice(cut, None))
    for step, out_ref in enumerate(along_x_refs):
        peer = lax.rem(at_ref[0] + step, side)
        for other in range(side):
            out_ref[other] = part(peer * side + other, slice(0, cut))


def cross_kernel(group, at_ref, *refs):
    parts, out_refs = refs[:-4], refs[-4:]
    for step, out_ref in enumerate(out_refs):
        peer = lax.rem(at_ref[1 - group] + step, len(out_refs))
        if len(parts) == 1:
            rows = [parts[0][source, peer] for source in range(parts[0].shape[0])]
        else:
            rows = [r_ref[peer] for r_ref in parts]
        total = rows[0].astype(F32)
        for row in rows[1:]:
            total = total + row.astype(F32)
        out_ref[...] = total.astype(out_ref.dtype)


def unpack_kernel(*refs):
    query_ref, late_ref, output_ref, up_ref, router_ref, total_ref = refs[-6:]
    heads = up_ref.shape[1] // (2 * NOPE)
    short = up_ref.shape[0]
    nope = heads * NOPE
    queries = nope + heads * ROPE
    edge = queries + LATENT + LANES
    outer = edge + heads * VDIM
    start = 0
    for group in range(2):
        parts = refs[4 * group : 4 * group + 4]
        width = parts[0].shape[1]
        total = parts[0][...]
        for r_ref in parts[1:]:
            total = total + r_ref[...].astype(F32)
        total_ref[:, start : start + width] = total
        start += width
    total = total_ref[...]
    for head in range(heads):
        start = head * (NOPE + ROPE)
        query_ref[:, start : start + NOPE] = total[:, head * NOPE : (head + 1) * NOPE]
        query_ref[:, start + NOPE : start + NOPE + ROPE] = total[
            :, nope + head * ROPE : nope + (head + 1) * ROPE
        ]
        up_ref[:, head * 2 * NOPE : (head + 1) * 2 * NOPE] = total[
            head * short : (head + 1) * short, outer : outer + 2 * NOPE
        ]
    late_ref[...] = total[:, queries:edge]
    output_ref[...] = total[:, edge:outer]
    router_ref[...] = total[:, outer + 2 * NOPE : outer + 2 * NOPE + ROPE]


def late_kernel(own_ref, r1_ref, r2_ref, r3_ref, down_ref, gains_ref):
    total = own_ref[...]
    for r_ref in (r1_ref, r2_ref, r3_ref):
        total = total + r_ref[...].astype(F32)
    down_ref[...] = total[:, : down_ref.shape[1]]
    columns = total[:, LATENT:]
    columns = jnp.concatenate([columns, jnp.zeros(columns.shape, F32)], axis=0)
    gains_ref[...] = columns.T[ROPE : ROPE + 8, :]


def stream_kernel(me_ref, middle_grad_ref, stream_ref, gains_ref, a0_ref, a1_ref, a2_ref, a3_ref, out_ref, wide_ref):
    piece = a0_ref.shape[1]
    count = stream_ref.shape[1] // piece
    for step, a_ref in enumerate((a0_ref, a1_ref, a2_ref, a3_ref)):
        wide_ref[:, block_at(me_ref[0], step, count, piece)] = a_ref[...].astype(F32)
    stream = stream_ref[...].astype(F32)
    norm_grad, _ = rms_back(stream, inverse_rms(stream), gains_ref[0:1, :], wide_ref[...])
    out_ref[...] = middle_grad_ref[...] + norm_grad


def routed_kernel(t0_ref, t1_ref, o_ref, own_ref, r1_ref, r2_ref, r3_ref, out_ref):
    owners, _, capacity, piece = o_ref.shape
    rows = owners * capacity
    total = own_ref[...]
    for r_ref in (r1_ref, r2_ref, r3_ref):
        total = total + r_ref[...].astype(F32)
    for index, t_ref in ((0, t0_ref), (1, t1_ref)):
        total = total + dot_nn(t_ref[...], o_ref[:, index].reshape(rows, piece))
    out_ref[...] = total.astype(BF16)


def result_kernel(me_ref, middle_ref, a0_ref, a1_ref, a2_ref, a3_ref, out_ref):
    piece = a0_ref.shape[1]
    count = middle_ref.shape[1] // piece
    for step, a_ref in enumerate((a0_ref, a1_ref, a2_ref, a3_ref)):
        place = block_at(me_ref[0], step, count, piece)
        out_ref[:, place] = middle_ref[:, place] + a_ref[...].astype(F32)


def shift(array, step):
    size = lax.axis_size("tensor")
    return lax.ppermute(array, "tensor", [(i, (i + step) % size) for i in range(size)])


def send_blocks(sends):
    return [shift(array, step + 1) for step, array in enumerate(sends)]


def share_small(low):
    size = lax.axis_size("tensor")
    return [low] + [shift(low, size - step) for step in range(1, size)]


def ring_first(rows):
    return shift(rows, 1), shift(rows, lax.axis_size("tensor") - 1)


def ring_second(rows, before, after):
    half = rows.shape[0] // 2
    across = [shift(before[:half], 1), shift(after[half:], lax.axis_size("tensor") - 1)]
    return [rows, after, jnp.concatenate(across, axis=0), before]


def after(array, *others):
    return lax.optimization_barrier((array, *others))[0]


def exchange(rows):
    shape = rows.shape
    return lax.all_to_all(
        rows.reshape(shape[0], -1, shape[-1]), "expert", split_axis=0, concat_axis=0, tiled=True
    ).reshape(shape)


def per_device(
    stream,
    segment_ids,
    expert_ids,
    first_gain,
    query_proj,
    latent_down,
    latent_gain,
    latent_up,
    output_proj,
    second_gain,
    router_proj,
    shared_gate,
    shared_up,
    shared_down,
    expert_gate,
    expert_up,
    expert_down,
    cotangent,
):
    tokens, width = stream.shape
    owners = lax.axis_size("expert")
    tensors = lax.axis_size("tensor")
    shard = query_proj.shape[0]
    heads = query_proj.shape[1] // (NOPE + ROPE)
    short = latent_up.shape[0]
    experts = router_proj.shape[1]
    hidden_columns = shared_gate.shape[1]
    local, _, expert_hidden = expert_gate.shape
    capacity = tokens * TOPK * 4 // (3 * experts)
    rows = owners * capacity
    piece = width // tensors
    nope = heads * NOPE
    queries = nope + heads * ROPE
    edge = queries + LATENT + LANES
    outer = edge + heads * VDIM
    me = lax.axis_index("tensor").astype(jnp.int32).reshape(1)
    base = (lax.axis_index("expert") * local).astype(jnp.int32).reshape(1)
    core = lax.rem(lax.axis_index("expert"), 2).astype(jnp.int32).reshape(1)
    smem = {0: pltpu.SMEM}

    (pack_one,) = run(
        pack_kernel,
        [((shard, outer + 2 * NOPE + ROPE), BF16)],
        [
            first_gain.reshape(1, shard),
            second_gain.reshape(1, shard),
            jnp.pad(latent_gain, (0, shard - short)).reshape(1, shard),
            query_proj,
            latent_down,
            router_proj,
            output_proj.T,
            latent_up,
        ],
        0,
        name="pack",
    )
    pack_two = jnp.concatenate([shared_gate, shared_up, shared_down.T], axis=1)
    one = lax.all_gather(pack_one, "expert", axis=0, tiled=True)
    two = lax.all_gather(pack_two, "expert", axis=0, tiled=True)

    position = jnp.arange(tokens).astype(F32)
    exponent = jnp.arange(ROPE // 2).astype(F32) * (2.0 / ROPE)
    angles = position[:, None] * jnp.exp(-math.log(ROTARY_BASE) * exponent)[None, :]
    cosine = jnp.tile(jnp.cos(angles), (1, 2 * heads))
    sine = jnp.sin(angles)
    sine = jnp.tile(jnp.concatenate([-sine, sine], axis=1), (1, heads))

    t0, t1, s0, s1, cot_low, cot_out = run(
        routing_kernel,
        [
            ((tokens, rows), BF16),
            ((tokens, rows), BF16),
            ((rows, tokens), BF16),
            ((rows, tokens), BF16),
            ((tokens, width), BF16),
            ((owners, local, capacity, piece), BF16),
        ],
        [me, expert_ids.T, cotangent],
        2 * local * tokens * rows * (piece + experts),
        places=smem,
        name="routing",
    )

    cot_own = exchange(cot_out)
    cot_before, cot_after = ring_first(cot_own)
    (
        own,
        send1,
        send2,
        send3,
        normed,
        query,
        expanded,
        key,
        latent,
        compressed,
        probs,
        attended,
        gain_rows,
        latent_gain_rows,
    ) = run(
        attend_kernel,
        [
            ((tokens, piece), F32),
            ((tokens, piece), BF16),
            ((tokens, piece), BF16),
            ((tokens, piece), BF16),
            ((tokens, width), BF16),
            ((tokens, queries), BF16),
            ((tokens, heads * 2 * NOPE), BF16),
            ((tokens, LANES), BF16),
            ((tokens, LATENT), BF16),
            ((tokens, LATENT), F32),
            ((heads, tokens, tokens), F32),
            ((tokens, heads * VDIM), BF16),
            ((8, width), F32),
            ((8, LATENT), F32),
        ],
        [after(me, cot_own), stream, one, segment_ids, segment_ids.T, cosine, sine],
        2 * tokens * width * outer,
        places=smem,
        name="attend",
    )
    got = send_blocks([send1, send2, send3])
    attention = (own + got[0].astype(F32) + got[1].astype(F32) + got[2].astype(F32)).astype(BF16)
    attention = after(attention, cot_before, cot_after)
    middle, mixed, x_out = run(
        dispatch_kernel,
        [
            ((tokens, width), F32),
            ((tokens, width), BF16),
            ((owners, capacity, width + piece), BF16),
        ],
        [me, stream, *share_small(attention), gain_rows, s0, s1],
        2 * tokens * rows * (width + piece),
        places=smem,
        name="dispatch",
    )
    x_in = exchange(x_out)
    cots = ring_second(cot_own, cot_before, cot_after)
    x1s = x_in[:, :, width:]
    x1_before, x1_after = ring_first(x1s)
    x1s = [x_in] + ring_second(x1s, x1_before, x1_after)[1:]
    router_block = one[:, queries + LATENT : edge]
    (
        shared_own,
        shared1,
        shared2,
        shared3,
        shared_back,
        router_probs,
        shared_grads,
    ) = run(
        shared_kernel,
        [
            ((tokens, piece), F32),
            ((tokens, piece), BF16),
            ((tokens, piece), BF16),
            ((tokens, piece), BF16),
            ((tokens, width), F32),
            ((tokens, LANES), F32),
            ((width, 3 * hidden_columns), BF16),
        ],
        [me, mixed, cot_low, two, router_block],
        18 * tokens * width * hidden_columns,
        places=smem,
        name="shared",
    )
    base = after(base, shared_back)

    gate_t = expert_gate.transpose(0, 2, 1)
    up_t = expert_up.transpose(0, 2, 1)
    chunk = owners // 2
    back0, c0, hg0, gr0, ur0 = expert_back(
        False, me, base, [x_in], cots, gate_t, up_t, expert_down, one, edge // LANES - 1, chunk // 2
    )
    back0 = exchange(back0)
    back1, c1, hg1, gr1, ur1, x1 = expert_back(
        True, me, after(base, hg0), x1s, cots, gate_t, up_t, expert_down, one, edge // LANES - 1, chunk // 2
    )
    back1 = exchange(after(back1, back0))
    gr0 = after(gr0, back0)
    gate_grad, up_grad, down_grad = expert_grads(
        (x_in, c0, hg0, gr0, ur0), (x1, c1, hg1, gr1, ur1), tensors
    )
    out0 = expert_out(0, hg0, expert_down, owners, tensors, chunk)
    out1 = expert_out(1, after(hg1, out0), expert_down, owners, tensors, chunk)
    out_rows = [
        lax.psum_scatter(out, "tensor", scatter_dimension=0, tiled=True).reshape(owners, 1, capacity, piece)
        for out in (out0, out1)
    ]

    out_cat = jnp.concatenate(out_rows, axis=1)
    shared_got = send_blocks([after(shared1, back0), shared2, shared3])
    first_sum, first_probs = run(
        combine_first_kernel,
        [((tokens, width), F32), ((tokens, LANES), F32)],
        [t0, back0, shared_back],
        2 * tokens * rows * width,
        name="combine_first",
    )
    own, probs_own, send1, send2, send3 = run(
        combine_kernel,
        [
            ((tokens, piece), F32),
            ((tokens, LANES), F32),
            ((tokens, piece + LANES), BF16),
            ((tokens, piece + LANES), BF16),
            ((tokens, piece + LANES), BF16),
        ],
        [after(me, out_cat, gate_grad, *shared_got), t1, back1, first_sum, first_probs],
        2 * tokens * rows * width,
        places=smem,
        name="combine",
    )
    got = send_blocks([send1, send2, send3])
    out_rows = exchange(after(out_cat, own))
    shared_sum = lax.psum_scatter(
        after(shared_grads, own), "expert", scatter_dimension=0, tiled=True
    )
    mixed_sum = (
        own
        + got[0][:, :piece].astype(F32)
        + got[1][:, :piece].astype(F32)
        + got[2][:, :piece].astype(F32)
    ).astype(BF16)
    keep, passed, middle_grad, own, send1, send2, send3 = run(
        attend_back_kernel,
        [
            ((owners // 2, shard, outer + 2 * NOPE + LANES), BF16),
            ((owners // 2, shard, outer + 2 * NOPE + LANES), BF16),
            ((tokens, width), F32),
            ((tokens, piece), F32),
            ((tokens, piece), BF16),
            ((tokens, piece), BF16),
            ((tokens, piece), BF16),
        ],
        [
            me,
            core,
            stream,
            cotangent,
            middle,
            *share_small(mixed_sum),
            *got,
            probs_own,
            router_probs,
            one,
            router_block,
            mixed,
            normed,
            query,
            expanded,
            key,
            latent,
            compressed,
            probs,
            attended,
            gain_rows,
            latent_gain_rows,
            cosine,
            sine,
        ],
        2 * tokens * width * (3 * edge + 2 * outer),
        scratch=[
            pltpu.VMEM((width, outer + 2 * NOPE + LANES), BF16),
            pltpu.VMEM((tokens, edge), BF16),
            pltpu.VMEM((tokens, width), F32),
            pltpu.VMEM((width, outer + 2 * NOPE), BF16),
            pltpu.VMEM(normed.shape, BF16),
            pltpu.VMEM(query.shape, BF16),
            pltpu.VMEM(expanded.shape, BF16),
            pltpu.VMEM(compressed.shape, F32),
            pltpu.VMEM(probs.shape, F32),
            pltpu.SemaphoreType.DMA((4,)),
            pltpu.SemaphoreType.DMA((7,)),
        ],
        places={0: pltpu.SMEM, 1: pltpu.SMEM} | {i: pl.ANY for i in (14, 17, 18, 19, 22, 23)},
        out_places={0: pl.ANY, 1: pl.ANY},
        name="attend_back",
    )
    paired = lax.ppermute(after(passed, out_rows), "expert", [(i, i ^ 1) for i in range(owners)])
    side = 4
    chip = lax.axis_index("expert") // 2
    at = jnp.stack([chip // side, lax.rem(chip, side)]).astype(jnp.int32)
    columns = outer + 2 * NOPE + LANES
    cut = columns // 2

    def along(group, array, step):
        def target(i):
            x, z, core = i // (2 * side), i // 2 % side, i % 2
            if group == 0:
                x = (x + step) % side
            else:
                z = (z + step) % side
            return (x * side + z) * 2 + core

        return lax.ppermute(array, "expert", [(i, target(i)) for i in range(owners)])

    widths = [cut, columns - cut]
    along_z, *along_x = run(
        pair_kernel,
        [((side, side, shard, widths[1]), BF16)] + [((side, shard, cut), BF16)] * side,
        [at, keep, paired],
        0,
        places=smem,
        name="pair",
    )
    came_z = lax.all_to_all(
        along_z.reshape(side, side * shard, widths[1]),
        "expert",
        split_axis=0,
        concat_axis=0,
        tiled=True,
        axis_index_groups=[[(x * side + z) * 2 + c for z in range(side)] for x in range(side) for c in range(2)],
    ).reshape(along_z.shape)
    came_x = [along_x[0]] + [along(0, along_x[step], step) for step in range(1, side)]
    got = send_blocks([send1, send2, send3])
    first_sum = (own + got[0].astype(F32) + got[1].astype(F32) + got[2].astype(F32)).astype(BF16)
    streams = share_small(first_sum)
    (branch,) = run(
        routed_kernel,
        [((tokens, piece), BF16)],
        [t0, t1, out_rows, shared_own, *shared_got],
        4 * tokens * rows * piece,
        name="routed",
    )
    at_last = after(at, branch, *streams[1:])
    parts = []
    for group, came in enumerate((came_x, [came_z])):
        crossed = run(
            functools.partial(cross_kernel, group),
            [((shard, widths[group]), F32)] + [((shard, widths[group]), BF16)] * (side - 1),
            [at_last, *came],
            0,
            places=smem,
            name="cross",
        )
        parts += [crossed[0]] + [along(1 - group, crossed[step], step) for step in range(1, side)]
    (stream_grad,) = run(
        stream_kernel,
        [((tokens, width), F32)],
        [after(me, parts[0], parts[4]), middle_grad, stream, gain_rows, *streams],
        0,
        scratch=[pltpu.VMEM((tokens, width), F32)],
        places=smem,
        name="stream",
    )

    shared_sum = shared_sum.astype(F32)
    gate_sum = shared_sum[:, :hidden_columns]
    up_sum = shared_sum[:, hidden_columns : 2 * hidden_columns]
    down_sum = shared_sum[:, 2 * hidden_columns :]
    parts[0] = after(parts[0], stream_grad, gate_sum, up_sum, down_sum)
    query_grad, late, output_grad, latent_up_grad, router_grad = run(
        unpack_kernel,
        [
            (query_proj.shape, F32),
            ((shard, edge - queries), F32),
            ((shard, heads * VDIM), F32),
            (latent_up.shape, F32),
            (router_proj.shape, F32),
        ],
        parts,
        0,
        scratch=[pltpu.VMEM((shard, columns), F32)],
        name="unpack",
    )
    (result,) = run(
        result_kernel,
        [((tokens, width), F32)],
        [after(me, late), middle, *share_small(branch)],
        0,
        places=smem,
        name="result",
    )

    latent_down_grad, gain_grads = run(
        late_kernel,
        [(latent_down.shape, F32), ((8, LANES), F32)],
        [late, *(shift(late.astype(BF16), step) for step in range(1, tensors))],
        0,
        name="late",
    )
    return (
        result,
        stream_grad,
        gain_grads[0, :shard],
        query_grad,
        latent_down_grad,
        gain_grads[2, :short],
        latent_up_grad,
        output_grad.T,
        gain_grads[1, :shard],
        router_grad,
        gate_sum,
        up_sum,
        down_sum.T,
        gate_grad.transpose(0, 2, 1),
        up_grad.transpose(0, 2, 1),
        down_grad,
    )


def solution(mesh):
    placed = (
        P("expert", None),
        P("expert", None),
        P("expert", None),
        P("expert"),
        P("expert", "tensor"),
        P("expert", None),
        P("expert"),
        P("expert", "tensor"),
        P("tensor", "expert"),
        P("expert"),
        P("expert", None),
        P("expert", "tensor"),
        P("expert", "tensor"),
        P("tensor", "expert"),
        P("expert", None, "tensor"),
        P("expert", None, "tensor"),
        P("expert", "tensor", None),
        P("expert", None),
    )
    return jax.shard_map(
        per_device,
        mesh=mesh,
        in_specs=placed,
        out_specs=(
            P("expert", None),
            P("expert", None),
            P("expert"),
            P("expert", "tensor"),
            P("expert", None),
            P("expert"),
            P("expert", "tensor"),
            P("tensor", "expert"),
            P("expert"),
            P("expert", None),
            P("expert", "tensor"),
            P("expert", "tensor"),
            P("tensor", "expert"),
            P("expert", None, "tensor"),
            P("expert", None, "tensor"),
            P("expert", "tensor", None),
        ),
        check_vma=False,
    )
```
